32 devices in a mesh: dp: 4 (over x, core), fsdp: 8 (over z, y).
Axes of the slice: x: 2, y: 2, z: 4, core: 2. Of those that a mesh axis runs over, the one named last changes fastest.
Arguments:
- tokens: bfloat16 [2, 32, 128, 1024], P(None, ('dp', 'fsdp')), may hold values from -6 to 6
- states: bfloat16 [2, 32, 1024, 1024], P(None, ('dp', 'fsdp')), may hold values from -6 to 6
- cotangent: bfloat16 [2, 32, 128, 1024], P(None, ('dp', 'fsdp')), may hold values from -6 to 6
- seq_len: int32 [2, 32], P(None, ('dp', 'fsdp')), may hold values from 1 to 128, as said below
- enc_len: int32 [2, 32], P(None, ('dp', 'fsdp')), may hold values from 1 to 1024, as said below
- attn_w: float32 [8, 1024, 1024], P(None, 'fsdp'), may hold values from -0.5 to 0.5
- attn_m: float32 [8, 1024, 1024], P(None, 'fsdp'), may hold values from -39.824254 to 39.824254
- attn_v: float32 [8, 1024, 1024], P(None, 'fsdp'), as said below
- fc1_w: float32 [1024, 4096], P('fsdp'), may hold values from -0.1875 to 0.1875
- fc1_m: float32 [1024, 4096], P('fsdp'), may hold values from -39.824254 to 39.824254
- fc1_v: float32 [1024, 4096], P('fsdp'), as said below
- fc2_w: float32 [4096, 1024], P('fsdp'), may hold values from -0.09375 to 0.09375
- fc2_m: float32 [4096, 1024], P('fsdp'), may hold values from -39.824254 to 39.824254
- fc2_v: float32 [4096, 1024], P('fsdp'), as said below
- vec_w: float32 [17, 1024], P(None, 'fsdp'), may hold values from -0.8 to 1.4
- vec_m: float32 [17, 1024], P(None, 'fsdp'), may hold values from -39.824254 to 39.824254
- vec_v: float32 [17, 1024], P(None, 'fsdp'), as said below
Outputs:
- mixed: bfloat16 [2, 32, 128, 1024], P(None, ('dp', 'fsdp'))
- grad_tokens: bfloat16 [2, 32, 128, 1024], P(None, ('dp', 'fsdp'))
- grad_states: bfloat16 [2, 32, 1024, 1024], P(None, ('dp', 'fsdp'))
- stream_rms: float32 [4], replicated
- attn_new: float32 [8, 1024, 1024], P(None, 'fsdp')
- attn_m_new: float32 [8, 1024, 1024], P(None, 'fsdp')
- attn_v_new: float32 [8, 1024, 1024], P(None, 'fsdp')
- fc1_new: float32 [1024, 4096], P('fsdp')
- fc1_m_new: float32 [1024, 4096], P('fsdp')
- fc1_v_new: float32 [1024, 4096], P('fsdp')
- fc2_new: float32 [4096, 1024], P('fsdp')
- fc2_m_new: float32 [4096, 1024], P('fsdp')
- fc2_v_new: float32 [4096, 1024], P('fsdp')
- vec_new: float32 [17, 1024], P(None, 'fsdp')
- vec_m_new: float32 [17, 1024], P(None, 'fsdp')
- vec_v_new: float32 [17, 1024], P(None, 'fsdp')
The draws below stay inside these ranges and needn't reach their ends.
Inputs may be any that keep to these rules, and one draw needn't show every extreme that they name: `seq_len`: valid tokens rise on the whole from the first sequences to the last, each sequence lying below that rise by a random dip of up to 17; in every draw some sequence has all 128. `enc_len`: in every draw some sequence has all 1024 encoder states valid. `attn_v`: Positive. `fc1_v`: Positive. `fc2_v`: Positive. `vec_v`: Positive.
All inputs are finite; a program needn't handle non-finite values.
Results may differ from the reference program's by a relative error of at most 0.03.
Values may be sent and summed in bfloat16 or wider, within the bound.
No kernel may reach another device: no remote copies, remote signals or barrier semaphores. Data moves between devices by JAX's collectives and lax.ppermute only.
A program may use at most 384 MiB of HBM per device.

```python
import math
import jax
import jax.numpy as jnp
from jax import lax

D = 1024
H = 16
FF = 4096
DH = 64
SEQ = 128
ENC = 1024
MICRO = 2
STEP = 7
SEQS = 32
TOKENS = 8192
NVEC = 17
N_DP = 4
N_FSDP = 8


def rising_lengths(key, most):
    seq_index = jnp.arange(SEQS, dtype=jnp.int32)
    outer_pos = seq_index // N_FSDP
    inner_pos = seq_index % N_FSDP
    baseline = most * (N_DP - 1 + 2 * outer_pos) * (N_FSDP - 1 + 2 * inner_pos) // (9 * (N_DP - 1) * (N_FSDP - 1))
    jitter = jax.random.randint(key, (MICRO, SEQS), 0, most // 8 + 2)
    drawn = jnp.maximum(baseline[None, :] - jitter, 1)
    corner = (jnp.arange(MICRO, dtype=jnp.int32)[:, None] == 0) & (seq_index[None, :] == SEQS - 1)
    return jnp.where(corner, most, drawn).astype(jnp.int32)


def unit_entries(key, array_shape):
    return jnp.clip(jax.random.normal(key, array_shape), -4.0, 4.0)


def attn_factor():
    self_part = 2.0 ** 0.5 * SEQ ** (-0.25)
    cross_part = 2.0 ** 0.5 * ENC ** (-0.25)
    return jnp.array([0.3, 0.3, self_part, self_part, 0.3, 0.3, cross_part, cross_part], jnp.float32)[:, None, None]


def first_moment(key, array_shape, factor):
    grad_size = TOKENS ** 0.5 * factor
    return (0.11 * grad_size * jnp.clip(jax.random.normal(key, array_shape), -4.0, 4.0)).astype(jnp.float32)


def second_moment(key, array_shape, factor):
    grad_size = TOKENS ** 0.5 * factor
    spread = jnp.exp(jax.random.uniform(key, array_shape, minval=0.0, maxval=math.log(4.0)))
    return (0.001 * grad_size * grad_size * spread).astype(jnp.float32)


def draw_seq_len(key, part):
    key = jax.random.fold_in(key, 1)
    return rising_lengths(key, SEQ)


def draw_enc_len(key, part):
    key = jax.random.fold_in(key, 2)
    return rising_lengths(key, ENC)


def draw_attn_w(key, part):
    key = jax.random.fold_in(key, 3)
    self_part = (0.5 * SEQ ** 0.5) ** 0.5
    cross_part = (0.5 * ENC ** 0.5) ** 0.5
    factor = jnp.array([1.0, 1.0, self_part, self_part, 1.0, 1.0, cross_part, cross_part], jnp.float32)[:, None, None]
    return (unit_entries(key, (8, D, D)) * factor / D ** 0.5).astype(jnp.float32)


def draw_vec_w(key, part):
    key = jax.random.fold_in(key, 4)
    row_index = jnp.arange(NVEC, dtype=jnp.int32)[:, None]
    gain_row = (row_index == 7) | (row_index == 9) | (row_index == 11)
    entries = unit_entries(key, (NVEC, D))
    return jnp.where(gain_row, 1.0 + 0.1 * entries, 0.2 * entries).astype(jnp.float32)


def draw_attn_m(key, part):
    key = jax.random.fold_in(key, 11)
    return first_moment(key, (8, D, D), attn_factor())


def draw_attn_v(key, part):
    key = jax.random.fold_in(key, 12)
    return second_moment(key, (8, D, D), attn_factor())


def draw_fc1_m(key, part):
    key = jax.random.fold_in(key, 13)
    return first_moment(key, (D, FF), 0.3)


def draw_fc1_v(key, part):
    key = jax.random.fold_in(key, 14)
    return second_moment(key, (D, FF), 0.3)


def draw_fc2_m(key, part):
    key = jax.random.fold_in(key, 15)
    return first_moment(key, (FF, D), 0.6)


def draw_fc2_v(key, part):
    key = jax.random.fold_in(key, 16)
    return second_moment(key, (FF, D), 0.6)


def draw_vec_m(key, part):
    key = jax.random.fold_in(key, 17)
    return first_moment(key, (NVEC, D), 1.0)


def draw_vec_v(key, part):
    key = jax.random.fold_in(key, 18)
    return second_moment(key, (NVEC, D), 1.0)


def block_levels(key, extent, shards, smallest, largest):
    def one(position, shards_of):
        heights = jax.random.uniform(jax.random.fold_in(jax.random.fold_in(key, 6), position), (shards_of,), jnp.float32, smallest / len(shards), largest / len(shards))
        return jnp.repeat(jnp.exp(heights), extent[position] // shards_of).reshape((-1,) + (1,) * (len(extent) - position - 1))

    level = one(*shards[0])
    for cut in shards[1:]:
        level = level * one(*cut)
    return level


def noise(rng, shape, scale, bound, cuts=(), kind=jnp.bfloat16):
    values = jax.random.normal(rng, shape, jnp.float32) * scale
    if len(cuts) > 0:
        values = block_levels(rng, shape, cuts, -0.22, 0.18) * values
    return jnp.clip(values, min=-bound, max=bound).astype(kind)


def setup_inputs(seed: int = 0) -> dict:
    keys = jax.random.split(jax.random.key(seed), 18)
    tokens = noise(keys[0], (MICRO, SEQS, SEQ, D), 1.0, 6.0, ((1, 32),))
    states = noise(keys[1], (MICRO, SEQS, ENC, D), 1.0, 6.0, ((1, 32),))
    cotangent = noise(keys[2], (MICRO, SEQS, SEQ, D), 1.0, 6.0, ((1, 32),))
    seq_len = draw_seq_len(jax.random.fold_in(keys[17], 71), 0)
    enc_len = draw_enc_len(jax.random.fold_in(keys[17], 71), 0)
    attn_w = draw_attn_w(jax.random.fold_in(keys[17], 71), 0)
    attn_m = draw_attn_m(jax.random.fold_in(keys[17], 71), 0)
    attn_v = draw_attn_v(jax.random.fold_in(keys[17], 71), 0)
    fc1_w = noise(keys[8], (D, FF), D ** -0.5, 0.1875, ((0, 8),), jnp.float32)
    fc1_m = draw_fc1_m(jax.random.fold_in(keys[17], 71), 0)
    fc1_v = draw_fc1_v(jax.random.fold_in(keys[17], 71), 0)
    fc2_w = noise(keys[11], (FF, D), FF ** -0.5, 0.09375, ((0, 8),), jnp.float32)
    fc2_m = draw_fc2_m(jax.random.fold_in(keys[17], 71), 0)
    fc2_v = draw_fc2_v(jax.random.fold_in(keys[17], 71), 0)
    vec_w = draw_vec_w(jax.random.fold_in(keys[17], 71), 0)
    vec_m = draw_vec_m(jax.random.fold_in(keys[17], 71), 0)
    vec_v = draw_vec_v(jax.random.fold_in(keys[17], 71), 0)
    return {"tokens": tokens, "states": states, "cotangent": cotangent, "seq_len": seq_len, "enc_len": enc_len, "attn_w": attn_w, "attn_m": attn_m, "attn_v": attn_v, "fc1_w": fc1_w, "fc1_m": fc1_m, "fc1_v": fc1_v, "fc2_w": fc2_w, "fc2_m": fc2_m, "fc2_v": fc2_v, "vec_w": vec_w, "vec_m": vec_m, "vec_v": vec_v}


@jax.custom_vjp
def low(v):
    return lax.optimization_barrier(v.astype(jnp.bfloat16)).astype(jnp.float32)

@jax.custom_vjp
def low_back(v):
    return v

def low_keep(v):
    return (low(v), None)

def low_pass(kept, grad):
    return (grad,)

def back_keep(v):
    return (v, None)

def back_low(kept, grad):
    return (low(grad),)
low.defvjp(low_keep, low_pass)
low_back.defvjp(back_keep, back_low)
highest = lax.Precision.HIGHEST
momentum_decay = 0.9
square_decay = 0.999
matrix_rate = 0.08
vector_rate = 0.3
matrix_decay = 0.01
epsilon = 1e-08
norm_epsilon = 1e-05

def layer_norm(stream, gains, biases):
    centred = stream - lax.optimization_barrier(jnp.mean(stream, axis=-1, keepdims=True))
    spread = lax.optimization_barrier(jnp.mean(centred * centred, axis=-1, keepdims=True))
    return centred * lax.rsqrt(spread + norm_epsilon) * gains + biases

def product(left, right):
    return jnp.dot(left, right, precision=highest)

def attend(queries, key_rows, value_rows, key_valid, causal):
    length = queries.shape[0]
    block_size = min(512, length)
    query_blocks = queries.reshape(length // block_size, block_size, H, DH)
    offsets = jnp.arange(length // block_size, dtype=jnp.int32) * block_size
    key_heads = key_rows.reshape(-1, H, DH)
    value_heads = value_rows.reshape(-1, H, DH)
    key_place = jnp.arange(key_heads.shape[0], dtype=jnp.int32)

    def one_block(block_pair):
        segment, offset = block_pair
        raw_scores = jnp.einsum('qhd,khd->hqk', segment, key_heads, precision=highest) * DH ** (-0.5)
        scores = low_back(raw_scores)
        allowed = jnp.broadcast_to(key_valid[None, :], (block_size, key_place.shape[0]))
        if causal:
            query_place = offset + jnp.arange(block_size, dtype=jnp.int32)
            allowed = allowed & (key_place[None, :] <= query_place[:, None])
        scores = jnp.where(allowed[None], scores, -1e+30)
        row_peak = lax.optimization_barrier(jnp.max(scores, axis=-1, keepdims=True))
        exponent = jnp.exp(scores - row_peak)
        softmax_w = exponent / lax.optimization_barrier(jnp.sum(exponent, axis=-1, keepdims=True))
        return jnp.einsum('hqk,khd->qhd', low(softmax_w), value_heads, precision=highest)
    mixed_out = lax.map(jax.checkpoint(one_block), (query_blocks, offsets))
    return mixed_out.reshape(length, H * DH)

def sequence_layer(params, tokens_row, states_row, tok_len, enc_count):
    attn, fc_in, fc_out, vectors = params
    fc_bias = vectors[13:].reshape(FF)
    tok_valid = jnp.arange(SEQ, dtype=jnp.int32) < tok_len
    enc_valid = jnp.arange(ENC, dtype=jnp.int32) < enc_count
    queries = low_back(low(product(tokens_row, attn[0]) + vectors[0]))
    key_rows = low_back(low(product(tokens_row, attn[1])))
    value_rows = low_back(low(product(tokens_row, attn[2]) + vectors[1]))
    context = low_back(low(attend(queries, key_rows, value_rows, tok_valid, True)))
    self_out = low_back(product(context, attn[3]) + vectors[2])
    normed_one = layer_norm(tokens_row + self_out, vectors[7], vectors[8])
    normed_low = low(normed_one)
    cross_q = low_back(low(product(normed_low, attn[4]) + vectors[3]))
    cross_k = low_back(low(product(states_row, attn[5])))
    cross_v = low_back(low(product(states_row, attn[6]) + vectors[4]))
    cross_ctx = low_back(low(attend(cross_q, cross_k, cross_v, enc_valid, False)))
    cross_out = low_back(product(cross_ctx, attn[7]) + vectors[5])
    normed_two = layer_norm(normed_one + cross_out, vectors[9], vectors[10])
    hidden_pre = low_back(product(low(normed_two), fc_in) + fc_bias)
    hidden = low(jax.nn.gelu(hidden_pre, approximate=False))
    ffn_out = low_back(product(hidden, fc_out) + vectors[6])
    result = layer_norm(normed_two + ffn_out, vectors[11], vectors[12])
    valid_rows = tok_valid.astype(jnp.float32)[:, None]
    sums = jnp.stack([jnp.sum(valid_rows * result * result), jnp.sum(valid_rows * self_out * self_out), jnp.sum(valid_rows * cross_out * cross_out), jnp.sum(valid_rows * ffn_out * ffn_out)])
    return (result, sums)

def group_layer(params, tokens_f, states_f, tok_lens, enc_lens):
    rounded = tuple((low(param) for param in params))
    results, sums = jax.vmap(sequence_layer, in_axes=(None, 0, 0, 0, 0))(rounded, tokens_f, states_f, tok_lens, enc_lens)
    return (results, lax.optimization_barrier(jnp.sum(sums, axis=0)))

def adam_update(weight, first, second, grad, rate, decay):
    first = momentum_decay * first + (1.0 - momentum_decay) * grad
    second = square_decay * second + (1.0 - square_decay) * grad * grad
    fix_first = 1.0 - momentum_decay ** STEP
    fix_second = 1.0 - square_decay ** STEP
    update = first / fix_first / (jnp.sqrt(second / fix_second) + epsilon) + decay * weight
    return (weight - rate * update, first, second)

def reference(tokens, states, cotangent, seq_len, enc_len, attn_w, attn_m, attn_v, fc1_w, fc1_m, fc1_v, fc2_w, fc2_m, fc2_v, vec_w, vec_m, vec_v):
    total_seqs = MICRO * SEQS
    group_size = math.gcd(total_seqs, max(1, 4096 // SEQ))
    rounds = total_seqs // group_size
    tok_groups = tokens.reshape(rounds, group_size, SEQ, D)
    state_groups = states.reshape(rounds, group_size, ENC, D)
    cot_groups = cotangent.reshape(rounds, group_size, SEQ, D)
    len_groups = seq_len.reshape(rounds, group_size).astype(jnp.int32)
    enc_groups = enc_len.reshape(rounds, group_size).astype(jnp.int32)
    params = (attn_w, fc1_w, fc2_w, vec_w)

    def one_round(carry_in, batch_in):
        grads, sums = carry_in
        tok_part, state_part, cot_part, len_part, enc_part = batch_in

        def forward(weights, tok_f, state_f):
            return group_layer(weights, tok_f, state_f, len_part, enc_part)
        result, pullback, part_sums = jax.vjp(forward, params, tok_part.astype(jnp.float32), state_part.astype(jnp.float32), has_aux=True)
        grad_params, grad_tok, grad_state = pullback(cot_part.astype(jnp.float32))
        grads = jax.tree.map(jnp.add, grads, grad_params)
        return ((grads, sums + part_sums), (result.astype(jnp.bfloat16), grad_tok.astype(jnp.bfloat16), grad_state.astype(jnp.bfloat16)))
    initial = (tuple((jnp.zeros_like(param) for param in params)), jnp.zeros((4,), jnp.float32))
    (grads, sums), (results, grad_tok, grad_state) = lax.scan(one_round, initial, (tok_groups, state_groups, cot_groups, len_groups, enc_groups))
    mixed = results.reshape(MICRO, SEQS, SEQ, D)
    grad_tokens = grad_tok.reshape(MICRO, SEQS, SEQ, D)
    grad_states = grad_state.reshape(MICRO, SEQS, ENC, D)
    count = jnp.sum(seq_len).astype(jnp.float32) * D
    stream_rms = jnp.sqrt(sums / count)
    attn_new, attn_m_new, attn_v_new = adam_update(attn_w, attn_m, attn_v, grads[0], matrix_rate, matrix_decay)
    fc1_new, fc1_m_new, fc1_v_new = adam_update(fc1_w, fc1_m, fc1_v, grads[1], matrix_rate, matrix_decay)
    fc2_new, fc2_m_new, fc2_v_new = adam_update(fc2_w, fc2_m, fc2_v, grads[2], matrix_rate, matrix_decay)
    vec_new, vec_m_new, vec_v_new = adam_update(vec_w, vec_m, vec_v, grads[3], vector_rate, 0.0)
    return (mixed, grad_tokens, grad_states, stream_rms, attn_new, attn_m_new, attn_v_new, fc1_new, fc1_m_new, fc1_v_new, fc2_new, fc2_m_new, fc2_v_new, vec_new, vec_m_new, vec_v_new)
```

```python
from functools import partial

import jax
import jax.numpy as jnp
from jax import lax
from jax.experimental import pallas as pl
from jax.experimental.pallas import tpu as pltpu
from jax.sharding import PartitionSpec as P

D = 1024
H = 16
DH = 64
STEP = 7
PAIRS = H // 2
UNITS = 4

momentum_decay = 0.9
square_decay = 0.999
matrix_rate = 0.08
vector_rate = 0.3
matrix_decay = 0.01
epsilon = 1e-08
norm_epsilon = 1e-05
fix_first = 1.0 - momentum_decay**STEP
fix_second = 1.0 - square_decay**STEP

f32 = jnp.float32
bf16 = jnp.bfloat16
ANY = pl.BlockSpec(memory_space=pl.ANY)
VMEM_BYTES = 40 * 1024 * 1024
CROSS_ORDER = (4, 7, 5, 6)


def params(**more):
    return pltpu.CompilerParams(vmem_limit_bytes=VMEM_BYTES, **more)


def cost(flops, nbytes, exps=0):
    return pl.CostEstimate(flops=int(flops), bytes_accessed=int(nbytes), transcendentals=int(exps))


def dot(left, right):
    return jnp.dot(left, right, preferred_element_type=f32)


def dot_back(left, right):
    return lax.dot_general(left, right, (((1,), (1,)), ((), ())), preferred_element_type=f32)


def dot_grad(inputs, grads):
    return lax.dot_general(inputs, grads, (((0,), (0,)), ((), ())), preferred_element_type=f32)


def two_heads(rows):
    low_half = lax.broadcasted_iota(jnp.int32, rows.shape, 1) < DH
    zero = jnp.zeros_like(rows)
    return jnp.concatenate([jnp.where(low_half, rows, zero), jnp.where(low_half, zero, rows)], axis=0)


def one_row(both):
    half = both.shape[0] // 2
    low_half = lax.broadcasted_iota(jnp.int32, (half, both.shape[1]), 1) < DH
    return jnp.where(low_half, both[:half], both[half:])


def masked_exp(queries, keys, valid, causal):
    scores = dot_back(queries, keys)
    place = lax.broadcasted_iota(jnp.int32, (1, scores.shape[1]), 1)
    if causal:
        rows = scores.shape[0] // 2
        spot = lax.broadcasted_iota(jnp.int32, scores.shape, 0)
        spot = jnp.where(spot >= rows, spot - rows, spot)
        spots = lax.broadcasted_iota(jnp.int32, scores.shape, 1)
        allowed = (spots <= spot) & (spots < valid)
        scores = jnp.where(allowed, scores, -1e30)
    else:
        scores = scores + jnp.where(place < valid, 0.0, -1e30)
    top = jnp.max(scores, axis=-1, keepdims=True)
    exponent = jnp.exp(scores - top)
    return exponent, 1.0 / jnp.sum(exponent, axis=-1, keepdims=True)


def attend_kernel(causal, len_ref, q_ref, k_ref, v_ref, o_ref):
    queries = two_heads(q_ref[...] * DH**-0.5)
    exponent, inverse = masked_exp(queries, k_ref[...], len_ref[pl.program_id(0)], causal)
    o_ref[...] = one_row(dot(exponent.astype(bf16), v_ref[...]) * inverse).astype(bf16)


def attend_back_kernel(causal, len_ref, q_ref, k_ref, v_ref, do_ref, dq_ref, dk_ref, dv_ref):
    queries = two_heads(q_ref[...] * DH**-0.5)
    exponent, inverse = masked_exp(queries, k_ref[...], len_ref[pl.program_id(0)], causal)
    grads = two_heads(do_ref[...])
    grad_probs = dot_back(grads, v_ref[...])
    row_dot = jnp.sum(exponent * grad_probs, axis=-1, keepdims=True) * inverse
    grad_scores = (exponent * (grad_probs - row_dot)).astype(bf16)
    dq_ref[...] = one_row(dot(grad_scores, k_ref[...]) * (inverse * DH**-0.5)).astype(bf16)
    dk_ref[...] = dot_grad(grad_scores, (queries * inverse).astype(bf16)).astype(bf16)
    dv_ref[...] = dot_grad(exponent.astype(bf16), (grads * inverse).astype(bf16)).astype(bf16)


def attend(lengths, queries, keys, values, seqs, causal, q_at, k_at, v_at):
    q_rows, k_rows = queries.shape[0] // seqs, keys.shape[0] // seqs

    def block(rows, at):
        return pl.BlockSpec((rows, 2 * DH), lambda m, p, n: (m, at + p))

    return pl.pallas_call(
        partial(attend_kernel, causal),
        out_shape=jax.ShapeDtypeStruct((seqs * q_rows, D), bf16),
        grid_spec=pltpu.PrefetchScalarGridSpec(
            num_scalar_prefetch=1,
            grid=(seqs, PAIRS),
            in_specs=[block(q_rows, q_at), block(k_rows, k_at), block(k_rows, v_at)],
            out_specs=block(q_rows, 0),
        ),
        compiler_params=params(),
        cost_estimate=cost(8 * seqs * q_rows * k_rows * D, 4 * seqs * (q_rows + k_rows) * D, seqs * H * q_rows * k_rows),
    )(lengths, queries, keys, values)


def attend_back(lengths, queries, keys, values, grads, seqs, causal, q_at, k_at, v_at):
    q_rows, k_rows = queries.shape[0] // seqs, keys.shape[0] // seqs

    def block(rows, at):
        return pl.BlockSpec((rows, 2 * DH), lambda m, p, n: (m, at + p))

    return pl.pallas_call(
        partial(attend_back_kernel, causal),
        out_shape=[
            jax.ShapeDtypeStruct((seqs * q_rows, D), bf16),
            jax.ShapeDtypeStruct((seqs * k_rows, D), bf16),
            jax.ShapeDtypeStruct((seqs * k_rows, D), bf16),
        ],
        grid_spec=pltpu.PrefetchScalarGridSpec(
            num_scalar_prefetch=1,
            grid=(seqs, PAIRS),
            in_specs=[block(q_rows, q_at), block(k_rows, k_at), block(k_rows, v_at), block(q_rows, 0)],
            out_specs=[block(q_rows, 0), block(k_rows, 0), block(k_rows, 0)],
        ),
        compiler_params=params(),
        cost_estimate=cost(20 * seqs * q_rows * k_rows * D, 8 * seqs * (q_rows + k_rows) * D, seqs * H * q_rows * k_rows),
    )(lengths, queries, keys, values, grads)


def place_kernel(count, rows, idx_ref, *refs):
    pieces, out_ref, sems = refs[:count], refs[count], refs[count + 1]
    copies = [
        pltpu.make_async_copy(
            piece, out_ref.at[pl.ds(pl.multiple_of(idx_ref[i] * rows, rows), rows), :], sems.at[i]
        )
        for i, piece in enumerate(pieces)
    ]
    for copy in copies:
        copy.start()
    for copy in copies:
        copy.wait()


def place(pieces, slots):
    count, (rows, width) = len(pieces), pieces[0].shape
    return pl.pallas_call(
        partial(place_kernel, count, rows),
        out_shape=jax.ShapeDtypeStruct((count * rows, width), pieces[0].dtype),
        grid_spec=pltpu.PrefetchScalarGridSpec(
            num_scalar_prefetch=1,
            grid=(),
            in_specs=[ANY] * count,
            out_specs=ANY,
            scratch_shapes=[pltpu.SemaphoreType.DMA((count,))],
        ),
        compiler_params=params(),
        cost_estimate=cost(0, 4 * count * rows * width),
    )(jnp.stack(slots).astype(jnp.int32), *pieces)


def assemble_kernel(wide, depth, rows, idx_ref, *refs):
    pieces, out_ref, sems = refs[:8], refs[8], refs[9]
    copies = []
    for i, piece in enumerate(pieces):
        unit, plane = idx_ref[2 * i], idx_ref[2 * i + 1]
        for z in range(depth):
            if wide:
                row = (2 * z + plane) * rows
                target = out_ref.at[
                    pl.ds(pl.multiple_of(row, rows), rows), pl.ds(pl.multiple_of(unit * D, D), D)
                ]
            else:
                row = ((2 * z + plane) * UNITS + unit) * rows
                target = out_ref.at[pl.ds(pl.multiple_of(row, rows), rows), :]
            copies.append(
                pltpu.make_async_copy(piece.at[pl.ds(z * rows, rows), :], target, sems.at[i * depth + z])
            )
    for copy in copies:
        copy.start()
    for copy in copies:
        copy.wait()


def assemble(pieces, places, depth, wide):
    total, width = pieces[0].shape
    rows = total // depth
    shape = (2 * total, UNITS * D) if wide else (2 * UNITS * total, D)
    return pl.pallas_call(
        partial(assemble_kernel, wide, depth, rows),
        out_shape=jax.ShapeDtypeStruct(shape, bf16),
        grid_spec=pltpu.PrefetchScalarGridSpec(
            num_scalar_prefetch=1,
            grid=(),
            in_specs=[ANY] * 8,
            out_specs=ANY,
            scratch_shapes=[pltpu.SemaphoreType.DMA((8 * depth,))],
        ),
        compiler_params=params(),
        cost_estimate=cost(0, 32 * total * width),
    )(jnp.stack([i for pair in places for i in pair]).astype(jnp.int32), *pieces)


def grad_kernel(idx_ref, xm_ref, xr_ref, ym_ref, yr_ref, out_ref):
    out_ref[...] = (dot_grad(xm_ref[...], ym_ref[...]) + dot_grad(xr_ref[...], yr_ref[...])).astype(bf16)


def plane_grad(x_mine, x_peer, y_mine, y_peer, x_at, y_at, stride, depth, rows):
    tokens = x_mine.shape[0]
    x_spec = pl.BlockSpec((tokens, rows), lambda z, i: (0, i[0] + stride * z))
    y_spec = pl.BlockSpec((tokens, D), lambda z, i: (0, i[1]))
    return pl.pallas_call(
        grad_kernel,
        out_shape=jax.ShapeDtypeStruct((depth * rows, D), bf16),
        grid_spec=pltpu.PrefetchScalarGridSpec(
            num_scalar_prefetch=1,
            grid=(depth,),
            in_specs=[x_spec, x_spec, y_spec, y_spec],
            out_specs=pl.BlockSpec((rows, D), lambda z, i: (z, 0)),
        ),
        compiler_params=params(),
        cost_estimate=cost(4 * tokens * depth * rows * D, 2 * depth * rows * D + 8 * tokens * D),
    )(jnp.stack([x_at, y_at]).astype(jnp.int32), x_mine, x_peer, y_mine, y_peer)


def adam_update(weight, first, second, grad, rate, decay):
    first = momentum_decay * first + (1.0 - momentum_decay) * grad
    second = square_decay * second + (1.0 - square_decay) * grad * grad
    update = first / fix_first / (jnp.sqrt(second / fix_second) + epsilon) + decay * weight
    return (weight - rate * update, first, second)


def adam_kernel(idx_ref, g0_ref, g1_ref, g2_ref, g3_ref, w_ref, m_ref, v_ref, *rest):
    w_out, m_out, v_out = rest[-3:]
    away = pl.program_id(0) ^ idx_ref[0]
    grad = jnp.where(
        away < 2,
        jnp.where(away == 0, g0_ref[...], g1_ref[...]),
        jnp.where(away == 2, g2_ref[...], g3_ref[...]),
    ).astype(f32)
    if len(w_ref.shape) == 3:
        grad = grad[None]
    w_out[...], m_out[...], v_out[...] = adam_update(
        w_ref[...], m_ref[...], v_ref[...], grad, matrix_rate, matrix_decay
    )


def adam_units(spot, grads, state, block_shape, at, earlier=None):
    spec = pl.BlockSpec(block_shape, lambda u, i: at(u))
    g_spec = pl.BlockSpec(grads[0].shape, lambda u, i: (0, 0))
    extra = list(earlier) if earlier is not None else []
    return pl.pallas_call(
        adam_kernel,
        out_shape=[jax.ShapeDtypeStruct(a.shape, f32) for a in state],
        grid_spec=pltpu.PrefetchScalarGridSpec(
            num_scalar_prefetch=1,
            grid=(UNITS,),
            in_specs=[g_spec] * 4 + [spec] * 3 + [ANY] * len(extra),
            out_specs=[spec] * 3,
        ),
        input_output_aliases={8 + i: i for i in range(len(extra))},
        compiler_params=params(),
        cost_estimate=cost(20 * UNITS * grads[0].size, 26 * UNITS * grads[0].size),
    )(jnp.stack([spot]).astype(jnp.int32), *grads, *state, *extra)


class Links:
    def __init__(self, n_dp, n_fsdp):
        self.n_fsdp, self.depth = n_fsdp, n_fsdp // 2
        spot = lax.axis_index("dp")
        shard = lax.axis_index("fsdp")
        self.spot, self.shard = spot, shard
        self.x, self.core = spot // 2, spot % 2
        self.z, self.y = shard // 2, shard % 2
        ids = [
            (x, c, z, y) for x in range(2) for c in range(2) for z in range(self.depth) for y in range(2)
        ]

        def number(x, c, z, y):
            return ((x * 2 + c) * self.depth + z) * 2 + y

        def perm(to):
            return [(number(*i), number(*to(*i))) for i in ids]

        flip_x = lambda x, c, z, y: (1 - x, c, z, y)
        flip_y = lambda x, c, z, y: (x, c, z, 1 - y)
        self.to_core = perm(lambda x, c, z, y: (x, 1 - c, z, y))
        self.to_x = perm(flip_x)
        self.to_y = perm(flip_y)
        self.swap1 = perm(lambda x, c, z, y: flip_y(x, c, z, y) if c == 0 else flip_x(x, c, z, y))
        self.swap2 = perm(lambda x, c, z, y: flip_x(x, c, z, y) if c == 0 else flip_y(x, c, z, y))
        self.shift_z = [
            perm(lambda x, c, z, y, s=s: (x, c, (z + s) % self.depth, y)) for s in range(self.depth)
        ]

    def send(self, block, perm):
        return lax.ppermute(block, ("dp", "fsdp"), perm)

    def along_z(self, block):
        arrived = [block] + [self.send(block, self.shift_z[s]) for s in range(1, self.depth)]
        return place(arrived, [(self.z + self.depth - s) % self.depth for s in range(self.depth)])

    def gather(self, block, wide):
        x, y, c = self.x, self.y, self.core
        own = self.along_z(block)
        near = self.send(own, self.swap1)
        far = self.send(own, self.swap2)
        both = self.send(near, self.swap2)
        here = [own, near, far, both]
        pieces = here + [self.send(piece, self.to_core) for piece in here]
        places = []
        for core in (c, 1 - c):
            for ux, uy in ((x, y), (x ^ core, y ^ (1 - core)), (x ^ (1 - core), y ^ core), (1 - x, 1 - y)):
                places.append((ux * 2 + core, uy))
        return assemble(pieces, places, self.depth, wide)

    def gather_vectors(self, block):
        rows, cols = block.shape
        padded = jnp.pad(block, ((0, -rows % 16), (0, 0)))
        own = self.along_z(padded)
        other = self.send(own, self.to_y)
        pair = jnp.stack([own, other])
        pair = jnp.where(self.y == 0, pair, pair[::-1])
        pair = pair.reshape(2, self.depth, -1, cols)[:, :, :rows]
        return pair.transpose(2, 1, 0, 3).reshape(rows, -1)

    def plane_order(self):
        x, y, c = self.x, self.y, self.core
        return ((x, y), (x ^ (1 - c), y ^ c), (1 - x, 1 - y), (x ^ c, y ^ (1 - c)))

    def reduce(self, planes):
        kept, first, corner, second = planes
        got_first = self.send(first, self.swap2)
        got_corner = self.send(corner, self.swap2)
        second = (second.astype(f32) + got_corner.astype(f32)).astype(bf16)
        got_second = self.send(second, self.swap1)
        kept = (kept.astype(f32) + got_first.astype(f32) + got_second.astype(f32)).astype(bf16)
        rows = kept.shape[0] // self.depth

        def block_of(z):
            return lax.dynamic_slice_in_dim(kept, z * rows, rows, 0)

        total = block_of(self.z).astype(f32)
        for s in range(1, self.depth):
            got = self.send(block_of((self.z + s) % self.depth), self.shift_z[s])
            total = total + got.astype(f32)
        total = total.astype(bf16)
        from_x = self.send(total, self.to_x)
        return [total, self.send(total, self.to_core), from_x, self.send(from_x, self.to_core)]

    def sum_all(self, values):
        for perm in (self.to_core, self.to_x, self.to_y):
            values = values + self.send(values, perm)
        step = 1
        while step < self.depth:
            flip = [
                (a, b)
                for a in range(4 * self.n_fsdp)
                for b in [(a // self.n_fsdp) * self.n_fsdp + ((((a % self.n_fsdp) // 2) ^ step) * 2 + a % 2)]
            ]
            values = values + self.send(values, flip)
            step *= 2
        return values


def norm_forward(stream, gain, bias):
    centred = stream - jnp.mean(stream, axis=-1, keepdims=True)
    spread = jnp.mean(centred * centred, axis=-1, keepdims=True)
    scale = lax.rsqrt(spread + norm_epsilon)
    unit = centred * scale
    return unit * gain + bias, unit, scale


def norm_backward(grad, unit, scale, gain):
    grad_gain = jnp.sum(grad * unit, axis=0)
    grad_bias = jnp.sum(grad, axis=0)
    scaled = grad * gain
    mean = jnp.mean(scaled, axis=-1, keepdims=True)
    along = jnp.mean(scaled * unit, axis=-1, keepdims=True)
    return scale * (scaled - mean - unit * along), grad_gain, grad_bias


def row_total(values):
    return jnp.sum(values.astype(f32), axis=0)


def column_units(shard):
    return [shard[:, u * D : (u + 1) * D] for u in range(UNITS)]


def on_device(
    n_dp,
    n_fsdp,
    tokens,
    states,
    cotangent,
    seq_len,
    enc_len,
    attn_w,
    attn_m,
    attn_v,
    fc1_w,
    fc1_m,
    fc1_v,
    fc2_w,
    fc2_m,
    fc2_v,
    vec_w,
    vec_m,
    vec_v,
):
    micro, local, length, width = tokens.shape
    enc_length = states.shape[2]
    seqs = micro * local
    shard_rows = attn_w.shape[1]
    linked = n_dp == 4 and n_fsdp == 8
    token_rows = tokens.reshape(seqs * length, width)
    state_rows = states.reshape(seqs * enc_length, width)
    cotan_rows = cotangent.reshape(seqs * length, width)
    tok_lens = seq_len.reshape(seqs)
    enc_lens = enc_len.reshape(seqs)

    if linked:
        links = Links(n_dp, n_fsdp)
        spot = links.spot
        vectors = links.gather_vectors(vec_w.astype(bf16))
        part_a = lax.dynamic_index_in_dim(attn_w, spot, 0, keepdims=False).astype(bf16)
        cross_at = 4 + jnp.where(spot < 2, 3 * spot, spot - 1)
        part_b = lax.dynamic_index_in_dim(attn_w, cross_at, 0, keepdims=False).astype(bf16)
        part_1 = lax.dynamic_slice_in_dim(fc1_w, spot * D, D, 1).astype(bf16)
        part_2 = lax.dynamic_slice_in_dim(fc2_w, spot * shard_rows, shard_rows, 0).astype(bf16)
        self_w = links.gather(part_a, True)
        cross_w = links.gather(part_b, True)
        fc_in = links.gather(part_1, True)
        fc_out = links.gather(part_2, False)
    else:
        vectors = lax.all_gather(vec_w.astype(bf16), "fsdp", axis=1, tiled=True)
        attn = lax.all_gather(attn_w.astype(bf16), "fsdp", axis=1, tiled=True)
        self_w = jnp.concatenate([attn[u] for u in range(4)], axis=1)
        cross_w = jnp.concatenate([attn[u] for u in CROSS_ORDER], axis=1)
        fc_in = lax.all_gather(fc1_w.astype(bf16), "fsdp", axis=0, tiled=True)
        fc_out = lax.all_gather(fc2_w.astype(bf16), "fsdp", axis=0, tiled=True)
    vec = vectors.astype(f32)
    fc_bias = vec[13:].reshape(-1)
    zeros = jnp.zeros((width,), f32)

    qkv_bias = jnp.concatenate([vec[0], zeros, vec[1]])
    qkv = (dot(token_rows, self_w[:, : 3 * D]) + qkv_bias).astype(bf16)
    context = attend(tok_lens, qkv, qkv, qkv, seqs, True, 0, PAIRS, 2 * PAIRS)
    self_out = dot(context, self_w[:, 3 * D :]) + vec[2]
    normed_one, unit_one, scale_one = norm_forward(token_rows.astype(f32) + self_out, vec[7], vec[8])
    normed_one_low = normed_one.astype(bf16)
    cross_q = (dot(normed_one_low, cross_w[:, :D]) + vec[3]).astype(bf16)
    kv_bias = jnp.concatenate([zeros, vec[4]])
    cross_kv = (dot(state_rows, cross_w[:, 2 * D :]) + kv_bias).astype(bf16)
    cross_ctx = attend(enc_lens, cross_q, cross_kv, cross_kv, seqs, False, 0, 0, PAIRS)
    cross_out = dot(cross_ctx, cross_w[:, D : 2 * D]) + vec[5]
    normed_two, unit_two, scale_two = norm_forward(normed_one + cross_out, vec[9], vec[10])
    normed_two_low = normed_two.astype(bf16)
    hidden_pre = dot(normed_two_low, fc_in) + fc_bias
    phi = 0.5 * (1.0 + lax.erf(hidden_pre * 2.0**-0.5))
    hidden = (hidden_pre * phi).astype(bf16)
    slope = phi + hidden_pre * jnp.exp(-0.5 * hidden_pre * hidden_pre) * (2.0 * jnp.pi) ** -0.5
    ffn_out = dot(hidden, fc_out) + vec[6]
    result, unit_three, scale_three = norm_forward(normed_two + ffn_out, vec[11], vec[12])
    mixed = result.astype(bf16).reshape(tokens.shape)
    valid = (jnp.arange(length, dtype=jnp.int32)[None, :] < tok_lens[:, None]).reshape(-1, 1)
    sums = [jnp.sum(jnp.where(valid, a * a, 0.0)) for a in (result, self_out, cross_out, ffn_out)]
    count = jnp.sum(seq_len).astype(f32)

    if linked:
        peer = lambda rows: links.send(rows, links.to_core)
        order = links.plane_order()
        self_in = jnp.concatenate([token_rows, context], axis=1)
        cross_in = jnp.concatenate([normed_one_low, cross_ctx], axis=1)
        self_in_peer, cross_in_peer = peer(self_in), peer(cross_in)
        hidden_peer, normed_two_peer = peer(hidden), peer(normed_two_low)
        core = links.core

    grad_three, grad_g3, grad_b3 = norm_backward(cotan_rows.astype(f32), unit_three, scale_three, vec[11])
    grad_ffn = grad_three.astype(bf16)
    if linked:
        grad_ffn_peer = peer(grad_ffn)
        planes = [
            plane_grad(
                hidden, hidden_peer, grad_ffn, grad_ffn_peer,
                y * UNITS + ux * 2 + core, 0 * y, 2 * UNITS, links.depth, shard_rows,
            )
            for ux, y in order
        ]
        blocks_2 = links.reduce(planes)
    else:
        grad_fc2 = dot_grad(hidden, grad_ffn).astype(bf16)
    grad_pre = (dot_back(grad_ffn, fc_out) * slope).astype(bf16)
    if linked:
        grad_pre_peer = peer(grad_pre)
        planes = [
            plane_grad(
                normed_two_low, normed_two_peer, grad_pre, grad_pre_peer,
                y, ux * 2 + core, 2, links.depth, shard_rows,
            )
            for ux, y in order
        ]
        blocks_1 = links.reduce(planes)
    else:
        grad_fc1 = dot_grad(normed_two_low, grad_pre).astype(bf16)
    grad_normed_two = grad_three + dot_back(grad_pre, fc_in)
    grad_two, grad_g2, grad_b2 = norm_backward(grad_normed_two, unit_two, scale_two, vec[9])
    grad_cross = grad_two.astype(bf16)
    grad_ctx = dot_back(grad_cross, cross_w[:, D : 2 * D]).astype(bf16)
    cross_gq, cross_gk, cross_gv = attend_back(
        enc_lens, cross_q, cross_kv, cross_kv, grad_ctx, seqs, False, 0, 0, PAIRS
    )
    if linked:
        cross_grads = jnp.concatenate([cross_gq, grad_cross], axis=1)
        cross_grads_peer = peer(cross_grads)
        grad_ck = dot_grad(state_rows, cross_gk).astype(bf16)
        grad_cv = dot_grad(state_rows, cross_gv).astype(bf16)
        mine = jnp.where(core == 0, grad_ck, grad_cv)
        theirs = peer(jnp.where(core == 0, grad_cv, grad_ck))
        enc_grad = (mine.astype(f32) + theirs.astype(f32)).astype(bf16)
        enc_grad = enc_grad.reshape(links.depth, 2, shard_rows, D)
        enc_planes = [
            lax.dynamic_index_in_dim(enc_grad, y, 1, keepdims=False).reshape(-1, D)
            for y in (links.y, 1 - links.y)
        ]
        tok_planes = [
            plane_grad(
                cross_in, cross_in_peer, cross_grads, cross_grads_peer,
                core * 2 * links.depth + y, core, 2, links.depth, shard_rows,
            )
            for y in (links.y, 1 - links.y)
        ]
        planes = []
        for ux, y in order:
            tok_plane = jnp.where(y == links.y, tok_planes[0], tok_planes[1])
            enc_plane = jnp.where(y == links.y, enc_planes[0], enc_planes[1])
            planes.append(jnp.where(ux == 0, tok_plane, enc_plane))
        blocks_b = links.reduce(planes)
    else:
        grad_b = [
            dot_grad(normed_one_low, cross_gq),
            dot_grad(state_rows, cross_gk),
            dot_grad(state_rows, cross_gv),
            dot_grad(cross_ctx, grad_cross),
        ]
    grad_states = (
        dot_back(cross_gk, cross_w[:, 2 * D : 3 * D]) + dot_back(cross_gv, cross_w[:, 3 * D :])
    ).astype(bf16)
    grad_normed_one = grad_two + dot_back(cross_gq, cross_w[:, :D])
    grad_one, grad_g1, grad_b1 = norm_backward(grad_normed_one, unit_one, scale_one, vec[7])
    grad_self = grad_one.astype(bf16)
    grad_ctx = dot_back(grad_self, self_w[:, 3 * D :]).astype(bf16)
    self_gq, self_gk, self_gv = attend_back(tok_lens, qkv, qkv, qkv, grad_ctx, seqs, True, 0, PAIRS, 2 * PAIRS)
    if linked:
        self_grads = jnp.concatenate([self_gq, self_gk, self_gv, grad_self], axis=1)
        self_grads_peer = peer(self_grads)
        planes = [
            plane_grad(
                self_in, self_in_peer, self_grads, self_grads_peer,
                y + 2 * links.depth * (ux * core), ux * 2 + core, 2, links.depth, shard_rows,
            )
            for ux, y in order
        ]
        blocks_a = links.reduce(planes)
    else:
        grad_a = [
            dot_grad(token_rows, self_gq),
            dot_grad(token_rows, self_gk),
            dot_grad(token_rows, self_gv),
            dot_grad(context, grad_self),
        ]
        grad_attn = jnp.stack(grad_a + grad_b).astype(bf16)
    grad_tokens = (
        grad_one
        + dot_back(self_gq, self_w[:, :D])
        + dot_back(self_gk, self_w[:, D : 2 * D])
        + dot_back(self_gv, self_w[:, 2 * D : 3 * D])
    ).astype(bf16)
    stat_row = jnp.pad(jnp.stack(sums + [count]), (0, width - 5))
    grad_vec = jnp.concatenate(
        [
            jnp.stack(
                [
                    row_total(self_gq),
                    row_total(self_gv),
                    row_total(grad_self),
                    row_total(cross_gq),
                    row_total(cross_gv),
                    row_total(grad_cross),
                    row_total(grad_ffn),
                    grad_g1,
                    grad_b1,
                    grad_g2,
                    grad_b2,
                    grad_g3,
                    grad_b3,
                ]
            ),
            row_total(grad_pre).reshape(-1, width),
            stat_row[None],
        ],
        axis=0,
    )

    if linked:
        grad_vec = links.sum_all(grad_vec)
        fc2_new = adam_units(
            spot, blocks_2, (fc2_w, fc2_m, fc2_v), (shard_rows, D), lambda u: (u, 0)
        )
        fc1_new = adam_units(
            spot, blocks_1, (fc1_w, fc1_m, fc1_v), (shard_rows, D), lambda u: (0, u)
        )
        attn_state = (attn_w, attn_m, attn_v)
        attn_new = adam_units(
            spot, blocks_b, attn_state, (1, shard_rows, D),
            lambda u: (4 + jnp.where(u < 2, 3 * u, u - 1), 0, 0),
        )
        attn_new = adam_units(
            spot, blocks_a, attn_state, (1, shard_rows, D), lambda u: (u, 0, 0), attn_new
        )
    else:
        grad_vec = lax.psum(grad_vec, ("dp", "fsdp"))

        def owned(grad, dim):
            part = lax.psum_scatter(grad, "fsdp", scatter_dimension=dim, tiled=True)
            return lax.psum(part, "dp").astype(f32)

        attn_new = adam_update(attn_w, attn_m, attn_v, owned(grad_attn, 1), matrix_rate, matrix_decay)
        fc1_new = adam_update(fc1_w, fc1_m, fc1_v, owned(grad_fc1, 0), matrix_rate, matrix_decay)
        fc2_new = adam_update(fc2_w, fc2_m, fc2_v, owned(grad_fc2, 0), matrix_rate, matrix_decay)
    stats = grad_vec[17]
    stream_rms = jnp.sqrt(stats[:4] / (stats[4] * D))
    cols = vec_w.shape[1]
    vec_grad = lax.dynamic_slice_in_dim(grad_vec[:17], lax.axis_index("fsdp") * cols, cols, 1)
    vec_new = adam_update(vec_w, vec_m, vec_v, vec_grad, vector_rate, 0.0)
    return (
        mixed,
        grad_tokens.reshape(tokens.shape),
        grad_states.reshape(states.shape),
        stream_rms,
        *attn_new,
        *fc1_new,
        *fc2_new,
        *vec_new,
    )


def solution(mesh):
    rows = P(None, ("dp", "fsdp"), None, None)
    lens = P(None, ("dp", "fsdp"))
    attn, fc, vec = P(None, "fsdp", None), P("fsdp", None), P(None, "fsdp")
    state = (attn,) * 3 + (fc,) * 6 + (vec,) * 3
    return jax.shard_map(
        partial(on_device, mesh.shape["dp"], mesh.shape["fsdp"]),
        mesh=mesh,
        in_specs=(rows, rows, rows, lens, lens) + state,
        out_specs=(rows, rows, rows, P()) + state,
        check_vma=False,
    )
```

```python
from functools import partial

import jax
import jax.numpy as jnp
from jax import lax
from jax.experimental import pallas as pl
from jax.experimental.pallas import tpu as pltpu
from jax.sharding import PartitionSpec as P

D = 1024
H = 16
DH = 64
STEP = 7
PAIRS = H // 2
UNITS = 4
LANES = 128
TAIL = 16

momentum_decay = 0.9
square_decay = 0.999
matrix_rate = 0.08
vector_rate = 0.3
matrix_decay = 0.01
epsilon = 1e-08
norm_epsilon = 1e-05
fix_first = 1.0 - momentum_decay**STEP
fix_second = 1.0 - square_decay**STEP

f32 = jnp.float32
bf16 = jnp.bfloat16
ANY = pl.BlockSpec(memory_space=pl.ANY)
VMEM_BYTES = 44 * 1024 * 1024
FIRST, SECOND = (0, 1, 5, 6), (2, 3, 4, 7)


def params(**more):
    return pltpu.CompilerParams(vmem_limit_bytes=VMEM_BYTES, **more)


def cost(nbytes):
    return pl.CostEstimate(flops=0, bytes_accessed=int(nbytes), transcendentals=0)


def array(shape, kind=bf16):
    return jax.ShapeDtypeStruct(shape, kind)


def whole(shape):
    return pl.BlockSpec(shape, lambda *at: (0,) * len(shape))


def dot(left, right):
    return jnp.dot(left, right, preferred_element_type=f32)


def dot_back(left, right):
    return lax.dot_general(left, right, (((1,), (1,)), ((), ())), preferred_element_type=f32)


def dot_grad(inputs, grads):
    return lax.dot_general(inputs, grads, (((0,), (0,)), ((), ())), preferred_element_type=f32)


def norm_forward(stream, gain, bias):
    centred = stream - jnp.mean(stream, axis=-1, keepdims=True)
    spread = jnp.mean(centred * centred, axis=-1, keepdims=True)
    scale = lax.rsqrt(spread + norm_epsilon)
    unit = centred * scale
    return unit * gain + bias, unit, scale


def norm_backward(grad, unit, scale, gain):
    scaled = grad * gain
    mean = jnp.mean(scaled, axis=-1, keepdims=True)
    along = jnp.mean(scaled * unit, axis=-1, keepdims=True)
    return scale * (scaled - mean - unit * along), column_sum(grad * unit), column_sum(grad)


def column_sum(values):
    return jnp.sum(values.astype(f32), axis=0, keepdims=True)


def valid_rows(len_ref, rows, length):
    spot = lax.broadcasted_iota(jnp.int32, (rows, 1), 0)
    limit = jnp.full((rows, 1), len_ref[0], jnp.int32)
    for m in range(1, rows // length):
        limit = jnp.where(spot >= m * length, m * length + len_ref[m], limit)
    return spot < limit


def add_up(total_ref, step, part):
    @pl.when(step == 0)
    def _():
        total_ref[...] = part

    @pl.when(step > 0)
    def _():
        total_ref[...] += part


BLOCK = 1024


def project_kernel(x_ref, w_ref, b_ref, o_ref):
    o_ref[...] = (dot(x_ref[...], w_ref[...]) + b_ref[...]).astype(bf16)


def project(rows, weights, bias, at):
    n_rows, depth = rows.shape
    width = bias.shape[1]
    return pl.pallas_call(
        project_kernel,
        out_shape=array((n_rows, width)),
        grid=(width // BLOCK,),
        in_specs=[
            whole((n_rows, depth)),
            pl.BlockSpec((depth, BLOCK), lambda n: (0, at // BLOCK + n)),
            pl.BlockSpec((1, BLOCK), lambda n: (0, n)),
        ],
        out_specs=pl.BlockSpec((n_rows, BLOCK), lambda n: (0, n)),
        compiler_params=params(),
        cost_estimate=cost(1024),
    )(rows, weights, bias)


def join_kernel(length, rows_at, len_ref, x_ref, w_ref, res_ref, vec_ref, *outs):
    h_ref, low_ref, unit_ref, scale_ref, sums_ref, total_ref = outs
    step = pl.program_id(0)
    add_up(total_ref, step, dot(x_ref[...], w_ref[...]))

    @pl.when(step == pl.num_programs(0) - 1)
    def _():
        bias, gain, offset = (vec_ref[r : r + 1, :] for r in rows_at)
        branch = total_ref[...] + bias
        out, unit, scale = norm_forward(res_ref[...].astype(f32) + branch, gain, offset)
        h_ref[...] = out
        low_ref[...] = out.astype(bf16)
        unit_ref[...] = unit
        scale_ref[...] = jnp.broadcast_to(scale, scale_ref.shape)
        valid = valid_rows(len_ref, branch.shape[0], length)
        sums_ref[...] = column_sum(jnp.where(valid, branch * branch, 0.0))


def join(lengths, rows, weights, at, residual, vec, rows_at):
    n_rows = residual.shape[0]
    slot = rows.ndim == 3
    x_spec = (
        pl.BlockSpec((None, n_rows, BLOCK), lambda k, n: (1, 0, k))
        if slot
        else pl.BlockSpec((n_rows, BLOCK), lambda k, n: (0, k))
    )
    return pl.pallas_call(
        partial(join_kernel, n_rows // lengths.shape[0], rows_at),
        out_shape=[
            array((n_rows, D), f32),
            array((n_rows, D)),
            array((n_rows, D), f32),
            array((n_rows, LANES), f32),
            array((1, D), f32),
        ],
        grid_spec=pltpu.PrefetchScalarGridSpec(
            num_scalar_prefetch=1,
            grid=(D // BLOCK,),
            in_specs=[
                x_spec,
                pl.BlockSpec((BLOCK, D), lambda k, n: (k, at // D)),
                whole((n_rows, D)),
                whole(vec.shape),
            ],
            out_specs=[whole((n_rows, D))] * 3 + [whole((n_rows, LANES)), whole((1, D))],
            scratch_shapes=[pltpu.VMEM((n_rows, D), f32)],
        ),
        compiler_params=params(),
        cost_estimate=cost(1024),
    )(lengths, rows, weights, residual, vec)


def hidden_kernel(x_ref, w_ref, b_ref, g_ref, slope_ref):
    u = dot(x_ref[...], w_ref[...]) + b_ref[...]
    phi = 0.5 * (1.0 + lax.erf(u * 2.0**-0.5))
    g_ref[...] = (u * phi).astype(bf16)
    slope_ref[...] = (phi + u * jnp.exp(-0.5 * u * u) * (2.0 * jnp.pi) ** -0.5).astype(bf16)


def hidden_layer(rows, weights, bias):
    n_rows, depth = rows.shape
    width = weights.shape[1]
    out_spec = pl.BlockSpec((n_rows, BLOCK), lambda n: (0, n))
    return pl.pallas_call(
        hidden_kernel,
        out_shape=[array((n_rows, width))] * 2,
        grid=(width // BLOCK,),
        in_specs=[
            whole((n_rows, depth)),
            pl.BlockSpec((depth, BLOCK), lambda n: (0, n)),
            pl.BlockSpec((1, BLOCK), lambda n: (0, n)),
        ],
        out_specs=[out_spec] * 2,
        compiler_params=params(),
        cost_estimate=cost(1024),
    )(rows, weights, bias)


def turn_kernel(length, rows_at, len_ref, x_ref, w_ref, res_ref, cot_ref, vec_ref, *outs):
    mixed_ref, dr_ref, low_ref, sums_ref, total_ref = outs
    step = pl.program_id(0)
    add_up(total_ref, step, dot(x_ref[...], w_ref[...]))

    @pl.when(step == pl.num_programs(0) - 1)
    def _():
        bias, gain, offset = (vec_ref[r : r + 1, :] for r in rows_at)
        branch = total_ref[...] + bias
        out, unit, scale = norm_forward(res_ref[...] + branch, gain, offset)
        mixed_ref[...] = out.astype(bf16)
        valid = valid_rows(len_ref, branch.shape[0], length)
        grad, grad_gain, grad_bias = norm_backward(cot_ref[...].astype(f32), unit, scale, gain)
        low = grad.astype(bf16)
        dr_ref[...] = grad
        low_ref[...] = low
        sums_ref[0:1, :] = column_sum(jnp.where(valid, out * out, 0.0))
        sums_ref[1:2, :] = column_sum(jnp.where(valid, branch * branch, 0.0))
        sums_ref[2:3, :] = grad_gain
        sums_ref[3:4, :] = grad_bias
        sums_ref[4:5, :] = column_sum(low)
        sums_ref[5:8, :] = jnp.zeros((3, D), f32)


def turn(lengths, rows, weights, residual, cotangent, vec, rows_at):
    n_rows, depth = rows.shape
    return pl.pallas_call(
        partial(turn_kernel, n_rows // lengths.shape[0], rows_at),
        out_shape=[array((n_rows, D)), array((n_rows, D), f32), array((n_rows, D)), array((8, D), f32)],
        grid_spec=pltpu.PrefetchScalarGridSpec(
            num_scalar_prefetch=1,
            grid=(depth // BLOCK,),
            in_specs=[
                pl.BlockSpec((n_rows, BLOCK), lambda k, n: (0, k)),
                pl.BlockSpec((BLOCK, D), lambda k, n: (k, 0)),
                whole((n_rows, D)),
                whole((n_rows, D)),
                whole(vec.shape),
            ],
            out_specs=[whole((n_rows, D))] * 3 + [whole((8, D))],
            scratch_shapes=[pltpu.VMEM((n_rows, D), f32)],
        ),
        compiler_params=params(),
        cost_estimate=cost(1024),
    )(lengths, rows, weights, residual, cotangent, vec)


def hidden_back_kernel(e_ref, w_ref, slope_ref, du_ref, sums_ref):
    du = (dot_back(e_ref[...], w_ref[...]) * slope_ref[...].astype(f32)).astype(bf16)
    du_ref[...] = du
    sums_ref[...] = column_sum(du)


def hidden_back(grads, weights, slope):
    n_rows, width = slope.shape
    block = pl.BlockSpec((n_rows, BLOCK), lambda n: (0, n))
    return pl.pallas_call(
        hidden_back_kernel,
        out_shape=[array((n_rows, width)), array((1, width), f32)],
        grid=(width // BLOCK,),
        in_specs=[whole((n_rows, D)), pl.BlockSpec((BLOCK, D), lambda n: (n, 0)), block],
        out_specs=[block, pl.BlockSpec((1, BLOCK), lambda n: (0, n))],
        compiler_params=params(),
        cost_estimate=cost(1024),
    )(grads, weights, slope)


def join_back_kernel(row_at, g_ref, w_ref, dr_ref, unit_ref, scale_ref, vec_ref, after_ref, *outs):
    out_ref, low_ref, next_ref, sums_ref, total_ref = outs
    step = pl.program_id(0)
    add_up(total_ref, step, dot_back(g_ref[...], w_ref[...]))

    @pl.when(step == pl.num_programs(0) - 1)
    def _():
        grad, grad_gain, grad_bias = norm_backward(
            dr_ref[...] + total_ref[...], unit_ref[...], scale_ref[:, 0:1], vec_ref[row_at : row_at + 1, :]
        )
        low = grad.astype(bf16)
        out_ref[...] = grad
        low_ref[...] = low
        next_ref[...] = dot_back(low, after_ref[...]).astype(bf16)
        sums_ref[0:1, :] = grad_gain
        sums_ref[1:2, :] = grad_bias
        sums_ref[2:3, :] = column_sum(low)
        sums_ref[3:8, :] = jnp.zeros((5, D), f32)


def join_back(grads, weights, at, above, unit, scale, vec, row_at, after, after_at):
    slot = grads.ndim == 3
    n_rows, width = grads.shape[-2:]
    g_spec = (
        pl.BlockSpec((None, n_rows, BLOCK), lambda k: (0, 0, k))
        if slot
        else pl.BlockSpec((n_rows, BLOCK), lambda k: (0, k))
    )
    return pl.pallas_call(
        partial(join_back_kernel, row_at),
        out_shape=[array((n_rows, D), f32), array((n_rows, D)), array((n_rows, D)), array((8, D), f32)],
        grid=(width // BLOCK,),
        in_specs=[
            g_spec,
            pl.BlockSpec((D, BLOCK), lambda k: (0, at // BLOCK + k)),
            whole((n_rows, D)),
            whole((n_rows, D)),
            whole((n_rows, LANES)),
            whole(vec.shape),
            pl.BlockSpec((D, D), lambda k: (0, after_at // D)),
        ],
        out_specs=[whole((n_rows, D))] * 3 + [whole((8, D))],
        scratch_shapes=[pltpu.VMEM((n_rows, D), f32)],
        compiler_params=params(),
        cost_estimate=cost(1024),
    )(grads, weights, above, unit, scale, vec, after)


def input_grad_kernel(count, *refs):
    gs, ws, rest, o_ref = refs[:count], refs[count : 2 * count], refs[2 * count : -1], refs[-1]
    total = sum(dot_back(g[...], w[...]) for g, w in zip(gs, ws))
    if rest:
        total = total + rest[0][...]
    o_ref[...] = total.astype(bf16)


def input_grad(grads, slots, weights, ats, block, rest=()):
    n_rows = grads.shape[1]
    row_block = pl.BlockSpec((block, D), lambda r: (r, 0))
    return pl.pallas_call(
        partial(input_grad_kernel, len(slots)),
        out_shape=array((n_rows, D)),
        grid=(n_rows // block,),
        in_specs=[pl.BlockSpec((None, block, D), lambda r, s=s: (s, r, 0)) for s in slots]
        + [pl.BlockSpec((D, D), lambda r, a=a: (0, a // D)) for a in ats]
        + [row_block] * len(rest),
        out_specs=row_block,
        compiler_params=params(),
        cost_estimate=cost(1024),
    )(*[grads] * len(slots), *weights, *rest)


def state_grad_kernel(slot_ref, e_ref, g_ref, o_ref):
    o_ref[...] = dot_grad(e_ref[...], g_ref[...]).astype(bf16)


def state_grad(states, grads, slot):
    n_rows, block = states.shape[0], D // 2
    return pl.pallas_call(
        state_grad_kernel,
        out_shape=array((D, D)),
        grid_spec=pltpu.PrefetchScalarGridSpec(
            num_scalar_prefetch=1,
            grid=(D // block,),
            in_specs=[
                pl.BlockSpec((n_rows, block), lambda r, s: (0, r)),
                pl.BlockSpec((None, n_rows, D), lambda r, s: (s[0], 0, 0)),
            ],
            out_specs=pl.BlockSpec((block, D), lambda r, s: (r, 0)),
        ),
        compiler_params=params(),
        cost_estimate=cost(1024),
    )(jnp.stack([slot]).astype(jnp.int32), states, grads)


def two_heads(rows):
    low_half = lax.broadcasted_iota(jnp.int32, rows.shape, 1) < DH
    zero = jnp.zeros_like(rows)
    return jnp.concatenate([jnp.where(low_half, rows, zero), jnp.where(low_half, zero, rows)], axis=0)


def one_row(both):
    half = both.shape[0] // 2
    low_half = lax.broadcasted_iota(jnp.int32, (half, both.shape[1]), 1) < DH
    return jnp.where(low_half, both[:half], both[half:])


def masked_exp(queries, keys, valid, causal):
    scores = dot_back(queries, keys)
    place = lax.broadcasted_iota(jnp.int32, (1, scores.shape[1]), 1)
    if causal:
        rows = scores.shape[0] // 2
        spot = lax.broadcasted_iota(jnp.int32, scores.shape, 0)
        spot = jnp.where(spot >= rows, spot - rows, spot)
        spots = lax.broadcasted_iota(jnp.int32, scores.shape, 1)
        allowed = (spots <= spot) & (spots < valid)
        scores = jnp.where(allowed, scores, -1e30)
    else:
        scores = scores + jnp.where(place < valid, 0.0, -1e30)
    top = jnp.max(scores, axis=-1, keepdims=True)
    exponent = jnp.exp(scores - top)
    return exponent, 1.0 / jnp.sum(exponent, axis=-1, keepdims=True)


def attend_kernel(causal, len_ref, q_ref, k_ref, v_ref, x_ref, o_ref):
    valid = len_ref[pl.program_id(0)]
    o_ref[0] = x_ref[...]
    for at in range(0, q_ref.shape[1], LANES):
        pair = slice(at, at + LANES)
        queries = two_heads(q_ref[:, pair] * DH**-0.5)
        exponent, inverse = masked_exp(queries, k_ref[:, pair], valid, causal)
        o_ref[1, :, pair] = one_row(dot(exponent.astype(bf16), v_ref[:, pair]) * inverse).astype(bf16)


def attend_back_kernel(causal, len_ref, q_ref, k_ref, v_ref, do_ref, x_ref, dq_ref, *more):
    dkv_refs, sums_ref = more[:-1], more[-1]
    valid = len_ref[pl.program_id(0)]
    dq_ref[dq_ref.shape[0] - 1] = x_ref[...]
    sums_ref[2:8, :] = jnp.zeros((6, sums_ref.shape[1]), f32)
    for at in range(0, q_ref.shape[1], LANES):
        pair = slice(at, at + LANES)
        keys = k_ref[:, pair]
        queries = two_heads(q_ref[:, pair] * DH**-0.5)
        exponent, inverse = masked_exp(queries, keys, valid, causal)
        grads = two_heads(do_ref[:, pair])
        grad_probs = dot_back(grads, v_ref[:, pair])
        row_dot = jnp.sum(exponent * grad_probs, axis=-1, keepdims=True) * inverse
        grad_scores = (exponent * (grad_probs - row_dot)).astype(bf16)
        dq = one_row(dot(grad_scores, keys) * (inverse * DH**-0.5)).astype(bf16)
        dk = dot_grad(grad_scores, (queries * inverse).astype(bf16)).astype(bf16)
        dv = dot_grad(exponent.astype(bf16), (grads * inverse).astype(bf16)).astype(bf16)
        dq_ref[0, :, pair] = dq
        if dkv_refs:
            dkv_refs[0][0, :, pair], dkv_refs[0][1, :, pair] = dk, dv
        else:
            dq_ref[1, :, pair], dq_ref[2, :, pair] = dk, dv
        sums_ref[0:1, pair] = column_sum(dq)
        sums_ref[1:2, pair] = column_sum(dv)


def head_block(rows, at, group):
    return pl.BlockSpec((rows, LANES * group), lambda m, p, n: (m, at // group + p))


def slots_block(slots, rows, group):
    return pl.BlockSpec((slots, rows, LANES * group), lambda m, p, n: (0, m, p))


def attend(lengths, queries, keys, values, beside, seqs, causal, q_at, k_at, v_at):
    q_rows, k_rows = queries.shape[0] // seqs, keys.shape[0] // seqs
    group = PAIRS if causal else PAIRS // 2
    return pl.pallas_call(
        partial(attend_kernel, causal),
        out_shape=array((2, seqs * q_rows, D)),
        grid_spec=pltpu.PrefetchScalarGridSpec(
            num_scalar_prefetch=1,
            grid=(seqs, PAIRS // group),
            in_specs=[
                head_block(q_rows, q_at, group),
                head_block(k_rows, k_at, group),
                head_block(k_rows, v_at, group),
                head_block(q_rows, 0, group),
            ],
            out_specs=slots_block(2, q_rows, group),
        ),
        compiler_params=params(),
        cost_estimate=cost(1024),
    )(lengths, queries, keys, values, beside)


def attend_back(lengths, queries, keys, values, grads, beside, seqs, causal, q_at, k_at, v_at):
    q_rows, k_rows = queries.shape[0] // seqs, keys.shape[0] // seqs
    group = PAIRS if causal else PAIRS // 2
    slots = 4 if causal else 2
    out_shape = [array((slots, seqs * q_rows, D))]
    out_specs = [slots_block(slots, q_rows, group)]
    if not causal:
        out_shape.append(array((2, seqs * k_rows, D)))
        out_specs.append(slots_block(2, k_rows, group))
    out_shape.append(array((8 * seqs, D), f32))
    out_specs.append(head_block(8, 0, group))
    return pl.pallas_call(
        partial(attend_back_kernel, causal),
        out_shape=out_shape,
        grid_spec=pltpu.PrefetchScalarGridSpec(
            num_scalar_prefetch=1,
            grid=(seqs, PAIRS // group),
            in_specs=[
                head_block(q_rows, q_at, group),
                head_block(k_rows, k_at, group),
                head_block(k_rows, v_at, group),
                head_block(q_rows, 0, group),
                head_block(q_rows, 0, group),
            ],
            out_specs=out_specs,
        ),
        compiler_params=params(),
        cost_estimate=cost(1024),
    )(lengths, queries, keys, values, grads, beside)


def place_kernel(rows, idx_ref, *refs):
    slot = 0
    for piece in refs[:-1]:
        for j in range(piece.shape[0] // rows):
            at = pl.multiple_of(idx_ref[slot] * rows, rows)
            refs[-1][pl.ds(at, rows), :] = piece[j * rows : (j + 1) * rows, :]
            slot += 1


def place(pieces, slots):
    total, width = sum(piece.shape[0] for piece in pieces), pieces[0].shape[1]
    return pl.pallas_call(
        partial(place_kernel, total // len(slots)),
        out_shape=array((total, width), pieces[0].dtype),
        grid_spec=pltpu.PrefetchScalarGridSpec(
            num_scalar_prefetch=1,
            grid=(),
            in_specs=[pl.BlockSpec(memory_space=pltpu.VMEM)] * len(pieces),
            out_specs=pl.BlockSpec(memory_space=pltpu.VMEM),
        ),
        compiler_params=params(),
        cost_estimate=cost(1024),
    )(jnp.stack(slots).astype(jnp.int32), *pieces)


def under(first, second):
    return place([first, second], [jnp.int32(0), jnp.int32(1)])


def assemble_kernel(wide, rows, step, counts, idx_ref, *refs):
    pieces, (out_ref, held, in_sems, out_sems) = refs[: len(counts)], refs[len(counts) :]
    loads, at = [], 0
    for i, (piece, count) in enumerate(zip(pieces, counts)):
        loads.append(pltpu.make_async_copy(piece, held.at[pl.ds(at * step, count * step), :], in_sems.at[i]))
        at += count
    for load in loads:
        load.start()
    stores, copy = [], 0
    for load, count in zip(loads, counts):
        load.wait()
        for _ in range(count):
            unit, shard = idx_ref[0, copy], idx_ref[1, copy]
            if wide:
                target = out_ref.at[
                    pl.ds(pl.multiple_of(shard * rows, rows), rows), pl.ds(pl.multiple_of(unit * D, D), D)
                ]
            else:
                row = (shard * UNITS + unit) * rows
                target = out_ref.at[pl.ds(pl.multiple_of(row, rows), rows), :]
            store = pltpu.make_async_copy(held.at[pl.ds(copy * step, rows), :], target, out_sems.at[copy])
            store.start()
            stores.append(store)
            copy += 1
    for store in stores:
        store.wait()


def assemble(pieces, places, rows, step, wide):
    counts = [piece.shape[0] // step for piece in pieces]
    shards = len(places) // UNITS
    return pl.pallas_call(
        partial(assemble_kernel, wide, rows, step, counts),
        out_shape=array((shards * rows, UNITS * D) if wide else (UNITS * shards * rows, D)),
        grid_spec=pltpu.PrefetchScalarGridSpec(
            num_scalar_prefetch=1,
            grid=(),
            in_specs=[ANY] * len(pieces),
            out_specs=ANY,
            scratch_shapes=[
                pltpu.VMEM((len(places) * step, D), bf16),
                pltpu.SemaphoreType.DMA((len(pieces),)),
                pltpu.SemaphoreType.DMA((len(places),)),
            ],
        ),
        compiler_params=params(),
        cost_estimate=cost(1024),
    )(jnp.stack([jnp.stack([place[j] for place in places]) for j in range(2)]).astype(jnp.int32), *pieces)


def store_plane(step, plane, outs):
    @pl.when(step < 2)
    def _():
        outs[0][...] = plane

    @pl.when(step == 2)
    def _():
        outs[1][...] = plane

    @pl.when(step == 3)
    def _():
        outs[2][...] = plane


def planes_kernel(depth, idx_ref, *refs):
    x_mine, x_peer = refs[:depth], refs[depth : 2 * depth]
    inputs = jnp.concatenate(
        [jnp.concatenate([x[...] for x in xs], axis=1) for xs in (x_mine, x_peer)], axis=0
    )
    grads = jnp.concatenate([y[...] for y in refs[2 * depth : 2 * depth + 2]], axis=0)
    store_plane(pl.program_id(0), dot_grad(inputs, grads).astype(bf16), refs[-3:])


def sum_planes_kernel(depth, idx_ref, *refs):
    mine, peer, outs = refs[:depth], refs[depth : 2 * depth], refs[-3:]
    plane = jnp.concatenate([a[...].astype(f32) + b[...].astype(f32) for a, b in zip(mine, peer)], axis=0)
    store_plane(pl.program_id(0), plane.astype(bf16), outs)


def planes_call(kernel, table, in_specs, operands, plane, width):
    return pl.pallas_call(
        kernel,
        out_shape=[array((n * plane, width)) for n in (2, 1, 1)],
        grid_spec=pltpu.PrefetchScalarGridSpec(
            num_scalar_prefetch=1,
            grid=(4,),
            in_specs=in_specs,
            out_specs=[
                pl.BlockSpec((plane, width), lambda k, i: (jnp.minimum(k, 1), 0)),
                pl.BlockSpec((plane, width), lambda k, i: (0, 0)),
                pl.BlockSpec((plane, width), lambda k, i: (0, 0)),
            ],
        ),
        compiler_params=params(),
        cost_estimate=cost(1024),
    )(jnp.stack(table).astype(jnp.int32), *operands)


def column(spots, j):
    return jnp.stack([spot[j] for spot in spots])


def unit_planes(x_mine, x_peer, y_mine, y_peer, spots, z, stride, rows, width=D):
    depth, tokens = 4, x_mine.shape[1]
    blocks = x_mine.shape[2] // rows

    def x_spec(j):
        def at(k, i):
            block = i[0, k] + stride * i[3, j]
            return (block // blocks, 0, block % blocks)

        return pl.BlockSpec((None, tokens, rows), at)

    x_specs = [x_spec(j) for j in range(depth)]
    y_spec = pl.BlockSpec((None, tokens, width), lambda k, i: (i[1, k], 0, i[2, k]))
    table = [column(spots, j) for j in range(3)] + [jnp.stack([z, z ^ 2, z ^ 1, z ^ 3])]
    operands = [x_mine] * depth + [x_peer] * depth + [y_mine, y_peer]
    return planes_call(
        partial(planes_kernel, depth), table, x_specs * 2 + [y_spec] * 2, operands, depth * rows, width
    )


def sum_planes(mine, peer, spots, z, rows, width):
    depth = 4
    specs = [
        pl.BlockSpec((rows, width), lambda k, i, j=j: (2 * i[2, j] + i[0, k], i[1, k])) for j in range(depth)
    ]
    table = [column(spots, j) for j in range(2)] + [jnp.stack([z, z ^ 2, z ^ 1, z ^ 3])]
    return planes_call(
        partial(sum_planes_kernel, depth), table, specs * 2, [mine] * depth + [peer] * depth, depth * rows, width
    )


def adam_update(weight, first, second, grad, rate, decay):
    first = momentum_decay * first + (1.0 - momentum_decay) * grad
    second = square_decay * second + (1.0 - square_decay) * grad * grad
    update = first / fix_first / (jnp.sqrt(second / fix_second) + epsilon) + decay * weight
    return (weight - rate * update, first, second)


def adam_kernel(idx_ref, here_ref, there_ref, w_ref, m_ref, v_ref, *rest):
    w_out, m_out, v_out = rest[-3:]
    away = pl.program_id(0) ^ idx_ref[0]
    grad = jnp.where(away % 2 == 0, here_ref[...], there_ref[...]).astype(f32)
    if len(w_ref.shape) == 3:
        grad = grad[None]
    w_out[...], m_out[...], v_out[...] = adam_update(
        w_ref[...], m_ref[...], v_ref[...], grad, matrix_rate, matrix_decay
    )


def adam_units(spot, grads, state, block_shape, at, earlier=None):
    spec = pl.BlockSpec(block_shape, lambda u, i: at(u))
    rows, width = grads[0].shape[0] // 2, grads[0].shape[1]
    g_spec = pl.BlockSpec((rows, width), lambda u, i: ((u ^ i[0]) // 2, 0))
    extra = list(earlier) if earlier is not None else []
    outs = pl.pallas_call(
        adam_kernel,
        out_shape=[array(a.shape, f32) for a in state],
        grid_spec=pltpu.PrefetchScalarGridSpec(
            num_scalar_prefetch=1,
            grid=(UNITS,),
            in_specs=[g_spec] * 2 + [spec] * 3 + [ANY] * len(extra),
            out_specs=[spec] * 3,
        ),
        input_output_aliases={6 + i: i for i in range(len(extra))},
        compiler_params=params(),
        cost_estimate=cost(1024),
    )(jnp.stack([spot]).astype(jnp.int32), *grads, *state, *extra)
    return list(outs)


def hold(*values):
    return lax.optimization_barrier(values)


class Links:
    def __init__(self, n_dp, n_fsdp):
        self.n_fsdp, self.depth = n_fsdp, n_fsdp // 2
        spot = lax.axis_index("dp")
        shard = lax.axis_index("fsdp")
        self.spot, self.shard = spot, shard
        self.x, self.core = spot // 2, spot % 2
        self.z, self.y = shard // 2, shard % 2
        ids = [
            (x, c, z, y) for x in range(2) for c in range(2) for z in range(self.depth) for y in range(2)
        ]

        def number(x, c, z, y):
            return ((x * 2 + c) * self.depth + z) * 2 + y

        def perm(to):
            return [(number(*i), number(*to(*i))) for i in ids]

        flip_x = lambda x, c, z, y: (1 - x, c, z, y)
        flip_y = lambda x, c, z, y: (x, c, z, 1 - y)
        self.to_core = perm(lambda x, c, z, y: (x, 1 - c, z, y))
        self.to_x = perm(flip_x)
        self.to_y = perm(flip_y)
        self.swap1 = perm(lambda x, c, z, y: flip_y(x, c, z, y) if c == 0 else flip_x(x, c, z, y))
        self.swap2 = perm(lambda x, c, z, y: flip_x(x, c, z, y) if c == 0 else flip_y(x, c, z, y))
        self.to_z1 = perm(lambda x, c, z, y: (x, c, z ^ 1, y))
        self.to_z2 = perm(lambda x, c, z, y: (x, c, z ^ 2, y))

    def send(self, block, perm):
        return lax.ppermute(block, ("dp", "fsdp"), perm)

    def column(self, arrived):
        return place(arrived, [self.z ^ away for away in (0, 2, 1, 3)])

    def kinds(self, core):
        x, y = self.x, self.y
        return ((x, y), (x ^ core, y ^ (1 - core)), (x ^ (1 - core), y ^ core), (1 - x, 1 - y))

    def finish(self, pieces, rows, wide, more=0):
        places = [
            (ux * 2 + core, 2 * z + y)
            for core in (self.core, 1 - self.core)
            for ux, y in self.kinds(core)
            for z in range(self.depth)
        ]
        return assemble(pieces, places, rows, rows + more, wide)

    def vectors(self, here, cols):
        half = here[0].shape[0] // 2
        own, other = [
            piece.reshape(self.depth, -1, D)[:, -TAIL:, : 2 * cols] for piece in (here[0][:half], here[1][half:])
        ]
        pair = [jnp.where(self.y == 0, own, other), jnp.where(self.y == 0, other, own)]
        parts = [pair[f % 2][f // 2] for f in range(self.n_fsdp)]
        return jnp.concatenate(
            [
                jnp.concatenate([part[:, :cols] for part in parts], axis=1),
                jnp.concatenate([part[:1, cols:] for part in parts], axis=1),
            ],
            axis=0,
        )

    def plane_order(self):
        own, near, far, both = self.kinds(self.core)
        return far, both, near, own


def add_kernel(rows, count, *refs):
    ins, outs = refs[: len(rows)], refs[len(rows) :]
    total = sum(a[r : r + count, :].astype(f32) for a, r in zip(ins, rows)).astype(bf16)
    part = count // len(outs)
    for i, out in enumerate(outs):
        out[...] = total[i * part : (i + 1) * part]


def add_rows(terms, count, parts=1):
    width = terms[0][0].shape[1]
    vmem = pl.BlockSpec(memory_space=pltpu.VMEM)
    return pl.pallas_call(
        partial(add_kernel, [r for _, r in terms], count),
        out_shape=[array((count // parts, width))] * parts,
        in_specs=[vmem] * len(terms),
        out_specs=[vmem] * parts,
        compiler_params=params(),
        cost_estimate=cost(1024),
    )(*[a for a, _ in terms])


class Sum:
    def __init__(self, links, planes):
        self.links, self.parts, self.step = links, list(planes), 0

    def add(self):
        parts = self.parts
        if self.step == 1:
            got, second, kept = parts
            half = second.shape[0]
            parts[1:2] = add_rows([(second, 0), (got, half)], half)
        elif self.step == 2:
            got, got_second, kept = parts
            self.parts = add_rows([(kept, 0), (got, 0), (got_second, 0)], kept.shape[0], 2)
        elif self.step == 3:
            self.parts = add_rows([(part, 0) for part in parts], parts[0].shape[0], 2)
        elif self.step == 4:
            self.parts = add_rows([(part, 0) for part in parts], parts[0].shape[0])
        elif self.step == 5:
            self.parts = [under(*parts)]
        self.parts = list(self.parts)

    def send(self):
        links, parts = self.links, self.parts
        if self.step == 0:
            parts[0] = links.send(parts[0], links.swap2)
        elif self.step < 4:
            parts[1] = links.send(parts[1], (links.swap1, links.to_z1, links.to_z2)[self.step - 1])
        elif self.step == 4:
            parts.append(links.send(parts[0], links.to_x))
        else:
            parts.append(links.send(parts[0], links.to_core))
        self.step += 1


def advance(value, *sums):
    def held(value):
        value, *parts = hold(value, *(part for one in sums for part in one.parts))
        for one in sums:
            one.parts, parts = parts[: len(one.parts)], parts[len(one.parts) :]
        return value

    value = held(value)
    for one in sums:
        one.add()
    value = held(value)
    for one in sums:
        one.send()
    return value


def on_device(
    n_dp,
    n_fsdp,
    tokens,
    states,
    cotangent,
    seq_len,
    enc_len,
    attn_w,
    attn_m,
    attn_v,
    fc1_w,
    fc1_m,
    fc1_v,
    fc2_w,
    fc2_m,
    fc2_v,
    vec_w,
    vec_m,
    vec_v,
):
    micro, local, length, width = tokens.shape
    enc_length = states.shape[2]
    seqs = micro * local
    shard_rows = attn_w.shape[1]
    linked = n_dp == 4 and n_fsdp == 8 and vec_w.shape[0] == TAIL + 1
    token_rows = tokens.reshape(seqs * length, width)
    state_rows = states.reshape(seqs * enc_length, width)
    cotan_rows = cotangent.reshape(seqs * length, width)
    tok_lens = seq_len.reshape(seqs)
    enc_lens = enc_len.reshape(seqs)

    if linked:
        links = Links(n_dp, n_fsdp)
        spot, core = links.spot, links.core
        peer = lambda rows: links.send(rows, links.to_core)
        part_a = lax.dynamic_index_in_dim(attn_w, spot + jnp.where(spot < 2, 0, 3), 0, keepdims=False).astype(bf16)
        part_b = lax.dynamic_index_in_dim(attn_w, spot + jnp.where(spot < 3, 2, 4), 0, keepdims=False).astype(bf16)
        part_1 = lax.dynamic_slice_in_dim(fc1_w, spot * D, D, 1).astype(bf16)
        part_2 = lax.dynamic_slice_in_dim(fc2_w, spot * shard_rows, shard_rows, 0).astype(bf16)
        vec_cols = vec_w.shape[1]
        small = vec_w.astype(bf16)
        small = jnp.concatenate(
            [
                small[:TAIL],
                jnp.pad(small[TAIL:], ((0, TAIL - 1), (0, 0))),
                jnp.zeros((TAIL, D - 2 * vec_cols), bf16),
            ],
            axis=1,
        )
        part_a = jnp.concatenate([part_a, small], axis=0)

        to_z1, to_z2, swap1, swap2 = links.to_z1, links.to_z2, links.swap1, links.swap2
        send = links.send
        a_2, a_1 = send(part_a, to_z2), send(part_a, to_z1)
        part_b, a_2, a_1 = hold(part_b, a_2, a_1)
        a_3, b_2 = send(a_2, to_z1), send(part_b, to_z2)
        a_own = links.column([part_a, a_2, a_1, a_3])
        a_near = send(a_own, swap1)
        part_1, b_2, a_near = hold(part_1, b_2, a_near)

        a_here = [under(a_own, a_near)]
        a_here.append(send(a_here[0], swap2))
        b_1, c_2 = send(under(part_b, b_2), to_z1), send(part_1, to_z2)
        a_there = [peer(a_here[0])]
        part_2, b_1, c_2 = hold(part_2, b_1, c_2)
        b_own = links.column([part_b, b_2, b_1])
        b_near = send(b_own, swap1)
        c_1 = send(under(part_1, c_2), to_z1)
        part_2, c_1, b_near, a_here[1], a_there[0] = hold(part_2, c_1, b_near, a_here[1], a_there[0])

        b_here = [under(b_own, b_near)]
        b_here.append(send(b_here[0], swap2))
        c_own = links.column([part_1, c_2, c_1])
        c_near = send(c_own, swap1)
        d_2 = send(part_2, to_z2)
        a_there.append(peer(a_here[1]))
        first_w = links.finish(a_here + a_there, shard_rows, True, TAIL)
        vectors = links.vectors(a_here, vec_cols)
    else:
        vectors = lax.all_gather(vec_w.astype(bf16), "fsdp", axis=1, tiled=True)
        attn = lax.all_gather(attn_w.astype(bf16), "fsdp", axis=1, tiled=True)
        first_w = jnp.concatenate([attn[u] for u in FIRST], axis=1)
        second_w = jnp.concatenate([attn[u] for u in SECOND], axis=1)
        fc_in = lax.all_gather(fc1_w.astype(bf16), "fsdp", axis=0, tiled=True)
        fc_out = lax.all_gather(fc2_w.astype(bf16), "fsdp", axis=0, tiled=True)
    vec = vectors.astype(f32)
    zeros = jnp.zeros((1, width), f32)
    qk_bias = jnp.concatenate([vec[0:1], zeros], axis=1)
    kv_bias = jnp.concatenate([zeros, vec[4:5]], axis=1)
    fc_bias = vec[13:].reshape(1, -1)

    queries_keys = project(token_rows, first_w, qk_bias, 0)
    if linked:
        queries_keys, first_w, d_2 = hold(queries_keys, first_w, d_2)
        d_1 = send(under(part_2, d_2), to_z1)
        b_there = [peer(b_here[0])]
    cross_kv = project(state_rows, first_w, kv_bias, 2 * D)
    if linked:
        cross_kv, d_1, c_near, b_here[1], b_there[0] = hold(cross_kv, d_1, c_near, b_here[1], b_there[0])
        c_here = [under(c_own, c_near)]
        c_here.append(send(c_here[0], swap2))
        d_own = links.column([part_2, d_2, d_1])
        d_near = send(d_own, swap1)
        b_there.append(peer(b_here[1]))
        second_w = links.finish(b_here + b_there, shard_rows, True)
        c_there = [peer(c_here[0])]
    values = project(token_rows, second_w, vec[1:2], 0)
    self_in = attend(tok_lens, queries_keys, queries_keys, values, token_rows, seqs, True, 0, PAIRS, 0)
    if linked:
        self_in_peer = peer(self_in)
    normed_one, normed_one_low, unit_one, scale_one, sums_one = join(
        tok_lens, self_in, second_w, D, token_rows, vec, (2, 7, 8)
    )
    cross_q = project(normed_one_low, second_w, vec[3:4], 2 * D)
    cross_in = attend(enc_lens, cross_q, cross_kv, cross_kv, normed_one_low, seqs, False, 0, 0, PAIRS)
    normed_two, normed_two_low, unit_two, scale_two, sums_two = join(
        tok_lens, cross_in, second_w, 3 * D, normed_one, vec, (5, 9, 10)
    )
    if linked:
        normed_two_low, d_near, c_here[1], c_there[0] = hold(normed_two_low, d_near, c_here[1], c_there[0])
        d_here = [under(d_own, d_near)]
        d_here.append(send(d_here[0], swap2))
        c_there.append(peer(c_here[1]))
        fc_in = links.finish(c_here + c_there, shard_rows, True)
        d_there = [peer(d_here[0])]
        cross_in_peer = peer(cross_in)
    hidden, slope = hidden_layer(normed_two_low, fc_in, fc_bias)
    if linked:
        hidden_peer, normed_two_peer = peer(hidden), peer(normed_two_low)
        hidden, d_here[1], d_there[0] = hold(hidden, d_here[1], d_there[0])
        d_there.append(peer(d_here[1]))
        fc_out = links.finish(d_here + d_there, shard_rows, False)
    mixed, grad_three, grad_ffn, sums_three = turn(
        tok_lens, hidden, fc_out, normed_two, cotan_rows, vec, (6, 11, 12)
    )

    if linked:
        order = links.plane_order()

        def planes_of(x_mine, x_peer, y_mine, y_peer, x_at, y_at, stride, width=D):
            spots = [(x_at(ux, y), *y_at(ux)) for ux, y in order]
            slots = [a if a.ndim == 3 else a[None] for a in (x_mine, x_peer, y_mine, y_peer)]
            return unit_planes(*slots, spots, links.z, stride, shard_rows, width)

        grad_ffn_peer = peer(grad_ffn)
    grad_pre, sums_pre = hidden_back(grad_ffn, fc_out, slope)
    if linked:
        grad_pre, grad_ffn_peer = hold(grad_pre, grad_ffn_peer)
        grad_pre_peer = peer(grad_pre)
        planes = planes_of(
            hidden, hidden_peer, grad_ffn, grad_ffn_peer,
            lambda ux, y: y * UNITS + ux * 2 + core, lambda ux: (0 * ux, 0 * ux), 2 * UNITS,
        )
        sum_2 = Sum(links, planes)
        grad_pre, grad_pre_peer = hold(grad_pre, grad_pre_peer)
        grad_pre = advance(grad_pre, sum_2)
    else:
        grad_fc2 = dot_grad(hidden, grad_ffn).astype(bf16)
    grad_two, grad_cross, grad_ctx, sums_back_two = join_back(
        grad_pre, fc_in, 0, grad_three, unit_two, scale_two, vec, 9, second_w, 3 * D
    )
    if linked:
        planes = planes_of(
            normed_two_low, normed_two_peer, grad_pre, grad_pre_peer,
            lambda ux, y: y, lambda ux: (0 * ux, ux * 2 + core), 2,
        )
        sum_1 = Sum(links, planes)
        grad_ctx = advance(grad_ctx, sum_1)
    else:
        grad_fc1 = dot_grad(normed_two_low, grad_pre).astype(bf16)
    cross_grads, cross_dkv, sums_cross = attend_back(
        enc_lens, cross_q, cross_kv, cross_kv, grad_ctx, grad_cross, seqs, False, 0, 0, PAIRS
    )
    if linked:
        cross_grads = advance(cross_grads, sum_2)
        cross_grads_peer = peer(cross_grads)
    grad_one, grad_self, grad_ctx, sums_back_one = join_back(
        cross_grads, second_w, 2 * D, grad_two, unit_one, scale_one, vec, 7, second_w, D
    )
    if linked:
        grad_ctx, cross_grads_peer = hold(grad_ctx, cross_grads_peer)
        planes_t = planes_of(
            cross_in, cross_in_peer, cross_grads, cross_grads_peer,
            lambda ux, y: core * 2 * links.depth + y, lambda ux: (core + 0 * ux, ux), 2, D // 2,
        )
        grad_ctx, *planes_t = hold(grad_ctx, *planes_t)
    self_grads, sums_self = attend_back(
        tok_lens, queries_keys, queries_keys, values, grad_ctx, grad_self, seqs, True, 0, PAIRS, 0
    )
    sums_cross = sums_cross.reshape(seqs, 8, width).sum(axis=0)
    sums_self = sums_self.reshape(seqs, 8, width).sum(axis=0)
    grad_vec = jnp.concatenate(
        [
            sums_self[0:2],
            sums_back_one[2:3],
            sums_cross[0:2],
            sums_back_two[2:3],
            sums_three[4:5],
            sums_back_one[0:2],
            sums_back_two[0:2],
            sums_three[2:4],
            sums_pre.reshape(-1, width),
            sums_three[0:1],
            sums_one,
            sums_two,
            sums_three[1:2],
            jnp.broadcast_to(jnp.sum(seq_len).astype(f32), (1, width)),
        ],
        axis=0,
    )
    n_vec = vec_w.shape[0]
    if linked:
        self_grads = advance(self_grads, sum_1, sum_2)
        sum_t = Sum(links, planes_t)
        self_grads = advance(self_grads, sum_t)
        self_grads_peer, vec_peer = peer(self_grads), peer(grad_vec)
        self_grads, cross_dkv = hold(self_grads, cross_dkv)
        theirs = state_grad(state_rows, cross_dkv, 1 - core)
        theirs, self_grads_peer, vec_peer = hold(theirs, self_grads_peer, vec_peer)
        theirs = advance(theirs, sum_t, sum_2)
        grad_vec = grad_vec + vec_peer
        vec_peer = send(grad_vec, to_z1)
        planes = planes_of(
            self_in, self_in_peer, self_grads, self_grads_peer,
            lambda ux, y: y + 2 * links.depth * (ux * core), lambda ux: (ux * 2 + core, 0 * ux), 2,
        )
        sum_a = Sum(links, planes)
        theirs = advance(theirs, sum_a, sum_1)
        theirs_peer = peer(theirs)
        cross_dkv, theirs = hold(cross_dkv, theirs)
        mine = state_grad(state_rows, cross_dkv, core)
        mine, theirs_peer, vec_peer = hold(mine, theirs_peer, vec_peer)
        grad_vec = grad_vec + vec_peer
        vec_peer = send(grad_vec, to_z2)
        planes = sum_planes(
            mine, theirs_peer, [(y, ux) for ux, y in order], links.z, shard_rows, D // 2
        )
        sum_e = Sum(links, planes)
        self_grads = advance(self_grads, sum_e, sum_t, sum_2)
    else:
        grad_attn = jnp.stack(
            [dot_grad(self_in[u // 3], self_grads[u]) for u in range(4)]
            + [
                dot_grad(normed_one_low, cross_grads[0]),
                dot_grad(state_rows, cross_dkv[0]),
                dot_grad(state_rows, cross_dkv[1]),
                dot_grad(cross_in[1], cross_grads[1]),
            ]
        ).astype(bf16)
    grad_tokens = input_grad(
        self_grads, (0, 1, 2), (first_w, first_w, second_w), (0, D, 0), seqs * length, (grad_one,)
    )
    if linked:
        cross_dkv, grad_tokens, vec_peer = hold(cross_dkv, grad_tokens, vec_peer)
        cross_dkv = advance(cross_dkv, sum_1)
        grad_vec = grad_vec + vec_peer
        vec_peer = send(grad_vec, swap1)
    grad_states = input_grad(cross_dkv, (0, 1), (first_w, first_w), (2 * D, 3 * D), BLOCK)

    if linked:
        state_1, state_2 = (fc1_w, fc1_m, fc1_v), (fc2_w, fc2_m, fc2_v)
        attn_state = (attn_w, attn_m, attn_v)
        grad_states = advance(grad_states, sum_a, sum_t)
        grad_states, vec_peer = hold(grad_states, vec_peer)
        grad_vec = grad_vec + vec_peer
        vec_peer = send(grad_vec, swap2)
        grad_states = advance(grad_states, sum_e, sum_1, sum_2)
        fc2_new = adam_units(spot, sum_2.parts, state_2, (shard_rows, D), lambda u: (u, 0))
        fc2_new[0], vec_peer = hold(fc2_new[0], vec_peer)
        grad_vec = grad_vec + vec_peer
        fc2_new[0] = advance(fc2_new[0], sum_a, sum_t, sum_1)
        fc1_new = adam_units(spot, sum_1.parts, state_1, (shard_rows, D), lambda u: (0, u))
        fc1_new[0] = advance(fc1_new[0], sum_e, sum_t)
        fc1_new[0] = advance(fc1_new[0], sum_a)
        attn_new = adam_units(
            spot, sum_t.parts, attn_state, (1, shard_rows, D // 2), lambda u: (4 + 3 * (u % 2), 0, u // 2)
        )
        attn_new[0] = advance(attn_new[0], sum_e)
        attn_new[0] = advance(attn_new[0], sum_a)
        attn_new[0] = advance(attn_new[0], sum_e)
        attn_new[0] = advance(attn_new[0], sum_a)
        attn_new[0] = advance(attn_new[0], sum_e)
        attn_new = adam_units(
            spot, sum_a.parts, attn_state, (1, shard_rows, D), lambda u: (u, 0, 0), attn_new
        )
        attn_new = adam_units(
            spot, sum_e.parts, attn_state, (1, shard_rows, D // 2), lambda u: (5 + u % 2, 0, u // 2), attn_new
        )
    else:
        grad_vec = lax.psum(grad_vec, ("dp", "fsdp"))

        def owned(grad, dim):
            part = lax.psum_scatter(grad, "fsdp", scatter_dimension=dim, tiled=True)
            return lax.psum(part, "dp").astype(f32)

        attn_new = adam_update(attn_w, attn_m, attn_v, owned(grad_attn, 1), matrix_rate, matrix_decay)
        fc1_new = adam_update(fc1_w, fc1_m, fc1_v, owned(grad_fc1, 0), matrix_rate, matrix_decay)
        fc2_new = adam_update(fc2_w, fc2_m, fc2_v, owned(grad_fc2, 0), matrix_rate, matrix_decay)
    stats = grad_vec[n_vec:]
    stream_rms = jnp.sqrt(jnp.sum(stats[:4], axis=1) / (stats[4, 0] * D))
    cols = vec_w.shape[1]
    vec_grad = lax.dynamic_slice_in_dim(grad_vec[:n_vec], lax.axis_index("fsdp") * cols, cols, 1)
    vec_new = adam_update(vec_w, vec_m, vec_v, vec_grad, vector_rate, 0.0)
    return (
        mixed.reshape(tokens.shape),
        grad_tokens.reshape(tokens.shape),
        grad_states.reshape(states.shape),
        stream_rms,
        *attn_new,
        *fc1_new,
        *fc2_new,
        *vec_new,
    )


def solution(mesh):
    rows = P(None, ("dp", "fsdp"), None, None)
    lens = P(None, ("dp", "fsdp"))
    attn, fc, vec = P(None, "fsdp", None), P("fsdp", None), P(None, "fsdp")
    state = (attn,) * 3 + (fc,) * 6 + (vec,) * 3
    return jax.shard_map(
        partial(on_device, mesh.shape["dp"], mesh.shape["fsdp"]),
        mesh=mesh,
        in_specs=(rows, rows, rows, lens, lens) + state,
        out_specs=(rows, rows, rows, P()) + state,
        check_vma=False,
    )
```

```python
from functools import partial

import jax
import jax.numpy as jnp
from jax import lax
from jax.experimental import pallas as pl
from jax.experimental.pallas import tpu as pltpu
from jax.sharding import PartitionSpec as P

D = 1024
H = 16
DH = 64
STEP = 7
PAIRS = H // 2
UNITS = 4
LANES = 128
TAIL = 16

momentum_decay = 0.9
square_decay = 0.999
matrix_rate = 0.08
vector_rate = 0.3
matrix_decay = 0.01
epsilon = 1e-08
norm_epsilon = 1e-05
fix_first = 1.0 - momentum_decay**STEP
fix_second = 1.0 - square_decay**STEP

f32 = jnp.float32
bf16 = jnp.bfloat16
ANY = pl.BlockSpec(memory_space=pl.ANY)
MIB = 1024 * 1024
FIRST, SECOND = (0, 1, 5, 6), (2, 3, 4, 7)


def params(mib):
    return pltpu.CompilerParams(vmem_limit_bytes=mib * MIB)


def cost(nbytes):
    return pl.CostEstimate(flops=0, bytes_accessed=int(nbytes), transcendentals=0)


def array(shape, kind=bf16):
    return jax.ShapeDtypeStruct(shape, kind)


def whole(shape):
    return pl.BlockSpec(shape, lambda *at: (0,) * len(shape))


def far(values):
    return pltpu.with_memory_space_constraint(values, pltpu.HBM)


def dot(left, right):
    return jnp.dot(left, right, preferred_element_type=f32)


def dot_back(left, right):
    return lax.dot_general(left, right, (((1,), (1,)), ((), ())), preferred_element_type=f32)


def dot_grad(inputs, grads):
    return lax.dot_general(inputs, grads, (((0,), (0,)), ((), ())), preferred_element_type=f32)


def norm_forward(stream, gain, bias):
    centred = stream - jnp.mean(stream, axis=-1, keepdims=True)
    spread = jnp.mean(centred * centred, axis=-1, keepdims=True)
    scale = lax.rsqrt(spread + norm_epsilon)
    unit = centred * scale
    return unit * gain + bias, unit, scale


def norm_backward(grad, unit, scale, gain):
    scaled = grad * gain
    mean = jnp.mean(scaled, axis=-1, keepdims=True)
    along = jnp.mean(scaled * unit, axis=-1, keepdims=True)
    return scale * (scaled - mean - unit * along), column_sum(grad * unit), column_sum(grad)


def column_sum(values):
    return jnp.sum(values.astype(f32), axis=0, keepdims=True)


def valid_rows(len_ref, rows, length):
    spot = lax.broadcasted_iota(jnp.int32, (rows, 1), 0)
    limit = jnp.full((rows, 1), len_ref[0], jnp.int32)
    for m in range(1, rows // length):
        limit = jnp.where(spot >= m * length, m * length + len_ref[m], limit)
    return spot < limit


def add_up(total_ref, step, part):
    @pl.when(step == 0)
    def _():
        total_ref[...] = part

    @pl.when(step > 0)
    def _():
        total_ref[...] += part


BLOCK = 1024


def project_kernel(x_ref, w_ref, b_ref, o_ref):
    o_ref[...] = (dot(x_ref[...], w_ref[...]) + b_ref[...]).astype(bf16)


def project(rows, weights, bias, at):
    n_rows, depth = rows.shape
    width = bias.shape[1]
    return pl.pallas_call(
        project_kernel,
        out_shape=array((n_rows, width)),
        grid=(width // BLOCK,),
        in_specs=[
            whole((n_rows, depth)),
            pl.BlockSpec((depth, BLOCK), lambda n: (0, at // BLOCK + n)),
            pl.BlockSpec((1, BLOCK), lambda n: (0, n)),
        ],
        out_specs=pl.BlockSpec((n_rows, BLOCK), lambda n: (0, n)),
        compiler_params=params(22),
        cost_estimate=cost(1024),
    )(rows, weights, bias)


def join_kernel(length, rows_at, len_ref, x_ref, w_ref, res_ref, vec_ref, *outs):
    h_ref, low_ref, unit_ref, scale_ref, sums_ref, total_ref = outs
    step = pl.program_id(0)
    add_up(total_ref, step, dot(x_ref[...], w_ref[...]))

    @pl.when(step == pl.num_programs(0) - 1)
    def _():
        bias, gain, offset = (vec_ref[r : r + 1, :] for r in rows_at)
        branch = total_ref[...] + bias
        out, unit, scale = norm_forward(res_ref[...].astype(f32) + branch, gain, offset)
        h_ref[...] = out
        low_ref[...] = out.astype(bf16)
        unit_ref[...] = unit
        scale_ref[...] = jnp.broadcast_to(scale, scale_ref.shape)
        valid = valid_rows(len_ref, branch.shape[0], length)
        sums_ref[...] = column_sum(jnp.where(valid, branch * branch, 0.0))


def join(lengths, rows, weights, at, residual, vec, rows_at):
    n_rows = residual.shape[0]
    slot = rows.ndim == 3
    x_spec = (
        pl.BlockSpec((None, n_rows, BLOCK), lambda k, n: (1, 0, k))
        if slot
        else pl.BlockSpec((n_rows, BLOCK), lambda k, n: (0, k))
    )
    return pl.pallas_call(
        partial(join_kernel, n_rows // lengths.shape[0], rows_at),
        out_shape=[
            array((n_rows, D), f32),
            array((n_rows, D)),
            array((n_rows, D), f32),
            array((n_rows, LANES), f32),
            array((1, D), f32),
        ],
        grid_spec=pltpu.PrefetchScalarGridSpec(
            num_scalar_prefetch=1,
            grid=(D // BLOCK,),
            in_specs=[
                x_spec,
                pl.BlockSpec((BLOCK, D), lambda k, n: (k, at // D)),
                whole((n_rows, D)),
                whole(vec.shape),
            ],
            out_specs=[whole((n_rows, D))] * 3 + [whole((n_rows, LANES)), whole((1, D))],
            scratch_shapes=[pltpu.VMEM((n_rows, D), f32)],
        ),
        compiler_params=params(12),
        cost_estimate=cost(1024),
    )(lengths, rows, weights, residual, vec)


def hidden_kernel(x_ref, w_ref, b_ref, g_ref, slope_ref):
    u = dot(x_ref[...], w_ref[...]) + b_ref[...]
    phi = 0.5 * (1.0 + lax.erf(u * 2.0**-0.5))
    g_ref[...] = (u * phi).astype(bf16)
    slope_ref[...] = (phi + u * jnp.exp(-0.5 * u * u) * (2.0 * jnp.pi) ** -0.5).astype(bf16)


def hidden_layer(rows, weights, bias):
    n_rows, depth = rows.shape
    width = weights.shape[1]
    out_spec = pl.BlockSpec((n_rows, BLOCK), lambda n: (0, n))
    return pl.pallas_call(
        hidden_kernel,
        out_shape=[array((n_rows, width))] * 2,
        grid=(width // BLOCK,),
        in_specs=[
            whole((n_rows, depth)),
            pl.BlockSpec((depth, BLOCK), lambda n: (0, n)),
            pl.BlockSpec((1, BLOCK), lambda n: (0, n)),
        ],
        out_specs=[out_spec] * 2,
        compiler_params=params(14),
        cost_estimate=cost(1024),
    )(rows, weights, bias)


def turn_kernel(length, rows_at, len_ref, x_ref, w_ref, res_ref, cot_ref, vec_ref, *outs):
    mixed_ref, dr_ref, low_ref, sums_ref, total_ref = outs
    step = pl.program_id(0)
    add_up(total_ref, step, dot(x_ref[...], w_ref[...]))

    @pl.when(step == pl.num_programs(0) - 1)
    def _():
        bias, gain, offset = (vec_ref[r : r + 1, :] for r in rows_at)
        branch = total_ref[...] + bias
        out, unit, scale = norm_forward(res_ref[...] + branch, gain, offset)
        mixed_ref[...] = out.astype(bf16)
        valid = valid_rows(len_ref, branch.shape[0], length)
        grad, grad_gain, grad_bias = norm_backward(cot_ref[...].astype(f32), unit, scale, gain)
        low = grad.astype(bf16)
        dr_ref[...] = grad
        low_ref[...] = low
        sums_ref[0:1, :] = column_sum(jnp.where(valid, out * out, 0.0))
        sums_ref[1:2, :] = column_sum(jnp.where(valid, branch * branch, 0.0))
        sums_ref[2:3, :] = grad_gain
        sums_ref[3:4, :] = grad_bias
        sums_ref[4:5, :] = column_sum(low)
        sums_ref[5:8, :] = jnp.zeros((3, D), f32)


def turn(lengths, rows, weights, residual, cotangent, vec, rows_at):
    n_rows, depth = rows.shape
    return pl.pallas_call(
        partial(turn_kernel, n_rows // lengths.shape[0], rows_at),
        out_shape=[array((n_rows, D)), array((n_rows, D), f32), array((n_rows, D)), array((8, D), f32)],
        grid_spec=pltpu.PrefetchScalarGridSpec(
            num_scalar_prefetch=1,
            grid=(depth // BLOCK,),
            in_specs=[
                pl.BlockSpec((n_rows, BLOCK), lambda k, n: (0, k)),
                pl.BlockSpec((BLOCK, D), lambda k, n: (k, 0)),
                whole((n_rows, D)),
                whole((n_rows, D)),
                whole(vec.shape),
            ],
            out_specs=[whole((n_rows, D))] * 3 + [whole((8, D))],
            scratch_shapes=[pltpu.VMEM((n_rows, D), f32)],
        ),
        compiler_params=params(14),
        cost_estimate=cost(1024),
    )(lengths, rows, weights, residual, cotangent, vec)


def hidden_back_kernel(e_ref, w_ref, slope_ref, du_ref, sums_ref):
    du = (dot_back(e_ref[...], w_ref[...]) * slope_ref[...].astype(f32)).astype(bf16)
    du_ref[...] = du
    sums_ref[...] = column_sum(du)


def hidden_back(grads, weights, slope):
    n_rows, width = slope.shape
    block = pl.BlockSpec((n_rows, BLOCK), lambda n: (0, n))
    return pl.pallas_call(
        hidden_back_kernel,
        out_shape=[array((n_rows, width)), array((1, width), f32)],
        grid=(width // BLOCK,),
        in_specs=[whole((n_rows, D)), pl.BlockSpec((BLOCK, D), lambda n: (n, 0)), block],
        out_specs=[block, pl.BlockSpec((1, BLOCK), lambda n: (0, n))],
        compiler_params=params(14),
        cost_estimate=cost(1024),
    )(grads, weights, slope)


def join_back_kernel(row_at, g_ref, w_ref, dr_ref, unit_ref, scale_ref, vec_ref, after_ref, *outs):
    out_ref, low_ref, next_ref, sums_ref, total_ref = outs
    step = pl.program_id(0)
    add_up(total_ref, step, dot_back(g_ref[...], w_ref[...]))

    @pl.when(step == pl.num_programs(0) - 1)
    def _():
        grad, grad_gain, grad_bias = norm_backward(
            dr_ref[...] + total_ref[...], unit_ref[...], scale_ref[:, 0:1], vec_ref[row_at : row_at + 1, :]
        )
        low = grad.astype(bf16)
        out_ref[...] = grad
        low_ref[...] = low
        next_ref[...] = dot_back(low, after_ref[...]).astype(bf16)
        sums_ref[0:1, :] = grad_gain
        sums_ref[1:2, :] = grad_bias
        sums_ref[2:3, :] = column_sum(low)
        sums_ref[3:8, :] = jnp.zeros((5, D), f32)


def join_back(grads, weights, at, above, unit, scale, vec, row_at, after, after_at):
    slot = grads.ndim == 3
    n_rows, width = grads.shape[-2:]
    g_spec = (
        pl.BlockSpec((None, n_rows, BLOCK), lambda k: (0, 0, k))
        if slot
        else pl.BlockSpec((n_rows, BLOCK), lambda k: (0, k))
    )
    return pl.pallas_call(
        partial(join_back_kernel, row_at),
        out_shape=[array((n_rows, D), f32), array((n_rows, D)), array((n_rows, D)), array((8, D), f32)],
        grid=(width // BLOCK,),
        in_specs=[
            g_spec,
            pl.BlockSpec((D, BLOCK), lambda k: (0, at // BLOCK + k)),
            whole((n_rows, D)),
            whole((n_rows, D)),
            whole((n_rows, LANES)),
            whole(vec.shape),
            pl.BlockSpec((D, D), lambda k: (0, after_at // D)),
        ],
        out_specs=[whole((n_rows, D))] * 3 + [whole((8, D))],
        scratch_shapes=[pltpu.VMEM((n_rows, D), f32)],
        compiler_params=params(18),
        cost_estimate=cost(1024),
    )(grads, far(weights), above, far(unit), scale, vec, far(after))


def input_grad_kernel(count, *refs):
    gs, ws, rest, o_ref = refs[:count], refs[count : 2 * count], refs[2 * count : -1], refs[-1]
    total = sum(dot_back(g[...], w[...]) for g, w in zip(gs, ws))
    if rest:
        total = total + rest[0][...]
    o_ref[...] = total.astype(bf16)


def input_grad(grads, slots, weights, ats, block, rest=()):
    n_rows = grads.shape[1]
    row_block = pl.BlockSpec((block, D), lambda r: (r, 0))
    return pl.pallas_call(
        partial(input_grad_kernel, len(slots)),
        out_shape=array((n_rows, D)),
        grid=(n_rows // block,),
        in_specs=[pl.BlockSpec((None, block, D), lambda r, s=s: (s, r, 0)) for s in slots]
        + [pl.BlockSpec((D, D), lambda r, a=a: (0, a // D)) for a in ats]
        + [row_block] * len(rest),
        out_specs=row_block,
        compiler_params=params(22),
        cost_estimate=cost(1024),
    )(*[far(grads)] * len(slots), *[far(w) for w in weights], *rest)


def state_grad_kernel(slot_ref, e_ref, g_ref, o_ref):
    o_ref[...] = dot_grad(e_ref[...], g_ref[...]).astype(bf16)


def state_grad(states, grads, slot):
    n_rows, block = states.shape[0], D // 2
    return pl.pallas_call(
        state_grad_kernel,
        out_shape=array((D, D)),
        grid_spec=pltpu.PrefetchScalarGridSpec(
            num_scalar_prefetch=1,
            grid=(D // block,),
            in_specs=[
                pl.BlockSpec((n_rows, block), lambda r, s: (0, r)),
                pl.BlockSpec((None, n_rows, D), lambda r, s: (s[0], 0, 0)),
            ],
            out_specs=pl.BlockSpec((block, D), lambda r, s: (r, 0)),
        ),
        compiler_params=params(18),
        cost_estimate=cost(1024),
    )(jnp.stack([slot]).astype(jnp.int32), states, far(grads))


def two_heads(rows):
    low_half = lax.broadcasted_iota(jnp.int32, rows.shape, 1) < DH
    zero = jnp.zeros_like(rows)
    return jnp.concatenate([jnp.where(low_half, rows, zero), jnp.where(low_half, zero, rows)], axis=0)


def one_row(both):
    half = both.shape[0] // 2
    low_half = lax.broadcasted_iota(jnp.int32, (half, both.shape[1]), 1) < DH
    return jnp.where(low_half, both[:half], both[half:])


def masked_exp(queries, keys, valid, causal):
    scores = dot_back(queries, keys)
    place = lax.broadcasted_iota(jnp.int32, (1, scores.shape[1]), 1)
    if causal:
        rows = scores.shape[0] // 2
        spot = lax.broadcasted_iota(jnp.int32, scores.shape, 0)
        spot = jnp.where(spot >= rows, spot - rows, spot)
        spots = lax.broadcasted_iota(jnp.int32, scores.shape, 1)
        allowed = (spots <= spot) & (spots < valid)
        scores = jnp.where(allowed, scores, -1e30)
    else:
        scores = scores + jnp.where(place < valid, 0.0, -1e30)
    top = jnp.max(scores, axis=-1, keepdims=True)
    exponent = jnp.exp(scores - top)
    return exponent, 1.0 / jnp.sum(exponent, axis=-1, keepdims=True)


def attend_kernel(causal, len_ref, q_ref, k_ref, v_ref, x_ref, o_ref):
    valid = len_ref[pl.program_id(0)]
    o_ref[0] = x_ref[...]
    for at in range(0, q_ref.shape[1], LANES):
        pair = slice(at, at + LANES)
        queries = two_heads(q_ref[:, pair] * DH**-0.5)
        exponent, inverse = masked_exp(queries, k_ref[:, pair], valid, causal)
        o_ref[1, :, pair] = one_row(dot(exponent.astype(bf16), v_ref[:, pair]) * inverse).astype(bf16)


def attend_back_kernel(causal, len_ref, q_ref, k_ref, v_ref, do_ref, x_ref, dq_ref, *more):
    dkv_refs, sums_ref = more[:-1], more[-1]
    valid = len_ref[pl.program_id(0)]
    dq_ref[dq_ref.shape[0] - 1] = x_ref[...]
    sums_ref[2:8, :] = jnp.zeros((6, sums_ref.shape[1]), f32)
    for at in range(0, q_ref.shape[1], LANES):
        pair = slice(at, at + LANES)
        keys = k_ref[:, pair]
        queries = two_heads(q_ref[:, pair] * DH**-0.5)
        exponent, inverse = masked_exp(queries, keys, valid, causal)
        grads = two_heads(do_ref[:, pair])
        grad_probs = dot_back(grads, v_ref[:, pair])
        row_dot = jnp.sum(exponent * grad_probs, axis=-1, keepdims=True) * inverse
        grad_scores = (exponent * (grad_probs - row_dot)).astype(bf16)
        dq = one_row(dot(grad_scores, keys) * (inverse * DH**-0.5)).astype(bf16)
        dk = dot_grad(grad_scores, (queries * inverse).astype(bf16)).astype(bf16)
        dv = dot_grad(exponent.astype(bf16), (grads * inverse).astype(bf16)).astype(bf16)
        dq_ref[0, :, pair] = dq
        if dkv_refs:
            dkv_refs[0][0, :, pair], dkv_refs[0][1, :, pair] = dk, dv
        else:
            dq_ref[1, :, pair], dq_ref[2, :, pair] = dk, dv
        sums_ref[0:1, pair] = column_sum(dq)
        sums_ref[1:2, pair] = column_sum(dv)


def head_block(rows, at, group):
    return pl.BlockSpec((rows, LANES * group), lambda m, p, n: (m, at // group + p))


def slots_block(slots, rows, group):
    return pl.BlockSpec((slots, rows, LANES * group), lambda m, p, n: (0, m, p))


def attend(lengths, queries, keys, values, beside, seqs, causal, q_at, k_at, v_at):
    q_rows, k_rows = queries.shape[0] // seqs, keys.shape[0] // seqs
    group = PAIRS if causal else PAIRS // 2
    return pl.pallas_call(
        partial(attend_kernel, causal),
        out_shape=array((2, seqs * q_rows, D)),
        grid_spec=pltpu.PrefetchScalarGridSpec(
            num_scalar_prefetch=1,
            grid=(seqs, PAIRS // group),
            in_specs=[
                head_block(q_rows, q_at, group),
                head_block(k_rows, k_at, group),
                head_block(k_rows, v_at, group),
                head_block(q_rows, 0, group),
            ],
            out_specs=slots_block(2, q_rows, group),
        ),
        compiler_params=params(20),
        cost_estimate=cost(1024),
    )(lengths, queries, keys, values, beside)


def attend_back(lengths, queries, keys, values, grads, beside, seqs, causal, q_at, k_at, v_at):
    q_rows, k_rows = queries.shape[0] // seqs, keys.shape[0] // seqs
    group = PAIRS if causal else PAIRS // 2
    slots = 4 if causal else 2
    out_shape = [array((slots, seqs * q_rows, D))]
    out_specs = [slots_block(slots, q_rows, group)]
    if not causal:
        out_shape.append(array((2, seqs * k_rows, D)))
        out_specs.append(slots_block(2, k_rows, group))
    out_shape.append(array((8 * seqs, D), f32))
    out_specs.append(head_block(8, 0, group))
    return pl.pallas_call(
        partial(attend_back_kernel, causal),
        out_shape=out_shape,
        grid_spec=pltpu.PrefetchScalarGridSpec(
            num_scalar_prefetch=1,
            grid=(seqs, PAIRS // group),
            in_specs=[
                head_block(q_rows, q_at, group),
                head_block(k_rows, k_at, group),
                head_block(k_rows, v_at, group),
                head_block(q_rows, 0, group),
                head_block(q_rows, 0, group),
            ],
            out_specs=out_specs,
        ),
        compiler_params=params(22),
        cost_estimate=cost(1024),
    )(lengths, queries, keys, values, grads, beside)


def place_kernel(rows, idx_ref, *refs):
    slot = 0
    for piece in refs[:-1]:
        for j in range(piece.shape[0] // rows):
            at = pl.multiple_of(idx_ref[slot] * rows, rows)
            refs[-1][pl.ds(at, rows), :] = piece[j * rows : (j + 1) * rows, :]
            slot += 1


def place(pieces, slots):
    total, width = sum(piece.shape[0] for piece in pieces), pieces[0].shape[1]
    return pl.pallas_call(
        partial(place_kernel, total // len(slots)),
        out_shape=array((total, width), pieces[0].dtype),
        grid_spec=pltpu.PrefetchScalarGridSpec(
            num_scalar_prefetch=1,
            grid=(),
            in_specs=[pl.BlockSpec(memory_space=pltpu.VMEM)] * len(pieces),
            out_specs=pl.BlockSpec(memory_space=pltpu.VMEM),
        ),
        compiler_params=params(6),
        cost_estimate=cost(1024),
    )(jnp.stack(slots).astype(jnp.int32), *pieces)


def under(first, second):
    return place([first, second], [jnp.int32(0), jnp.int32(1)])


def assemble_kernel(wide, rows, step, counts, idx_ref, *refs):
    pieces, (out_ref, held, in_sems, out_sems) = refs[: len(counts)], refs[len(counts) :]
    loads, at = [], 0
    for i, (piece, count) in enumerate(zip(pieces, counts)):
        loads.append(pltpu.make_async_copy(piece, held.at[pl.ds(at * step, count * step), :], in_sems.at[i]))
        at += count
    for load in loads:
        load.start()
    stores, copy = [], 0
    for load, count in zip(loads, counts):
        load.wait()
        for _ in range(count):
            unit, shard = idx_ref[0, copy], idx_ref[1, copy]
            if wide:
                target = out_ref.at[
                    pl.ds(pl.multiple_of(shard * rows, rows), rows), pl.ds(pl.multiple_of(unit * D, D), D)
                ]
            else:
                row = (shard * UNITS + unit) * rows
                target = out_ref.at[pl.ds(pl.multiple_of(row, rows), rows), :]
            store = pltpu.make_async_copy(held.at[pl.ds(copy * step, rows), :], target, out_sems.at[copy])
            store.start()
            stores.append(store)
            copy += 1
    for store in stores:
        store.wait()


def assemble(pieces, places, rows, step, wide):
    counts = [piece.shape[0] // step for piece in pieces]
    shards = len(places) // UNITS
    return pl.pallas_call(
        partial(assemble_kernel, wide, rows, step, counts),
        out_shape=array((shards * rows, UNITS * D) if wide else (UNITS * shards * rows, D)),
        grid_spec=pltpu.PrefetchScalarGridSpec(
            num_scalar_prefetch=1,
            grid=(),
            in_specs=[ANY] * len(pieces),
            out_specs=ANY,
            scratch_shapes=[
                pltpu.VMEM((len(places) * step, D), bf16),
                pltpu.SemaphoreType.DMA((len(pieces),)),
                pltpu.SemaphoreType.DMA((len(places),)),
            ],
        ),
        compiler_params=params(10),
        cost_estimate=cost(1024),
    )(jnp.stack([jnp.stack([place[j] for place in places]) for j in range(2)]).astype(jnp.int32), *pieces)


def store_plane(step, plane, outs):
    @pl.when(step < 2)
    def _():
        outs[0][...] = plane

    @pl.when(step == 2)
    def _():
        outs[1][...] = plane

    @pl.when(step == 3)
    def _():
        outs[2][...] = plane


def planes_kernel(depth, idx_ref, *refs):
    x_mine, x_peer = refs[:depth], refs[depth : 2 * depth]
    inputs = jnp.concatenate(
        [jnp.concatenate([x[...] for x in xs], axis=1) for xs in (x_mine, x_peer)], axis=0
    )
    grads = jnp.concatenate([y[...] for y in refs[2 * depth : 2 * depth + 2]], axis=0)
    store_plane(pl.program_id(0), dot_grad(inputs, grads).astype(bf16), refs[-3:])


def sum_planes_kernel(depth, idx_ref, *refs):
    mine, peer, outs = refs[:depth], refs[depth : 2 * depth], refs[-3:]
    plane = jnp.concatenate([a[...].astype(f32) + b[...].astype(f32) for a, b in zip(mine, peer)], axis=0)
    store_plane(pl.program_id(0), plane.astype(bf16), outs)


def planes_call(kernel, table, in_specs, operands, plane, width):
    return pl.pallas_call(
        kernel,
        out_shape=[array((n * plane, width)) for n in (2, 1, 1)],
        grid_spec=pltpu.PrefetchScalarGridSpec(
            num_scalar_prefetch=1,
            grid=(4,),
            in_specs=in_specs,
            out_specs=[
                pl.BlockSpec((plane, width), lambda k, i: (jnp.minimum(k, 1), 0)),
                pl.BlockSpec((plane, width), lambda k, i: (0, 0)),
                pl.BlockSpec((plane, width), lambda k, i: (0, 0)),
            ],
        ),
        compiler_params=params(13),
        cost_estimate=cost(1024),
    )(jnp.stack(table).astype(jnp.int32), *operands)


def column(spots, j):
    return jnp.stack([spot[j] for spot in spots])


def unit_planes(x_mine, x_peer, y_mine, y_peer, spots, z, stride, rows, width=D):
    depth, tokens = 4, x_mine.shape[1]
    blocks = x_mine.shape[2] // rows

    def x_spec(j):
        def at(k, i):
            block = i[0, k] + stride * i[3, j]
            return (block // blocks, 0, block % blocks)

        return pl.BlockSpec((None, tokens, rows), at)

    x_specs = [x_spec(j) for j in range(depth)]
    y_spec = pl.BlockSpec((None, tokens, width), lambda k, i: (i[1, k], 0, i[2, k]))
    table = [column(spots, j) for j in range(3)] + [jnp.stack([z, z ^ 2, z ^ 1, z ^ 3])]
    if x_peer.shape[2] > 2 * D:
        x_mine, x_peer = far(x_mine), far(x_peer)
    operands = [x_mine] * depth + [x_peer] * depth + [y_mine, y_peer]
    return planes_call(
        partial(planes_kernel, depth), table, x_specs * 2 + [y_spec] * 2, operands, depth * rows, width
    )


def sum_planes(mine, peer, spots, z, rows, width):
    depth = 4
    specs = [
        pl.BlockSpec((rows, width), lambda k, i, j=j: (2 * i[2, j] + i[0, k], i[1, k])) for j in range(depth)
    ]
    table = [column(spots, j) for j in range(2)] + [jnp.stack([z, z ^ 2, z ^ 1, z ^ 3])]
    return planes_call(
        partial(sum_planes_kernel, depth), table, specs * 2, [mine] * depth + [peer] * depth, depth * rows, width
    )


def adam_update(weight, first, second, grad, rate, decay):
    first = momentum_decay * first + (1.0 - momentum_decay) * grad
    second = square_decay * second + (1.0 - square_decay) * grad * grad
    update = first / fix_first / (jnp.sqrt(second / fix_second) + epsilon) + decay * weight
    return (weight - rate * update, first, second)


def adam_kernel(idx_ref, here_ref, there_ref, w_ref, m_ref, v_ref, *rest):
    w_out, m_out, v_out = rest[-3:]
    away = pl.program_id(0) ^ idx_ref[0]
    grad = jnp.where(away % 2 == 0, here_ref[...], there_ref[...]).astype(f32)
    if len(w_ref.shape) == 3:
        grad = grad[None]
    w_out[...], m_out[...], v_out[...] = adam_update(
        w_ref[...], m_ref[...], v_ref[...], grad, matrix_rate, matrix_decay
    )


def adam_units(spot, grads, state, block_shape, at, earlier=None):
    spec = pl.BlockSpec(block_shape, lambda u, i: at(u))
    rows, width = grads[0].shape[0] // 2, grads[0].shape[1]
    g_spec = pl.BlockSpec((rows, width), lambda u, i: ((u ^ i[0]) // 2, 0))
    extra = list(earlier) if earlier is not None else []
    state = [far(a) for a in state]
    outs = pl.pallas_call(
        adam_kernel,
        out_shape=[array(a.shape, f32) for a in state],
        grid_spec=pltpu.PrefetchScalarGridSpec(
            num_scalar_prefetch=1,
            grid=(UNITS,),
            in_specs=[g_spec] * 2 + [spec] * 3 + [ANY] * len(extra),
            out_specs=[spec] * 3,
        ),
        input_output_aliases={6 + i: i for i in range(len(extra))},
        compiler_params=params(8),
        cost_estimate=cost(1024),
    )(jnp.stack([spot]).astype(jnp.int32), *grads, *state, *extra)
    return list(outs)


CLOCK = []


def hold(*values):
    CLOCK[0], *held = lax.optimization_barrier((CLOCK[0], *values))
    return held


class Links:
    def __init__(self, n_dp, n_fsdp):
        self.n_fsdp, self.depth = n_fsdp, n_fsdp // 2
        spot = lax.axis_index("dp")
        shard = lax.axis_index("fsdp")
        self.spot, self.shard = spot, shard
        self.x, self.core = spot // 2, spot % 2
        self.z, self.y = shard // 2, shard % 2
        ids = [
            (x, c, z, y) for x in range(2) for c in range(2) for z in range(self.depth) for y in range(2)
        ]

        def number(x, c, z, y):
            return ((x * 2 + c) * self.depth + z) * 2 + y

        def perm(to):
            return [(number(*i), number(*to(*i))) for i in ids]

        flip_x = lambda x, c, z, y: (1 - x, c, z, y)
        flip_y = lambda x, c, z, y: (x, c, z, 1 - y)
        self.to_core = perm(lambda x, c, z, y: (x, 1 - c, z, y))
        self.to_x = perm(flip_x)
        self.to_y = perm(flip_y)
        self.swap1 = perm(lambda x, c, z, y: flip_y(x, c, z, y) if c == 0 else flip_x(x, c, z, y))
        self.swap2 = perm(lambda x, c, z, y: flip_x(x, c, z, y) if c == 0 else flip_y(x, c, z, y))
        self.to_z1 = perm(lambda x, c, z, y: (x, c, z ^ 1, y))
        self.to_z2 = perm(lambda x, c, z, y: (x, c, z ^ 2, y))

    def send(self, block, perm):
        return lax.ppermute(block, ("dp", "fsdp"), perm)

    def column(self, arrived):
        return place(arrived, [self.z ^ away for away in (0, 2, 1, 3)])

    def kinds(self, core):
        x, y = self.x, self.y
        return ((x, y), (x ^ core, y ^ (1 - core)), (x ^ (1 - core), y ^ core), (1 - x, 1 - y))

    def finish(self, pieces, rows, wide, more=0):
        places = [
            (ux * 2 + core, 2 * z + y)
            for core in (self.core, 1 - self.core)
            for ux, y in self.kinds(core)
            for z in range(self.depth)
        ]
        return assemble(pieces, places, rows, rows + more, wide)

    def vectors(self, here, cols):
        half = here[0].shape[0] // 2
        step = half // self.depth

        def tails(piece, first):
            return jnp.stack(
                [
                    lax.slice(piece, (first + (z + 1) * step - TAIL, 0), (first + (z + 1) * step, 2 * cols))
                    for z in range(self.depth)
                ]
            )

        own, other = tails(here[0], 0), tails(here[1], half)
        pair = [jnp.where(self.y == 0, own, other), jnp.where(self.y == 0, other, own)]
        parts = [pair[f % 2][f // 2] for f in range(self.n_fsdp)]
        return jnp.concatenate(
            [
                jnp.concatenate([part[:, :cols] for part in parts], axis=1),
                jnp.concatenate([part[:1, cols:] for part in parts], axis=1),
            ],
            axis=0,
        )

    def plane_order(self):
        own, near, far, both = self.kinds(self.core)
        return far, both, near, own


def add_kernel(rows, count, *refs):
    ins, outs = refs[: len(rows)], refs[len(rows) :]
    total = sum(a[r : r + count, :].astype(f32) for a, r in zip(ins, rows)).astype(bf16)
    part = count // len(outs)
    for i, out in enumerate(outs):
        out[...] = total[i * part : (i + 1) * part]


def add_rows(terms, count, parts=1):
    width = terms[0][0].shape[1]
    vmem = pl.BlockSpec(memory_space=pltpu.VMEM)
    return pl.pallas_call(
        partial(add_kernel, [r for _, r in terms], count),
        out_shape=[array((count // parts, width))] * parts,
        in_specs=[vmem] * len(terms),
        out_specs=[vmem] * parts,
        compiler_params=params(8),
        cost_estimate=cost(1024),
    )(*[a for a, _ in terms])


class Sum:
    def __init__(self, links, planes):
        self.links, self.parts, self.step = links, list(planes), 0

    def add(self):
        parts = self.parts
        if self.step == 1:
            got, second, kept = parts
            half = second.shape[0]
            parts[1:2] = add_rows([(second, 0), (got, half)], half)
        elif self.step == 2:
            got, got_second, kept = parts
            self.parts = add_rows([(kept, 0), (got, 0), (got_second, 0)], kept.shape[0], 2)
        elif self.step == 3:
            self.parts = add_rows([(part, 0) for part in parts], parts[0].shape[0], 2)
        elif self.step == 4:
            self.parts = add_rows([(part, 0) for part in parts], parts[0].shape[0])
        elif self.step == 5:
            self.parts = [under(*parts)]
        self.parts = list(self.parts)

    def send(self):
        links, parts = self.links, self.parts
        if self.step == 0:
            parts[0] = links.send(parts[0], links.swap2)
        elif self.step < 4:
            parts[1] = links.send(parts[1], (links.swap1, links.to_z1, links.to_z2)[self.step - 1])
        elif self.step == 4:
            parts.append(links.send(parts[0], links.to_x))
        else:
            parts.append(links.send(parts[0], links.to_core))
        self.step += 1


def land(sums, *values):
    parts = hold(*values, *(part for one in sums for part in one.parts))
    values, parts = parts[: len(values)], parts[len(values) :]
    for one in sums:
        one.parts, parts = parts[: len(one.parts)], parts[len(one.parts) :]
    return values


def add(*sums):
    for one in sums:
        one.add()


def go(*sums):
    for one in sums:
        one.send()


PLAN = (
    ("", "give grad_ffn", "give hidden"),
    ("hidden", "land grad_ffn", "land hidden", "give grad_pre", "give normed_two_low"),
    ("planes_2", "land grad_pre", "land normed_two_low", "sum 2"),
    ("two",),
    ("planes_1",),
    ("", "sum 1"),
    ("cross", "sum 2", "give cross_grads"),
    ("one", "land cross_grads"),
    ("self",),
    ("planes_t", "sum 1", "sum 2", "give self_grads", "vec c"),
    ("", "sum t"),
    ("theirs", "land self_grads", "land vec", "sum 2", "give theirs"),
    ("planes_a", "vec z1", "sum 1", "sum t"),
    ("", "sum a"),
    ("mine", "land theirs", "land vec", "vec z2", "sum t"),
    ("planes_e", "sum 2"),
    ("tokens", "vec s1", "sum 1", "sum e", "land vec"),
    ("", "sum a", "sum t", "sum 2"),
    ("states", "land vec", "vec s2"),
    ("", "sum 1"),
    ("adam_2", "sum e", "sum a"),
    ("", "sum t", "sum 1"),
    ("adam_1", "sum e", "sum t", "land vec"),
    ("", "sum a"),
    ("adam_t", "sum e"),
    ("", "sum a"),
    ("", "sum e"),
    ("", "sum a", "sum e"),
    ("adam_e",),
    ("adam_a",),
)


def on_device(
    n_dp,
    n_fsdp,
    tokens,
    states,
    cotangent,
    seq_len,
    enc_len,
    attn_w,
    attn_m,
    attn_v,
    fc1_w,
    fc1_m,
    fc1_v,
    fc2_w,
    fc2_m,
    fc2_v,
    vec_w,
    vec_m,
    vec_v,
):
    micro, local, length, width = tokens.shape
    enc_length = states.shape[2]
    seqs = micro * local
    shard_rows = attn_w.shape[1]
    linked = n_dp == 4 and n_fsdp == 8 and vec_w.shape[0] == TAIL + 1
    token_rows = tokens.reshape(seqs * length, width)
    state_rows = states.reshape(seqs * enc_length, width)
    cotan_rows = cotangent.reshape(seqs * length, width)
    tok_lens = seq_len.reshape(seqs)
    enc_lens = enc_len.reshape(seqs)

    if linked:
        links = Links(n_dp, n_fsdp)
        spot, core = links.spot, links.core
        peer = lambda rows: links.send(rows, links.to_core)
        part_a = lax.dynamic_index_in_dim(attn_w, spot + jnp.where(spot < 2, 0, 3), 0, keepdims=False).astype(bf16)
        part_b = lax.dynamic_index_in_dim(attn_w, spot + jnp.where(spot < 3, 2, 4), 0, keepdims=False).astype(bf16)
        part_1 = lax.dynamic_slice_in_dim(fc1_w, spot * D, D, 1).astype(bf16)
        part_2 = lax.dynamic_slice_in_dim(fc2_w, spot * shard_rows, shard_rows, 0).astype(bf16)
        vec_cols = vec_w.shape[1]
        small = vec_w.astype(bf16)
        small = jnp.concatenate(
            [
                small[:TAIL],
                jnp.pad(small[TAIL:], ((0, TAIL - 1), (0, 0))),
                jnp.zeros((TAIL, D - 2 * vec_cols), bf16),
            ],
            axis=1,
        )
        part_a = jnp.concatenate([part_a, small], axis=0)

        to_z1, to_z2, swap1, swap2 = links.to_z1, links.to_z2, links.swap1, links.swap2
        send = links.send
        CLOCK[:] = [vec_m]
        a_2, a_1 = send(part_a, to_z2), send(part_a, to_z1)
        part_a, part_b, a_2, a_1 = hold(part_a, part_b, a_2, a_1)

        a_3, b_2, b_1 = send(a_2, to_z1), send(part_b, to_z2), send(part_b, to_z1)
        (a_3,) = hold(a_3)
        a_own = links.column([part_a, a_2, a_1, a_3])
        a_near = send(a_own, swap1)
        part_b, part_1, b_2, b_1, a_near = hold(part_b, part_1, b_2, b_1, a_near)

        a_here = [under(a_own, a_near)]
        a_here.append(send(a_here[0], swap2))
        b_3, c_2 = send(b_2, to_z1), send(part_1, to_z2)
        part_1, b_3, c_2 = hold(part_1, b_3, c_2)
        b_own = links.column([part_b, b_2, b_1, b_3])
        b_near = send(b_own, swap1)
        c_1 = send(under(part_1, c_2), to_z1)
        a_there = [peer(a_here[0])]
        part_1, c_1 = hold(part_1, c_1)
        c_own = links.column([part_1, c_2, c_1])
        c_own, part_2, b_own, b_near, *held = hold(c_own, part_2, b_own, b_near, *a_here, a_there[0])
        a_here, a_there = held[:2], held[2:]

        c_near = send(c_own, swap1)
        b_here = [under(b_own, b_near)]
        b_here.append(send(b_here[0], swap2))
        d_2 = send(part_2, to_z2)
        a_there.append(peer(a_here[1]))
        first_w = links.finish(a_here + a_there, shard_rows, True, TAIL)
        vectors = links.vectors(a_here, vec_cols)
    else:
        vectors = lax.all_gather(vec_w.astype(bf16), "fsdp", axis=1, tiled=True)
        attn = lax.all_gather(attn_w.astype(bf16), "fsdp", axis=1, tiled=True)
        first_w = jnp.concatenate([attn[u] for u in FIRST], axis=1)
        second_w = jnp.concatenate([attn[u] for u in SECOND], axis=1)
        fc_in = lax.all_gather(fc1_w.astype(bf16), "fsdp", axis=0, tiled=True)
        fc_out = lax.all_gather(fc2_w.astype(bf16), "fsdp", axis=0, tiled=True)
    vec = vectors.astype(f32)
    zeros = jnp.zeros((1, width), f32)
    qk_bias = jnp.concatenate([vec[0:1], zeros], axis=1)
    kv_bias = jnp.concatenate([zeros, vec[4:5]], axis=1)
    fc_bias = vec[13:].reshape(1, -1)

    queries_keys = project(token_rows, first_w, qk_bias, 0)
    if linked:
        queries_keys, first_w, part_2, d_2 = hold(queries_keys, first_w, part_2, d_2)
        d_1 = send(under(part_2, d_2), to_z1)
        b_there = [peer(b_here[0])]
    cross_kv = project(state_rows, first_w, kv_bias, 2 * D)
    if linked:
        cross_kv, d_1 = hold(cross_kv, d_1)
        d_own = links.column([part_2, d_2, d_1])
        d_own, c_own, c_near, b_here[1], b_there[0] = hold(d_own, c_own, c_near, b_here[1], b_there[0])
        c_here = [under(c_own, c_near)]
        c_here.append(send(c_here[0], swap2))
        d_near = send(d_own, swap1)
        b_there.append(peer(b_here[1]))
        second_w = links.finish(b_here + b_there, shard_rows, True)
        c_there = [peer(c_here[0])]
    values = project(token_rows, second_w, vec[1:2], 0)
    self_in = attend(tok_lens, queries_keys, queries_keys, values, token_rows, seqs, True, 0, PAIRS, 0)
    if linked:
        self_in_peer = peer(self_in)
    normed_one, normed_one_low, unit_one, scale_one, sums_one = join(
        tok_lens, self_in, second_w, D, token_rows, vec, (2, 7, 8)
    )
    cross_q = project(normed_one_low, second_w, vec[3:4], 2 * D)
    cross_in = attend(enc_lens, cross_q, cross_kv, cross_kv, normed_one_low, seqs, False, 0, 0, PAIRS)
    normed_two, normed_two_low, unit_two, scale_two, sums_two = join(
        tok_lens, cross_in, second_w, 3 * D, normed_one, vec, (5, 9, 10)
    )
    if linked:
        normed_two_low, d_own, d_near, c_here[1], c_there[0] = hold(
            normed_two_low, d_own, d_near, c_here[1], c_there[0]
        )
        d_here = [under(d_own, d_near)]
        d_here.append(send(d_here[0], swap2))
        c_there.append(peer(c_here[1]))
        fc_in = links.finish(c_here + c_there, shard_rows, True)
        d_there = [peer(d_here[0])]
        cross_in_peer = peer(cross_in)
    hidden, slope = hidden_layer(normed_two_low, fc_in, fc_bias)
    if linked:
        hidden, normed_two_low, d_here[1], d_there[0] = hold(hidden, normed_two_low, d_here[1], d_there[0])
        d_there.append(peer(d_here[1]))
        fc_out = links.finish(d_here + d_there, shard_rows, False)
    mixed, grad_three, grad_ffn, sums_three = turn(
        tok_lens, hidden, fc_out, normed_two, cotan_rows, vec, (6, 11, 12)
    )

    env = dict(
        hidden=hidden, normed_two_low=normed_two_low, grad_three=grad_three, grad_ffn=grad_ffn, self_in=self_in,
        cross_in=cross_in, sums_three=sums_three,
    )

    def k_hidden(e):
        e["grad_pre"], e["sums_pre"] = hidden_back(e["grad_ffn"], fc_out, slope)

    def k_two(e):
        e["grad_two"], e["grad_cross"], e["grad_ctx"], e["sums_two"] = join_back(
            e["grad_pre"], fc_in, 0, grad_three, unit_two, scale_two, vec, 9, second_w, 3 * D
        )

    def k_cross(e):
        e["cross_grads"], e["cross_dkv"], e["sums_cross"] = attend_back(
            enc_lens, cross_q, cross_kv, cross_kv, e["grad_ctx"], e["grad_cross"], seqs, False, 0, 0, PAIRS
        )

    def k_one(e):
        e["grad_one"], e["grad_self"], e["grad_ctx"], e["sums_one"] = join_back(
            e["cross_grads"], second_w, 2 * D, e["grad_two"], unit_one, scale_one, vec, 7, second_w, D
        )

    def k_self(e):
        e["self_grads"], sums_self = attend_back(
            tok_lens, queries_keys, queries_keys, values, e["grad_ctx"], e["grad_self"], seqs, True, 0, PAIRS, 0
        )
        sums_cross = e["sums_cross"].reshape(seqs, 8, width).sum(axis=0)
        sums_self = sums_self.reshape(seqs, 8, width).sum(axis=0)
        last = e["sums_three"]
        e["grad_vec"] = jnp.concatenate(
            [
                sums_self[0:2],
                e["sums_one"][2:3],
                sums_cross[0:2],
                e["sums_two"][2:3],
                last[4:5],
                e["sums_one"][0:2],
                e["sums_two"][0:2],
                last[2:4],
                e["sums_pre"].reshape(-1, width),
                last[0:1],
                sums_one,
                sums_two,
                last[1:2],
                jnp.broadcast_to(jnp.sum(seq_len).astype(f32), (1, width)),
            ],
            axis=0,
        )

    def k_states(e):
        e["grad_states"] = input_grad(e["cross_dkv"], (0, 1), (first_w, first_w), (2 * D, 3 * D), BLOCK)

    def k_tokens(e):
        e["grad_tokens"] = input_grad(
            e["self_grads"], (0, 1, 2), (first_w, first_w, second_w), (0, D, 0), seqs * length, (e["grad_one"],)
        )

    kernels = {
        "hidden": (k_hidden, ("grad_ffn",), ("grad_pre", "sums_pre")),
        "two": (k_two, ("grad_pre",), ("grad_two", "grad_cross", "grad_ctx", "sums_two")),
        "cross": (k_cross, ("grad_ctx", "grad_cross"), ("cross_grads", "cross_dkv", "sums_cross")),
        "one": (k_one, ("cross_grads",), ("grad_one", "grad_self", "grad_ctx", "sums_one")),
        "self": (k_self, ("grad_ctx", "grad_self"), ("self_grads", "grad_vec")),
        "states": (k_states, ("cross_dkv",), ("grad_states",)),
        "tokens": (k_tokens, ("self_grads",), ("grad_tokens",)),
    }
    n_vec = vec_w.shape[0]
    if linked:
        order = links.plane_order()
        sums = {}

        def planes_of(name, x_mine, x_peer, y_mine, y_peer, x_at, y_at, stride, wide=D):
            spots = [(x_at(ux, y), *y_at(ux)) for ux, y in order]
            slots = [a if a.ndim == 3 else a[None] for a in (x_mine, x_peer, y_mine, y_peer)]
            sums[name] = Sum(links, unit_planes(*slots, spots, links.z, stride, shard_rows, wide))

        def k_planes_2(e):
            planes_of(
                "2", e["hidden"], e["hidden_peer"], e["grad_ffn"], e["grad_ffn_peer"],
                lambda ux, y: y * UNITS + ux * 2 + core, lambda ux: (0 * ux, 0 * ux), 2 * UNITS,
            )

        def k_planes_1(e):
            planes_of(
                "1", e["normed_two_low"], e["normed_two_low_peer"], e["grad_pre"], e["grad_pre_peer"],
                lambda ux, y: y, lambda ux: (0 * ux, ux * 2 + core), 2,
            )

        def k_planes_t(e):
            planes_of(
                "t", e["cross_in"], e["cross_in_peer"], e["cross_grads"], e["cross_grads_peer"],
                lambda ux, y: core * 2 * links.depth + y, lambda ux: (core + 0 * ux, ux), 2, D // 2,
            )

        def k_planes_a(e):
            planes_of(
                "a", e["self_in"], e["self_in_peer"], e["self_grads"], e["self_grads_peer"],
                lambda ux, y: y + 2 * links.depth * (ux * core), lambda ux: (ux * 2 + core, 0 * ux), 2,
            )

        def k_theirs(e):
            e["theirs"] = state_grad(state_rows, e["cross_dkv"], 1 - core)

        def k_mine(e):
            e["mine"] = state_grad(state_rows, e["cross_dkv"], core)

        def k_planes_e(e):
            spots = [(y, ux) for ux, y in order]
            sums["e"] = Sum(links, sum_planes(e["mine"], e["theirs_peer"], spots, links.z, shard_rows, D // 2))

        states_of = {"1": (fc1_w, fc1_m, fc1_v), "2": (fc2_w, fc2_m, fc2_v)}
        whole_unit, half_unit = (1, shard_rows, D), (1, shard_rows, D // 2)
        ways = {
            "2": ((shard_rows, D), lambda u: (u, 0)),
            "1": ((shard_rows, D), lambda u: (0, u)),
            "a": (whole_unit, lambda u: (u, 0, 0)),
            "t": (half_unit, lambda u: (4 + 3 * (u % 2), 0, u // 2)),
            "e": (half_unit, lambda u: (5 + u % 2, 0, u // 2)),
        }

        def k_adam(name):
            def kernel(e):
                place_of = name if name in states_of else "attn"
                state = states_of.get(name, (attn_w, attn_m, attn_v))
                e[place_of] = adam_units(spot, sums[name].parts, state, *ways[name], e.get(place_of))

            return kernel

        kernels |= {
            "planes_2": (k_planes_2, ("hidden", "hidden_peer", "grad_ffn", "grad_ffn_peer"), ()),
            "planes_1": (k_planes_1, ("normed_two_low", "normed_two_low_peer", "grad_pre", "grad_pre_peer"), ()),
            "planes_t": (k_planes_t, ("cross_in", "cross_in_peer", "cross_grads", "cross_grads_peer"), ()),
            "planes_a": (k_planes_a, ("self_in", "self_in_peer", "self_grads", "self_grads_peer"), ()),
            "theirs": (k_theirs, ("cross_dkv",), ("theirs",)),
            "mine": (k_mine, ("cross_dkv",), ("mine",)),
            "planes_e": (k_planes_e, ("mine", "theirs_peer"), ()),
        }
        for name in "21ate":
            kernels["adam_" + name] = (k_adam(name), (), ())
        env |= {"self_in_peer": self_in_peer, "cross_in_peer": cross_in_peer}
        vec_perms = {"c": links.to_core, "z1": to_z1, "z2": to_z2, "s1": swap1, "s2": swap2}
        CLOCK[:] = [CLOCK[0]]
        for at, (kernel, *events) in enumerate(PLAN):
            if kernel:
                kernels[kernel][0](env)
            moved = [event[4:] for event in events if event.startswith("sum ")]
            made = [name[-1] for name in (kernel,) if name.startswith("planes")]
            landing = [event[5:] for event in events if event.startswith("land ")]
            names = set(kernels[kernel][2]) if kernel else set()
            for later in PLAN[at + 1 :]:
                if later[0]:
                    names |= set(kernels[later[0]][1])
                    break
            names |= {name + "_peer" for name in landing}
            names |= {event[5:] for event in events if event.startswith("give ")}
            if "vec" in landing or any(event.startswith("vec ") for event in events):
                names |= {"grad_vec"}
            names = sorted(name for name in names if name in env)
            here = [sums[name] for name in sorted({*moved, *made})]
            arrays = [env[name] for name in names]
            if kernel.startswith("adam"):
                place_of = kernel[5:] if kernel[5:] in states_of else "attn"
                arrays.append(env[place_of][0])
            held = land(here, *arrays)
            env.update(zip(names, held))
            if kernel.startswith("adam"):
                env[place_of][0] = held[-1]
            if "vec" in landing:
                env["grad_vec"] = env["grad_vec"] + env["vec_peer"]
            add(*[sums[name] for name in moved])
            if moved:
                held = land(here, *[env[name] for name in names])
                env.update(zip(names, held))
            go(*[sums[name] for name in moved])
            for event in events:
                if event.startswith("give "):
                    env[event[5:] + "_peer"] = peer(env[event[5:]])
                elif event.startswith("vec "):
                    env["vec_peer"] = send(env["grad_vec"], vec_perms[event[4:]])
        fc1_new, fc2_new, attn_new = env["1"], env["2"], env["attn"]
        grad_vec = env["grad_vec"]
    else:
        for name in ("hidden", "two", "cross", "one", "self", "states", "tokens"):
            kernels[name][0](env)
        self_grads, cross_grads, cross_dkv = env["self_grads"], env["cross_grads"], env["cross_dkv"]
        grad_vec = lax.psum(env["grad_vec"], ("dp", "fsdp"))

        def owned(inputs, grads, dim):
            part = dot_grad(inputs, grads).astype(bf16)
            part = lax.psum_scatter(part, "fsdp", scatter_dimension=dim, tiled=True)
            return lax.psum(part, "dp").astype(f32)

        grad_attn = jnp.stack(
            [owned(self_in[u // 3], self_grads[u], 0) for u in range(4)]
            + [
                owned(normed_one_low, cross_grads[0], 0),
                owned(state_rows, cross_dkv[0], 0),
                owned(state_rows, cross_dkv[1], 0),
                owned(cross_in[1], cross_grads[1], 0),
            ]
        )
        grad_fc1, grad_fc2 = owned(normed_two_low, env["grad_pre"], 0), owned(hidden, grad_ffn, 0)
        attn_new = adam_update(attn_w, attn_m, attn_v, grad_attn, matrix_rate, matrix_decay)
        fc1_new = adam_update(fc1_w, fc1_m, fc1_v, grad_fc1, matrix_rate, matrix_decay)
        fc2_new = adam_update(fc2_w, fc2_m, fc2_v, grad_fc2, matrix_rate, matrix_decay)
    grad_tokens, grad_states = env["grad_tokens"], env["grad_states"]
    stats = grad_vec[n_vec:]
    stream_rms = jnp.sqrt(jnp.sum(stats[:4], axis=1) / (stats[4, 0] * D))
    cols = vec_w.shape[1]
    vec_grad = lax.dynamic_slice_in_dim(grad_vec[:n_vec], lax.axis_index("fsdp") * cols, cols, 1)
    vec_new = adam_update(vec_w, CLOCK[0] if linked else vec_m, vec_v, vec_grad, vector_rate, 0.0)
    return (
        mixed.reshape(tokens.shape),
        grad_tokens.reshape(tokens.shape),
        grad_states.reshape(states.shape),
        stream_rms,
        *attn_new,
        *fc1_new,
        *fc2_new,
        *vec_new,
    )


def solution(mesh):
    rows = P(None, ("dp", "fsdp"), None, None)
    lens = P(None, ("dp", "fsdp"))
    attn, fc, vec = P(None, "fsdp", None), P("fsdp", None), P(None, "fsdp")
    state = (attn,) * 3 + (fc,) * 6 + (vec,) * 3
    return jax.shard_map(
        partial(on_device, mesh.shape["dp"], mesh.shape["fsdp"]),
        mesh=mesh,
        in_specs=(rows, rows, rows, lens, lens) + state,
        out_specs=(rows, rows, rows, P()) + state,
        check_vma=False,
    )
```

```python
from functools import partial

import jax
import jax.numpy as jnp
from jax import lax
from jax.experimental import pallas as pl
from jax.experimental.pallas import tpu as pltpu
from jax.sharding import PartitionSpec as P

D = 1024
H = 16
DH = 64
STEP = 7
PAIRS = H // 2
UNITS = 4
LANES = 128
TAIL = 16

momentum_decay = 0.9
square_decay = 0.999
matrix_rate = 0.08
vector_rate = 0.3
matrix_decay = 0.01
epsilon = 1e-08
norm_epsilon = 1e-05
fix_first = 1.0 - momentum_decay**STEP
fix_second = 1.0 - square_decay**STEP

f32 = jnp.float32
bf16 = jnp.bfloat16
ANY = pl.BlockSpec(memory_space=pl.ANY)
MIB = 1024 * 1024
FIRST, SECOND = (0, 1, 5, 6), (2, 3, 4, 7)


def params(mib):
    return pltpu.CompilerParams(vmem_limit_bytes=mib * MIB)


def cost(nbytes):
    return pl.CostEstimate(flops=0, bytes_accessed=int(nbytes), transcendentals=0)


def array(shape, kind=bf16):
    return jax.ShapeDtypeStruct(shape, kind)


def far_array(shape, kind=bf16):
    return pltpu.HBM(shape, kind)


def whole(shape):
    return pl.BlockSpec(shape, lambda *at: (0,) * len(shape))


def far(values):
    return pltpu.with_memory_space_constraint(values, pltpu.HBM)


def dot(left, right):
    return jnp.dot(left, right, preferred_element_type=f32)


def dot_back(left, right):
    return lax.dot_general(left, right, (((1,), (1,)), ((), ())), preferred_element_type=f32)


def dot_grad(inputs, grads):
    return lax.dot_general(inputs, grads, (((0,), (0,)), ((), ())), preferred_element_type=f32)


def norm_forward(stream, gain, bias):
    centred = stream - jnp.mean(stream, axis=-1, keepdims=True)
    spread = jnp.mean(centred * centred, axis=-1, keepdims=True)
    scale = lax.rsqrt(spread + norm_epsilon)
    unit = centred * scale
    return unit * gain + bias, unit, scale


def norm_backward(grad, unit, scale, gain):
    scaled = grad * gain
    mean = jnp.mean(scaled, axis=-1, keepdims=True)
    along = jnp.mean(scaled * unit, axis=-1, keepdims=True)
    return scale * (scaled - mean - unit * along), column_sum(grad * unit), column_sum(grad)


def column_sum(values):
    return jnp.sum(values.astype(f32), axis=0, keepdims=True)


def valid_rows(len_ref, rows, length):
    spot = lax.broadcasted_iota(jnp.int32, (rows, 1), 0)
    limit = jnp.full((rows, 1), len_ref[0], jnp.int32)
    for m in range(1, rows // length):
        limit = jnp.where(spot >= m * length, m * length + len_ref[m], limit)
    return spot < limit


def add_up(total_ref, step, part):
    @pl.when(step == 0)
    def _():
        total_ref[...] = part

    @pl.when(step > 0)
    def _():
        total_ref[...] += part


BLOCK = 1024


def project_kernel(x_ref, w_ref, b_ref, o_ref):
    o_ref[...] = (dot(x_ref[...], w_ref[...]) + b_ref[...]).astype(bf16)


def project(rows, weights, bias, at):
    n_rows, depth = rows.shape
    width = bias.shape[1]
    return pl.pallas_call(
        project_kernel,
        out_shape=array((n_rows, width)),
        grid=(width // BLOCK,),
        in_specs=[
            whole((n_rows, depth)),
            pl.BlockSpec((depth, BLOCK), lambda n: (0, at // BLOCK + n)),
            pl.BlockSpec((1, BLOCK), lambda n: (0, n)),
        ],
        out_specs=pl.BlockSpec((n_rows, BLOCK), lambda n: (0, n)),
        compiler_params=params(22),
        cost_estimate=cost(1024),
    )(rows, weights, bias)


def join_kernel(length, rows_at, len_ref, x_ref, w_ref, res_ref, vec_ref, *outs):
    h_ref, low_ref, unit_ref, scale_ref, sums_ref, total_ref = outs
    step = pl.program_id(0)
    add_up(total_ref, step, dot(x_ref[...], w_ref[...]))

    @pl.when(step == pl.num_programs(0) - 1)
    def _():
        bias, gain, offset = (vec_ref[r : r + 1, :] for r in rows_at)
        branch = total_ref[...] + bias
        out, unit, scale = norm_forward(res_ref[...].astype(f32) + branch, gain, offset)
        h_ref[...] = out
        low_ref[...] = out.astype(bf16)
        unit_ref[...] = unit
        scale_ref[...] = jnp.broadcast_to(scale, scale_ref.shape)
        valid = valid_rows(len_ref, branch.shape[0], length)
        sums_ref[...] = column_sum(jnp.where(valid, branch * branch, 0.0))


def join(lengths, rows, weights, at, residual, vec, rows_at):
    n_rows = residual.shape[0]
    slot = rows.ndim == 3
    x_spec = (
        pl.BlockSpec((None, n_rows, BLOCK), lambda k, n: (1, 0, k))
        if slot
        else pl.BlockSpec((n_rows, BLOCK), lambda k, n: (0, k))
    )
    return pl.pallas_call(
        partial(join_kernel, n_rows // lengths.shape[0], rows_at),
        out_shape=[
            array((n_rows, D), f32),
            array((n_rows, D)),
            far_array((n_rows, D), f32),
            array((n_rows, LANES), f32),
            array((1, D), f32),
        ],
        grid_spec=pltpu.PrefetchScalarGridSpec(
            num_scalar_prefetch=1,
            grid=(D // BLOCK,),
            in_specs=[
                x_spec,
                pl.BlockSpec((BLOCK, D), lambda k, n: (k, at // D)),
                whole((n_rows, D)),
                whole(vec.shape),
            ],
            out_specs=[whole((n_rows, D))] * 3 + [whole((n_rows, LANES)), whole((1, D))],
            scratch_shapes=[pltpu.VMEM((n_rows, D), f32)],
        ),
        compiler_params=params(12),
        cost_estimate=cost(1024),
    )(lengths, rows, weights, residual, vec)


def hidden_kernel(x_ref, w_ref, b_ref, g_ref, slope_ref):
    u = dot(x_ref[...], w_ref[...]) + b_ref[...]
    phi = 0.5 * (1.0 + lax.erf(u * 2.0**-0.5))
    g_ref[...] = (u * phi).astype(bf16)
    slope_ref[...] = (phi + u * jnp.exp(-0.5 * u * u) * (2.0 * jnp.pi) ** -0.5).astype(bf16)


def hidden_layer(rows, weights, bias):
    n_rows, depth = rows.shape
    width = weights.shape[1]
    out_spec = pl.BlockSpec((n_rows, BLOCK), lambda n: (0, n))
    return pl.pallas_call(
        hidden_kernel,
        out_shape=[array((n_rows, width))] * 2,
        grid=(width // BLOCK,),
        in_specs=[
            whole((n_rows, depth)),
            pl.BlockSpec((depth, BLOCK), lambda n: (0, n)),
            pl.BlockSpec((1, BLOCK), lambda n: (0, n)),
        ],
        out_specs=[out_spec] * 2,
        compiler_params=params(14),
        cost_estimate=cost(1024),
    )(rows, weights, bias)


def turn_kernel(length, rows_at, len_ref, x_ref, w_ref, res_ref, cot_ref, vec_ref, *outs):
    mixed_ref, dr_ref, low_ref, sums_ref, total_ref = outs
    step = pl.program_id(0)
    add_up(total_ref, step, dot(x_ref[...], w_ref[...]))

    @pl.when(step == pl.num_programs(0) - 1)
    def _():
        bias, gain, offset = (vec_ref[r : r + 1, :] for r in rows_at)
        branch = total_ref[...] + bias
        out, unit, scale = norm_forward(res_ref[...] + branch, gain, offset)
        mixed_ref[...] = out.astype(bf16)
        valid = valid_rows(len_ref, branch.shape[0], length)
        grad, grad_gain, grad_bias = norm_backward(cot_ref[...].astype(f32), unit, scale, gain)
        low = grad.astype(bf16)
        dr_ref[...] = grad
        low_ref[...] = low
        sums_ref[0:1, :] = column_sum(jnp.where(valid, out * out, 0.0))
        sums_ref[1:2, :] = column_sum(jnp.where(valid, branch * branch, 0.0))
        sums_ref[2:3, :] = grad_gain
        sums_ref[3:4, :] = grad_bias
        sums_ref[4:5, :] = column_sum(low)
        sums_ref[5:8, :] = jnp.zeros((3, D), f32)


def turn(lengths, rows, weights, residual, cotangent, vec, rows_at):
    n_rows, depth = rows.shape
    return pl.pallas_call(
        partial(turn_kernel, n_rows // lengths.shape[0], rows_at),
        out_shape=[array((n_rows, D)), far_array((n_rows, D), f32), array((n_rows, D)), array((8, D), f32)],
        grid_spec=pltpu.PrefetchScalarGridSpec(
            num_scalar_prefetch=1,
            grid=(depth // BLOCK,),
            in_specs=[
                pl.BlockSpec((n_rows, BLOCK), lambda k, n: (0, k)),
                pl.BlockSpec((BLOCK, D), lambda k, n: (k, 0)),
                whole((n_rows, D)),
                whole((n_rows, D)),
                whole(vec.shape),
            ],
            out_specs=[whole((n_rows, D))] * 3 + [whole((8, D))],
            scratch_shapes=[pltpu.VMEM((n_rows, D), f32)],
        ),
        compiler_params=params(14),
        cost_estimate=cost(1024),
    )(lengths, rows, weights, residual, cotangent, vec)


def hidden_back_kernel(e_ref, w_ref, slope_ref, du_ref, sums_ref):
    du = (dot_back(e_ref[...], w_ref[...]) * slope_ref[...].astype(f32)).astype(bf16)
    du_ref[...] = du
    sums_ref[...] = column_sum(du)


def hidden_back(grads, weights, slope):
    n_rows, width = slope.shape
    block = pl.BlockSpec((n_rows, BLOCK), lambda n: (0, n))
    return pl.pallas_call(
        hidden_back_kernel,
        out_shape=[far_array((n_rows, width)), array((1, width), f32)],
        grid=(width // BLOCK,),
        in_specs=[whole((n_rows, D)), pl.BlockSpec((BLOCK, D), lambda n: (n, 0)), block],
        out_specs=[block, pl.BlockSpec((1, BLOCK), lambda n: (0, n))],
        compiler_params=params(14),
        cost_estimate=cost(1024),
    )(grads, weights, slope)


def join_back_kernel(row_at, g_ref, w_ref, dr_ref, unit_ref, scale_ref, vec_ref, after_ref, *outs):
    out_ref, low_ref, next_ref, sums_ref, total_ref = outs
    step = pl.program_id(0)
    add_up(total_ref, step, dot_back(g_ref[...], w_ref[...]))

    @pl.when(step == pl.num_programs(0) - 1)
    def _():
        grad, grad_gain, grad_bias = norm_backward(
            dr_ref[...] + total_ref[...], unit_ref[...], scale_ref[:, 0:1], vec_ref[row_at : row_at + 1, :]
        )
        low = grad.astype(bf16)
        out_ref[...] = grad
        low_ref[...] = low
        next_ref[...] = dot_back(low, after_ref[...]).astype(bf16)
        sums_ref[0:1, :] = grad_gain
        sums_ref[1:2, :] = grad_bias
        sums_ref[2:3, :] = column_sum(low)
        sums_ref[3:8, :] = jnp.zeros((5, D), f32)


def join_back(grads, weights, at, above, unit, scale, vec, row_at, after, after_at):
    slot = grads.ndim == 3
    n_rows, width = grads.shape[-2:]
    g_spec = (
        pl.BlockSpec((None, n_rows, BLOCK), lambda k: (0, 0, k))
        if slot
        else pl.BlockSpec((n_rows, BLOCK), lambda k: (0, k))
    )
    return pl.pallas_call(
        partial(join_back_kernel, row_at),
        out_shape=[far_array((n_rows, D), f32), array((n_rows, D)), array((n_rows, D)), array((8, D), f32)],
        grid=(width // BLOCK,),
        in_specs=[
            g_spec,
            pl.BlockSpec((D, BLOCK), lambda k: (0, at // BLOCK + k)),
            whole((n_rows, D)),
            whole((n_rows, D)),
            whole((n_rows, LANES)),
            whole(vec.shape),
            pl.BlockSpec((D, D), lambda k: (0, after_at // D)),
        ],
        out_specs=[whole((n_rows, D))] * 3 + [whole((8, D))],
        scratch_shapes=[pltpu.VMEM((n_rows, D), f32)],
        compiler_params=params(18),
        cost_estimate=cost(1024),
    )(grads, far(weights), far(above), far(unit), scale, vec, far(after))


def input_grad_kernel(count, *refs):
    gs, ws, rest, o_ref = refs[:count], refs[count : 2 * count], refs[2 * count : -1], refs[-1]
    total = sum(dot_back(g[...], w[...]) for g, w in zip(gs, ws))
    if rest:
        total = total + rest[0][...]
    o_ref[...] = total.astype(bf16)


def input_grad(grads, slots, weights, ats, block, rest=()):
    n_rows = grads.shape[1]
    row_block = pl.BlockSpec((block, D), lambda r: (r, 0))
    return pl.pallas_call(
        partial(input_grad_kernel, len(slots)),
        out_shape=array((n_rows, D)),
        grid=(n_rows // block,),
        in_specs=[pl.BlockSpec((None, block, D), lambda r, s=s: (s, r, 0)) for s in slots]
        + [pl.BlockSpec((D, D), lambda r, a=a: (0, a // D)) for a in ats]
        + [row_block] * len(rest),
        out_specs=row_block,
        compiler_params=params(22),
        cost_estimate=cost(1024),
    )(*[far(grads)] * len(slots), *[far(w) for w in weights], *rest)


def state_grad_kernel(slot_ref, e_ref, g_ref, o_ref):
    o_ref[...] = dot_grad(e_ref[...], g_ref[...]).astype(bf16)


def state_grad(states, grads, slot):
    n_rows, block = states.shape[0], D // 2
    return pl.pallas_call(
        state_grad_kernel,
        out_shape=array((D, D)),
        grid_spec=pltpu.PrefetchScalarGridSpec(
            num_scalar_prefetch=1,
            grid=(D // block,),
            in_specs=[
                pl.BlockSpec((n_rows, block), lambda r, s: (0, r)),
                pl.BlockSpec((None, n_rows, D), lambda r, s: (s[0], 0, 0)),
            ],
            out_specs=pl.BlockSpec((block, D), lambda r, s: (r, 0)),
        ),
        compiler_params=params(18),
        cost_estimate=cost(1024),
    )(jnp.stack([slot]).astype(jnp.int32), states, far(grads))


def two_heads(rows):
    low_half = lax.broadcasted_iota(jnp.int32, rows.shape, 1) < DH
    zero = jnp.zeros_like(rows)
    return jnp.concatenate([jnp.where(low_half, rows, zero), jnp.where(low_half, zero, rows)], axis=0)


def one_row(both):
    half = both.shape[0] // 2
    low_half = lax.broadcasted_iota(jnp.int32, (half, both.shape[1]), 1) < DH
    return jnp.where(low_half, both[:half], both[half:])


def masked_exp(queries, keys, valid, causal):
    scores = dot_back(queries, keys)
    place = lax.broadcasted_iota(jnp.int32, (1, scores.shape[1]), 1)
    if causal:
        rows = scores.shape[0] // 2
        spot = lax.broadcasted_iota(jnp.int32, scores.shape, 0)
        spot = jnp.where(spot >= rows, spot - rows, spot)
        spots = lax.broadcasted_iota(jnp.int32, scores.shape, 1)
        allowed = (spots <= spot) & (spots < valid)
        scores = jnp.where(allowed, scores, -1e30)
    else:
        scores = scores + jnp.where(place < valid, 0.0, -1e30)
    top = jnp.max(scores, axis=-1, keepdims=True)
    exponent = jnp.exp(scores - top)
    return exponent, 1.0 / jnp.sum(exponent, axis=-1, keepdims=True)


def attend_kernel(causal, len_ref, q_ref, k_ref, v_ref, x_ref, o_ref):
    valid = len_ref[pl.program_id(0)]
    o_ref[0] = x_ref[...]
    for at in range(0, q_ref.shape[1], LANES):
        pair = slice(at, at + LANES)
        queries = two_heads(q_ref[:, pair] * DH**-0.5)
        exponent, inverse = masked_exp(queries, k_ref[:, pair], valid, causal)
        o_ref[1, :, pair] = one_row(dot(exponent.astype(bf16), v_ref[:, pair]) * inverse).astype(bf16)


def attend_back_kernel(causal, len_ref, q_ref, k_ref, v_ref, do_ref, x_ref, dq_ref, *more):
    dkv_refs, sums_ref = more[:-1], more[-1]
    valid = len_ref[pl.program_id(0)]
    dq_ref[dq_ref.shape[0] - 1] = x_ref[...]
    sums_ref[2:8, :] = jnp.zeros((6, sums_ref.shape[1]), f32)
    for at in range(0, q_ref.shape[1], LANES):
        pair = slice(at, at + LANES)
        keys = k_ref[:, pair]
        queries = two_heads(q_ref[:, pair] * DH**-0.5)
        exponent, inverse = masked_exp(queries, keys, valid, causal)
        grads = two_heads(do_ref[:, pair])
        grad_probs = dot_back(grads, v_ref[:, pair])
        row_dot = jnp.sum(exponent * grad_probs, axis=-1, keepdims=True) * inverse
        grad_scores = (exponent * (grad_probs - row_dot)).astype(bf16)
        dq = one_row(dot(grad_scores, keys) * (inverse * DH**-0.5)).astype(bf16)
        dk = dot_grad(grad_scores, (queries * inverse).astype(bf16)).astype(bf16)
        dv = dot_grad(exponent.astype(bf16), (grads * inverse).astype(bf16)).astype(bf16)
        dq_ref[0, :, pair] = dq
        if dkv_refs:
            dkv_refs[0][0, :, pair], dkv_refs[0][1, :, pair] = dk, dv
        else:
            dq_ref[1, :, pair], dq_ref[2, :, pair] = dk, dv
        sums_ref[0:1, pair] = column_sum(dq)
        sums_ref[1:2, pair] = column_sum(dv)


def head_block(rows, at, group):
    return pl.BlockSpec((rows, LANES * group), lambda m, p, n: (m, at // group + p))


def slots_block(slots, rows, group):
    return pl.BlockSpec((slots, rows, LANES * group), lambda m, p, n: (0, m, p))


def attend(lengths, queries, keys, values, beside, seqs, causal, q_at, k_at, v_at):
    q_rows, k_rows = queries.shape[0] // seqs, keys.shape[0] // seqs
    group = PAIRS if causal else PAIRS // 2
    return pl.pallas_call(
        partial(attend_kernel, causal),
        out_shape=array((2, seqs * q_rows, D)),
        grid_spec=pltpu.PrefetchScalarGridSpec(
            num_scalar_prefetch=1,
            grid=(seqs, PAIRS // group),
            in_specs=[
                head_block(q_rows, q_at, group),
                head_block(k_rows, k_at, group),
                head_block(k_rows, v_at, group),
                head_block(q_rows, 0, group),
            ],
            out_specs=slots_block(2, q_rows, group),
        ),
        compiler_params=params(20),
        cost_estimate=cost(1024),
    )(lengths, queries, keys, values, beside)


def attend_back(lengths, queries, keys, values, grads, beside, seqs, causal, q_at, k_at, v_at):
    q_rows, k_rows = queries.shape[0] // seqs, keys.shape[0] // seqs
    group = PAIRS if causal else PAIRS // 2
    slots = 4 if causal else 2
    out_shape = [(far_array if causal else array)((slots, seqs * q_rows, D))]
    out_specs = [slots_block(slots, q_rows, group)]
    if not causal:
        out_shape.append(far_array((2, seqs * k_rows, D)))
        out_specs.append(slots_block(2, k_rows, group))
    out_shape.append(array((8 * seqs, D), f32))
    out_specs.append(head_block(8, 0, group))
    return pl.pallas_call(
        partial(attend_back_kernel, causal),
        out_shape=out_shape,
        grid_spec=pltpu.PrefetchScalarGridSpec(
            num_scalar_prefetch=1,
            grid=(seqs, PAIRS // group),
            in_specs=[
                head_block(q_rows, q_at, group),
                head_block(k_rows, k_at, group),
                head_block(k_rows, v_at, group),
                head_block(q_rows, 0, group),
                head_block(q_rows, 0, group),
            ],
            out_specs=out_specs,
        ),
        compiler_params=params(22),
        cost_estimate=cost(1024),
    )(lengths, queries, keys if causal else far(keys), values if causal else far(values), grads, beside)


def place_kernel(rows, idx_ref, *refs):
    slot = 0
    for piece in refs[:-1]:
        for j in range(piece.shape[0] // rows):
            at = pl.multiple_of(idx_ref[slot] * rows, rows)
            refs[-1][pl.ds(at, rows), :] = piece[j * rows : (j + 1) * rows, :]
            slot += 1


def place(pieces, slots):
    total, width = sum(piece.shape[0] for piece in pieces), pieces[0].shape[1]
    return pl.pallas_call(
        partial(place_kernel, total // len(slots)),
        out_shape=array((total, width), pieces[0].dtype),
        grid_spec=pltpu.PrefetchScalarGridSpec(
            num_scalar_prefetch=1,
            grid=(),
            in_specs=[pl.BlockSpec(memory_space=pltpu.VMEM)] * len(pieces),
            out_specs=pl.BlockSpec(memory_space=pltpu.VMEM),
        ),
        compiler_params=params(6),
        cost_estimate=cost(1024),
    )(jnp.stack(slots).astype(jnp.int32), *pieces)


def under(first, second):
    return place([first, second], [jnp.int32(0), jnp.int32(1)])


def assemble_kernel(wide, rows, step, counts, idx_ref, *refs):
    pieces, (out_ref, held, in_sems, out_sems) = refs[: len(counts)], refs[len(counts) :]
    loads, at = [], 0
    for i, (piece, count) in enumerate(zip(pieces, counts)):
        loads.append(pltpu.make_async_copy(piece, held.at[pl.ds(at * step, count * step), :], in_sems.at[i]))
        at += count
    for load in loads:
        load.start()
    stores, copy = [], 0
    for load, count in zip(loads, counts):
        load.wait()
        for _ in range(count):
            unit, shard = idx_ref[0, copy], idx_ref[1, copy]
            if wide:
                target = out_ref.at[
                    pl.ds(pl.multiple_of(shard * rows, rows), rows), pl.ds(pl.multiple_of(unit * D, D), D)
                ]
            else:
                row = (shard * UNITS + unit) * rows
                target = out_ref.at[pl.ds(pl.multiple_of(row, rows), rows), :]
            store = pltpu.make_async_copy(held.at[pl.ds(copy * step, rows), :], target, out_sems.at[copy])
            store.start()
            stores.append(store)
            copy += 1
    for store in stores:
        store.wait()


def assemble(pieces, places, rows, step, wide):
    counts = [piece.shape[0] // step for piece in pieces]
    shards = len(places) // UNITS
    return pl.pallas_call(
        partial(assemble_kernel, wide, rows, step, counts),
        out_shape=array((shards * rows, UNITS * D) if wide else (UNITS * shards * rows, D)),
        grid_spec=pltpu.PrefetchScalarGridSpec(
            num_scalar_prefetch=1,
            grid=(),
            in_specs=[ANY] * len(pieces),
            out_specs=ANY,
            scratch_shapes=[
                pltpu.VMEM((len(places) * step, D), bf16),
                pltpu.SemaphoreType.DMA((len(pieces),)),
                pltpu.SemaphoreType.DMA((len(places),)),
            ],
        ),
        compiler_params=params(10),
        cost_estimate=cost(1024),
    )(jnp.stack([jnp.stack([place[j] for place in places]) for j in range(2)]).astype(jnp.int32), *pieces)


def store_plane(step, plane, outs):
    @pl.when(step < 2)
    def _():
        outs[0][...] = plane

    @pl.when(step == 2)
    def _():
        outs[1][...] = plane

    @pl.when(step == 3)
    def _():
        outs[2][...] = plane


def planes_kernel(depth, idx_ref, *refs):
    x_mine, x_peer = refs[:depth], refs[depth : 2 * depth]
    inputs = jnp.concatenate(
        [jnp.concatenate([x[...] for x in xs], axis=1) for xs in (x_mine, x_peer)], axis=0
    )
    grads = jnp.concatenate([y[...] for y in refs[2 * depth : 2 * depth + 2]], axis=0)
    store_plane(pl.program_id(0), dot_grad(inputs, grads).astype(bf16), refs[-3:])


def sum_planes_kernel(depth, idx_ref, *refs):
    mine, peer, outs = refs[:depth], refs[depth : 2 * depth], refs[-3:]
    plane = jnp.concatenate([a[...].astype(f32) + b[...].astype(f32) for a, b in zip(mine, peer)], axis=0)
    store_plane(pl.program_id(0), plane.astype(bf16), outs)


def planes_call(kernel, table, in_specs, operands, plane, width):
    return pl.pallas_call(
        kernel,
        out_shape=[array((n * plane, width)) for n in (2, 1, 1)],
        grid_spec=pltpu.PrefetchScalarGridSpec(
            num_scalar_prefetch=1,
            grid=(4,),
            in_specs=in_specs,
            out_specs=[
                pl.BlockSpec((plane, width), lambda k, i: (jnp.minimum(k, 1), 0)),
                pl.BlockSpec((plane, width), lambda k, i: (0, 0)),
                pl.BlockSpec((plane, width), lambda k, i: (0, 0)),
            ],
        ),
        compiler_params=params(13),
        cost_estimate=cost(1024),
    )(jnp.stack(table).astype(jnp.int32), *operands)


def column(spots, j):
    return jnp.stack([spot[j] for spot in spots])


def unit_planes(x_mine, x_peer, y_mine, y_peer, spots, z, stride, rows, width=D):
    depth, tokens = 4, x_mine.shape[1]
    blocks = x_mine.shape[2] // rows

    def x_spec(j):
        def at(k, i):
            block = i[0, k] + stride * i[3, j]
            return (block // blocks, 0, block % blocks)

        return pl.BlockSpec((None, tokens, rows), at)

    x_specs = [x_spec(j) for j in range(depth)]
    y_spec = pl.BlockSpec((None, tokens, width), lambda k, i: (i[1, k], 0, i[2, k]))
    table = [column(spots, j) for j in range(3)] + [jnp.stack([z, z ^ 2, z ^ 1, z ^ 3])]
    if x_peer.shape[2] > 2 * D:
        x_mine, x_peer = far(x_mine), far(x_peer)
    operands = [x_mine] * depth + [x_peer] * depth + [y_mine, y_peer]
    return planes_call(
        partial(planes_kernel, depth), table, x_specs * 2 + [y_spec] * 2, operands, depth * rows, width
    )


def sum_planes(mine, peer, spots, z, rows, width):
    depth = 4
    specs = [
        pl.BlockSpec((rows, width), lambda k, i, j=j: (2 * i[2, j] + i[0, k], i[1, k])) for j in range(depth)
    ]
    table = [column(spots, j) for j in range(2)] + [jnp.stack([z, z ^ 2, z ^ 1, z ^ 3])]
    return planes_call(
        partial(sum_planes_kernel, depth), table, specs * 2, [mine] * depth + [peer] * depth, depth * rows, width
    )


def adam_update(weight, first, second, grad, rate, decay):
    first = momentum_decay * first + (1.0 - momentum_decay) * grad
    second = square_decay * second + (1.0 - square_decay) * grad * grad
    update = first / fix_first / (jnp.sqrt(second / fix_second) + epsilon) + decay * weight
    return (weight - rate * update, first, second)


def adam_kernel(idx_ref, here_ref, there_ref, w_ref, m_ref, v_ref, *rest):
    w_out, m_out, v_out = rest[-3:]
    away = pl.program_id(0) ^ idx_ref[0]
    grad = jnp.where(away % 2 == 0, here_ref[...], there_ref[...]).astype(f32)
    if len(w_ref.shape) == 3:
        grad = grad[None]
    w_out[...], m_out[...], v_out[...] = adam_update(
        w_ref[...], m_ref[...], v_ref[...], grad, matrix_rate, matrix_decay
    )


def adam_units(spot, grads, state, block_shape, at, earlier=None):
    spec = pl.BlockSpec(block_shape, lambda u, i: at(u))
    rows, width = grads[0].shape[0] // 2, grads[0].shape[1]
    g_spec = pl.BlockSpec((rows, width), lambda u, i: ((u ^ i[0]) // 2, 0))
    extra = list(earlier) if earlier is not None else []
    state = [far(a) for a in state]
    outs = pl.pallas_call(
        adam_kernel,
        out_shape=[array(a.shape, f32) for a in state],
        grid_spec=pltpu.PrefetchScalarGridSpec(
            num_scalar_prefetch=1,
            grid=(UNITS,),
            in_specs=[g_spec] * 2 + [spec] * 3 + [ANY] * len(extra),
            out_specs=[spec] * 3,
        ),
        input_output_aliases={6 + i: i for i in range(len(extra))},
        compiler_params=params(8),
        cost_estimate=cost(1024),
    )(jnp.stack([spot]).astype(jnp.int32), *grads, *state, *extra)
    return list(outs)


CLOCK = []


def hold(*values):
    CLOCK[0], *held = lax.optimization_barrier((CLOCK[0], *values))
    return held


class Links:
    def __init__(self, n_dp, n_fsdp):
        self.n_fsdp, self.depth = n_fsdp, n_fsdp // 2
        spot = lax.axis_index("dp")
        shard = lax.axis_index("fsdp")
        self.spot, self.shard = spot, shard
        self.x, self.core = spot // 2, spot % 2
        self.z, self.y = shard // 2, shard % 2
        ids = [
            (x, c, z, y) for x in range(2) for c in range(2) for z in range(self.depth) for y in range(2)
        ]

        def number(x, c, z, y):
            return ((x * 2 + c) * self.depth + z) * 2 + y

        def perm(to):
            return [(number(*i), number(*to(*i))) for i in ids]

        flip_x = lambda x, c, z, y: (1 - x, c, z, y)
        flip_y = lambda x, c, z, y: (x, c, z, 1 - y)
        self.to_core = perm(lambda x, c, z, y: (x, 1 - c, z, y))
        self.to_x = perm(flip_x)
        self.to_y = perm(flip_y)
        self.swap1 = perm(lambda x, c, z, y: flip_y(x, c, z, y) if c == 0 else flip_x(x, c, z, y))
        self.swap2 = perm(lambda x, c, z, y: flip_x(x, c, z, y) if c == 0 else flip_y(x, c, z, y))
        self.to_z1 = perm(lambda x, c, z, y: (x, c, z ^ 1, y))
        self.to_z2 = perm(lambda x, c, z, y: (x, c, z ^ 2, y))

    def send(self, block, perm):
        return lax.ppermute(block, ("dp", "fsdp"), perm)

    def column(self, arrived):
        return place(arrived, [self.z ^ away for away in (0, 2, 1, 3)])

    def kinds(self, core):
        x, y = self.x, self.y
        return ((x, y), (x ^ core, y ^ (1 - core)), (x ^ (1 - core), y ^ core), (1 - x, 1 - y))

    def finish(self, pieces, rows, wide, more=0):
        places = [
            (ux * 2 + core, 2 * z + y)
            for core in (self.core, 1 - self.core)
            for ux, y in self.kinds(core)
            for z in range(self.depth)
        ]
        return assemble(pieces, places, rows, rows + more, wide)

    def vectors(self, here, cols):
        half = here[0].shape[0] // 2
        step = half // self.depth

        def tails(piece, first):
            return jnp.stack(
                [
                    lax.slice(piece, (first + (z + 1) * step - TAIL, 0), (first + (z + 1) * step, 2 * cols))
                    for z in range(self.depth)
                ]
            )

        own, other = tails(here[0], 0), tails(here[1], half)
        pair = [jnp.where(self.y == 0, own, other), jnp.where(self.y == 0, other, own)]
        parts = [pair[f % 2][f // 2] for f in range(self.n_fsdp)]
        return jnp.concatenate(
            [
                jnp.concatenate([part[:, :cols] for part in parts], axis=1),
                jnp.concatenate([part[:1, cols:] for part in parts], axis=1),
            ],
            axis=0,
        )

    def plane_order(self):
        own, near, far, both = self.kinds(self.core)
        return far, both, near, own


def add_kernel(rows, count, *refs):
    ins, outs = refs[: len(rows)], refs[len(rows) :]
    total = sum(a[r : r + count, :].astype(f32) for a, r in zip(ins, rows)).astype(bf16)
    part = count // len(outs)
    for i, out in enumerate(outs):
        out[...] = total[i * part : (i + 1) * part]


def add_rows(terms, count, parts=1):
    width = terms[0][0].shape[1]
    vmem = pl.BlockSpec(memory_space=pltpu.VMEM)
    return pl.pallas_call(
        partial(add_kernel, [r for _, r in terms], count),
        out_shape=[array((count // parts, width))] * parts,
        in_specs=[vmem] * len(terms),
        out_specs=[vmem] * parts,
        compiler_params=params(8),
        cost_estimate=cost(1024),
    )(*[a for a, _ in terms])


class Sum:
    def __init__(self, links, planes):
        self.links, self.parts, self.step = links, list(planes), 0

    def add(self):
        parts = self.parts
        if self.step == 1:
            got, second, kept = parts
            half = second.shape[0]
            parts[1:2] = add_rows([(second, 0), (got, half)], half)
        elif self.step == 2:
            got, got_second, kept = parts
            self.parts = add_rows([(kept, 0), (got, 0), (got_second, 0)], kept.shape[0], 2)
        elif self.step == 3:
            self.parts = add_rows([(part, 0) for part in parts], parts[0].shape[0], 2)
        elif self.step == 4:
            self.parts = add_rows([(part, 0) for part in parts], parts[0].shape[0])
        elif self.step == 5:
            self.parts = [under(*parts)]
        self.parts = list(self.parts)

    def send(self):
        links, parts = self.links, self.parts
        if self.step == 0:
            parts[0] = links.send(parts[0], links.swap2)
        elif self.step < 4:
            parts[1] = links.send(parts[1], (links.swap1, links.to_z1, links.to_z2)[self.step - 1])
        elif self.step == 4:
            parts.append(links.send(parts[0], links.to_x))
        else:
            parts.append(links.send(parts[0], links.to_core))
        self.step += 1


def land(sums, *values):
    parts = hold(*values, *(part for one in sums for part in one.parts))
    values, parts = parts[: len(values)], parts[len(values) :]
    for one in sums:
        one.parts, parts = parts[: len(one.parts)], parts[len(one.parts) :]
    return values


def add(*sums):
    for one in sums:
        one.add()


def go(*sums):
    for one in sums:
        one.send()


PLAN = (
    ("", "give grad_ffn", "give hidden"),
    ("hidden", "land grad_ffn", "land hidden", "give grad_pre", "give normed_two_low"),
    ("planes_2", "land grad_pre", "land normed_two_low", "sum 2"),
    ("two",),
    ("planes_1",),
    ("", "sum 1"),
    ("cross", "sum 2", "give cross_grads"),
    ("one", "land cross_grads"),
    ("self",),
    ("planes_t", "sum 1", "sum 2", "give self_grads", "vec c"),
    ("", "sum t"),
    ("theirs", "land self_grads", "land vec", "sum 2", "give theirs"),
    ("planes_a", "vec z1", "sum 1", "sum t"),
    ("", "sum a"),
    ("mine", "land theirs", "land vec", "vec z2", "sum t"),
    ("planes_e", "sum 2"),
    ("tokens", "vec s1", "sum 1", "sum e", "land vec"),
    ("", "sum a", "sum t", "sum 2"),
    ("states", "land vec", "vec s2"),
    ("", "sum 1"),
    ("adam_2", "sum e", "sum a"),
    ("", "sum t", "sum 1"),
    ("adam_1", "sum e", "sum t", "land vec"),
    ("", "sum a"),
    ("adam_t", "sum e"),
    ("", "sum a"),
    ("", "sum e"),
    ("", "sum a", "sum e"),
    ("adam_e",),
    ("adam_a",),
)


def on_device(
    n_dp,
    n_fsdp,
    tokens,
    states,
    cotangent,
    seq_len,
    enc_len,
    attn_w,
    attn_m,
    attn_v,
    fc1_w,
    fc1_m,
    fc1_v,
    fc2_w,
    fc2_m,
    fc2_v,
    vec_w,
    vec_m,
    vec_v,
):
    micro, local, length, width = tokens.shape
    enc_length = states.shape[2]
    seqs = micro * local
    shard_rows = attn_w.shape[1]
    linked = n_dp == 4 and n_fsdp == 8 and vec_w.shape[0] == TAIL + 1
    token_rows = tokens.reshape(seqs * length, width)
    state_rows = states.reshape(seqs * enc_length, width)
    cotan_rows = cotangent.reshape(seqs * length, width)
    tok_lens = seq_len.reshape(seqs)
    enc_lens = enc_len.reshape(seqs)

    if linked:
        links = Links(n_dp, n_fsdp)
        spot, core = links.spot, links.core
        peer = lambda rows: links.send(rows, links.to_core)
        part_a = lax.dynamic_index_in_dim(attn_w, spot + jnp.where(spot < 2, 0, 3), 0, keepdims=False).astype(bf16)
        part_b = lax.dynamic_index_in_dim(attn_w, spot + jnp.where(spot < 3, 2, 4), 0, keepdims=False).astype(bf16)
        part_1 = lax.dynamic_slice_in_dim(fc1_w, spot * D, D, 1).astype(bf16)
        part_2 = lax.dynamic_slice_in_dim(fc2_w, spot * shard_rows, shard_rows, 0).astype(bf16)
        vec_cols = vec_w.shape[1]
        small = vec_w.astype(bf16)
        small = jnp.concatenate(
            [
                small[:TAIL],
                jnp.pad(small[TAIL:], ((0, TAIL - 1), (0, 0))),
                jnp.zeros((TAIL, D - 2 * vec_cols), bf16),
            ],
            axis=1,
        )
        part_a = jnp.concatenate([part_a, small], axis=0)

        to_z1, to_z2, swap1, swap2 = links.to_z1, links.to_z2, links.swap1, links.swap2
        send = links.send
        CLOCK[:] = [vec_m]
        a_2, a_1 = send(part_a, to_z2), send(part_a, to_z1)
        part_a, part_b, a_2, a_1 = hold(part_a, part_b, a_2, a_1)

        a_3, b_2, b_1 = send(a_2, to_z1), send(part_b, to_z2), send(part_b, to_z1)
        (a_3,) = hold(a_3)
        a_own = links.column([part_a, a_2, a_1, a_3])
        a_near = send(a_own, swap1)
        part_b, part_1, b_2, b_1, a_near = hold(part_b, part_1, b_2, b_1, a_near)

        a_here = [under(a_own, a_near)]
        a_here.append(send(a_here[0], swap2))
        b_3, c_2 = send(b_2, to_z1), send(part_1, to_z2)
        part_1, b_3, c_2 = hold(part_1, b_3, c_2)
        b_own = links.column([part_b, b_2, b_1, b_3])
        b_near = send(b_own, swap1)
        c_1 = send(under(part_1, c_2), to_z1)
        a_there = [peer(a_here[0])]
        part_1, c_1 = hold(part_1, c_1)
        c_own = links.column([part_1, c_2, c_1])
        c_own, part_2, b_own, b_near, *held = hold(c_own, part_2, b_own, b_near, *a_here, a_there[0])
        a_here, a_there = held[:2], held[2:]

        c_near = send(c_own, swap1)
        b_here = [under(b_own, b_near)]
        b_here.append(send(b_here[0], swap2))
        d_2 = send(part_2, to_z2)
        a_there.append(peer(a_here[1]))
        first_w = links.finish(a_here + a_there, shard_rows, True, TAIL)
        vectors = links.vectors(a_here, vec_cols)
    else:
        vectors = lax.all_gather(vec_w.astype(bf16), "fsdp", axis=1, tiled=True)
        attn = lax.all_gather(attn_w.astype(bf16), "fsdp", axis=1, tiled=True)
        first_w = jnp.concatenate([attn[u] for u in FIRST], axis=1)
        second_w = jnp.concatenate([attn[u] for u in SECOND], axis=1)
        fc_in = lax.all_gather(fc1_w.astype(bf16), "fsdp", axis=0, tiled=True)
        fc_out = lax.all_gather(fc2_w.astype(bf16), "fsdp", axis=0, tiled=True)
    vec = vectors.astype(f32)
    zeros = jnp.zeros((1, width), f32)
    qk_bias = jnp.concatenate([vec[0:1], zeros], axis=1)
    kv_bias = jnp.concatenate([zeros, vec[4:5]], axis=1)
    fc_bias = vec[13:].reshape(1, -1)

    queries_keys = project(token_rows, first_w, qk_bias, 0)
    if linked:
        queries_keys, first_w, part_2, d_2 = hold(queries_keys, first_w, part_2, d_2)
        d_1 = send(under(part_2, d_2), to_z1)
        b_there = [peer(b_here[0])]
    cross_kv = project(state_rows, first_w, kv_bias, 2 * D)
    if linked:
        cross_kv, d_1 = hold(cross_kv, d_1)
        d_own = links.column([part_2, d_2, d_1])
        d_own, c_own, c_near, b_here[1], b_there[0] = hold(d_own, c_own, c_near, b_here[1], b_there[0])
        c_here = [under(c_own, c_near)]
        c_here.append(send(c_here[0], swap2))
        d_near = send(d_own, swap1)
        b_there.append(peer(b_here[1]))
        second_w = links.finish(b_here + b_there, shard_rows, True)
        c_there = [peer(c_here[0])]
    values = project(token_rows, second_w, vec[1:2], 0)
    self_in = attend(tok_lens, queries_keys, queries_keys, values, token_rows, seqs, True, 0, PAIRS, 0)
    if linked:
        self_in_peer = peer(self_in)
    normed_one, normed_one_low, unit_one, scale_one, sums_one = join(
        tok_lens, self_in, second_w, D, token_rows, vec, (2, 7, 8)
    )
    cross_q = project(normed_one_low, second_w, vec[3:4], 2 * D)
    cross_in = attend(enc_lens, cross_q, cross_kv, cross_kv, normed_one_low, seqs, False, 0, 0, PAIRS)
    normed_two, normed_two_low, unit_two, scale_two, sums_two = join(
        tok_lens, cross_in, second_w, 3 * D, normed_one, vec, (5, 9, 10)
    )
    if linked:
        normed_two_low, d_own, d_near, c_here[1], c_there[0] = hold(
            normed_two_low, d_own, d_near, c_here[1], c_there[0]
        )
        d_here = [under(d_own, d_near)]
        d_here.append(send(d_here[0], swap2))
        c_there.append(peer(c_here[1]))
        fc_in = links.finish(c_here + c_there, shard_rows, True)
        d_there = [peer(d_here[0])]
        cross_in_peer = peer(cross_in)
    hidden, slope = hidden_layer(normed_two_low, fc_in, fc_bias)
    if linked:
        hidden, normed_two_low, d_here[1], d_there[0] = hold(hidden, normed_two_low, d_here[1], d_there[0])
        d_there.append(peer(d_here[1]))
        fc_out = links.finish(d_here + d_there, shard_rows, False)
    mixed, grad_three, grad_ffn, sums_three = turn(
        tok_lens, hidden, fc_out, normed_two, cotan_rows, vec, (6, 11, 12)
    )

    env = dict(
        hidden=hidden, normed_two_low=normed_two_low, grad_three=grad_three, grad_ffn=grad_ffn, self_in=self_in,
        cross_in=cross_in, sums_three=sums_three,
    )

    def k_hidden(e):
        e["grad_pre"], e["sums_pre"] = hidden_back(e["grad_ffn"], fc_out, slope)

    def k_two(e):
        e["grad_two"], e["grad_cross"], e["grad_ctx"], e["sums_two"] = join_back(
            e["grad_pre"], fc_in, 0, grad_three, unit_two, scale_two, vec, 9, second_w, 3 * D
        )

    def k_cross(e):
        e["cross_grads"], e["cross_dkv"], e["sums_cross"] = attend_back(
            enc_lens, cross_q, cross_kv, cross_kv, e["grad_ctx"], e["grad_cross"], seqs, False, 0, 0, PAIRS
        )

    def k_one(e):
        e["grad_one"], e["grad_self"], e["grad_ctx"], e["sums_one"] = join_back(
            e["cross_grads"], second_w, 2 * D, e["grad_two"], unit_one, scale_one, vec, 7, second_w, D
        )

    def k_self(e):
        e["self_grads"], sums_self = attend_back(
            tok_lens, queries_keys, queries_keys, values, e["grad_ctx"], e["grad_self"], seqs, True, 0, PAIRS, 0
        )
        sums_cross = e["sums_cross"].reshape(seqs, 8, width).sum(axis=0)
        sums_self = sums_self.reshape(seqs, 8, width).sum(axis=0)
        last = e["sums_three"]
        e["grad_vec"] = jnp.concatenate(
            [
                sums_self[0:2],
                e["sums_one"][2:3],
                sums_cross[0:2],
                e["sums_two"][2:3],
                last[4:5],
                e["sums_one"][0:2],
                e["sums_two"][0:2],
                last[2:4],
                e["sums_pre"].reshape(-1, width),
                last[0:1],
                sums_one,
                sums_two,
                last[1:2],
                jnp.broadcast_to(jnp.sum(seq_len).astype(f32), (1, width)),
            ],
            axis=0,
        )

    def k_states(e):
        e["grad_states"] = input_grad(e["cross_dkv"], (0, 1), (first_w, first_w), (2 * D, 3 * D), BLOCK)

    def k_tokens(e):
        e["grad_tokens"] = input_grad(
            e["self_grads"], (0, 1, 2), (first_w, first_w, second_w), (0, D, 0), seqs * length, (e["grad_one"],)
        )

    kernels = {
        "hidden": (k_hidden, ("grad_ffn",), ("grad_pre", "sums_pre")),
        "two": (k_two, ("grad_pre",), ("grad_two", "grad_cross", "grad_ctx", "sums_two")),
        "cross": (k_cross, ("grad_ctx", "grad_cross"), ("cross_grads", "cross_dkv", "sums_cross")),
        "one": (k_one, ("cross_grads",), ("grad_one", "grad_self", "grad_ctx", "sums_one")),
        "self": (k_self, ("grad_ctx", "grad_self"), ("self_grads", "grad_vec")),
        "states": (k_states, ("cross_dkv",), ("grad_states",)),
        "tokens": (k_tokens, ("self_grads",), ("grad_tokens",)),
    }
    n_vec = vec_w.shape[0]
    if linked:
        order = links.plane_order()
        sums = {}

        def planes_of(name, x_mine, x_peer, y_mine, y_peer, x_at, y_at, stride, wide=D):
            spots = [(x_at(ux, y), *y_at(ux)) for ux, y in order]
            slots = [a if a.ndim == 3 else a[None] for a in (x_mine, x_peer, y_mine, y_peer)]
            sums[name] = Sum(links, unit_planes(*slots, spots, links.z, stride, shard_rows, wide))

        def k_planes_2(e):
            planes_of(
                "2", e["hidden"], e["hidden_peer"], e["grad_ffn"], e["grad_ffn_peer"],
                lambda ux, y: y * UNITS + ux * 2 + core, lambda ux: (0 * ux, 0 * ux), 2 * UNITS,
            )

        def k_planes_1(e):
            planes_of(
                "1", e["normed_two_low"], e["normed_two_low_peer"], e["grad_pre"], e["grad_pre_peer"],
                lambda ux, y: y, lambda ux: (0 * ux, ux * 2 + core), 2,
            )

        def k_planes_t(e):
            planes_of(
                "t", e["cross_in"], e["cross_in_peer"], e["cross_grads"], e["cross_grads_peer"],
                lambda ux, y: core * 2 * links.depth + y, lambda ux: (core + 0 * ux, ux), 2, D // 2,
            )

        def k_planes_a(e):
            planes_of(
                "a", e["self_in"], e["self_in_peer"], e["self_grads"], e["self_grads_peer"],
                lambda ux, y: y + 2 * links.depth * (ux * core), lambda ux: (ux * 2 + core, 0 * ux), 2,
            )

        def k_theirs(e):
            e["theirs"] = state_grad(state_rows, e["cross_dkv"], 1 - core)

        def k_mine(e):
            e["mine"] = state_grad(state_rows, e["cross_dkv"], core)

        def k_planes_e(e):
            spots = [(y, ux) for ux, y in order]
            sums["e"] = Sum(links, sum_planes(e["mine"], e["theirs_peer"], spots, links.z, shard_rows, D // 2))

        states_of = {"1": (fc1_w, fc1_m, fc1_v), "2": (fc2_w, fc2_m, fc2_v)}
        whole_unit, half_unit = (1, shard_rows, D), (1, shard_rows, D // 2)
        ways = {
            "2": ((shard_rows, D), lambda u: (u, 0)),
            "1": ((shard_rows, D), lambda u: (0, u)),
            "a": (whole_unit, lambda u: (u, 0, 0)),
            "t": (half_unit, lambda u: (4 + 3 * (u % 2), 0, u // 2)),
            "e": (half_unit, lambda u: (5 + u % 2, 0, u // 2)),
        }

        def k_adam(name):
            def kernel(e):
                place_of = name if name in states_of else "attn"
                state = states_of.get(name, (attn_w, attn_m, attn_v))
                e[place_of] = adam_units(spot, sums[name].parts, state, *ways[name], e.get(place_of))

            return kernel

        kernels |= {
            "planes_2": (k_planes_2, ("hidden", "hidden_peer", "grad_ffn", "grad_ffn_peer"), ()),
            "planes_1": (k_planes_1, ("normed_two_low", "normed_two_low_peer", "grad_pre", "grad_pre_peer"), ()),
            "planes_t": (k_planes_t, ("cross_in", "cross_in_peer", "cross_grads", "cross_grads_peer"), ()),
            "planes_a": (k_planes_a, ("self_in", "self_in_peer", "self_grads", "self_grads_peer"), ()),
            "theirs": (k_theirs, ("cross_dkv",), ("theirs",)),
            "mine": (k_mine, ("cross_dkv",), ("mine",)),
            "planes_e": (k_planes_e, ("mine", "theirs_peer"), ()),
        }
        for name in "21ate":
            kernels["adam_" + name] = (k_adam(name), (), ())
        env |= {"self_in_peer": self_in_peer, "cross_in_peer": cross_in_peer}
        vec_perms = {"c": links.to_core, "z1": to_z1, "z2": to_z2, "s1": swap1, "s2": swap2}
        CLOCK[:] = [CLOCK[0]]
        for at, (kernel, *events) in enumerate(PLAN):
            if kernel:
                kernels[kernel][0](env)
            moved = [event[4:] for event in events if event.startswith("sum ")]
            made = [name[-1] for name in (kernel,) if name.startswith("planes")]
            landing = [event[5:] for event in events if event.startswith("land ")]
            names = set(kernels[kernel][2]) if kernel else set()
            for later in PLAN[at + 1 :]:
                if later[0]:
                    names |= set(kernels[later[0]][1])
                    break
            names |= {name + "_peer" for name in landing}
            names |= {event[5:] for event in events if event.startswith("give ")}
            if "vec" in landing or any(event.startswith("vec ") for event in events):
                names |= {"grad_vec"}
            names = sorted(name for name in names if name in env)
            here = [sums[name] for name in sorted({*moved, *made})]
            arrays = [env[name] for name in names]
            if kernel.startswith("adam"):
                place_of = kernel[5:] if kernel[5:] in states_of else "attn"
                arrays.append(env[place_of][0])
            held = land(here, *arrays)
            env.update(zip(names, held))
            if kernel.startswith("adam"):
                env[place_of][0] = held[-1]
            if "vec" in landing:
                env["grad_vec"] = env["grad_vec"] + env["vec_peer"]
            add(*[sums[name] for name in moved])
            if moved:
                held = land(here, *[env[name] for name in names])
                env.update(zip(names, held))
            go(*[sums[name] for name in moved])
            for event in events:
                if event.startswith("give "):
                    env[event[5:] + "_peer"] = peer(env[event[5:]])
                elif event.startswith("vec "):
                    env["vec_peer"] = send(env["grad_vec"], vec_perms[event[4:]])
        fc1_new, fc2_new, attn_new = env["1"], env["2"], env["attn"]
        grad_vec = env["grad_vec"]
    else:
        for name in ("hidden", "two", "cross", "one", "self", "states", "tokens"):
            kernels[name][0](env)
        self_grads, cross_grads, cross_dkv = env["self_grads"], env["cross_grads"], env["cross_dkv"]
        grad_vec = lax.psum(env["grad_vec"], ("dp", "fsdp"))

        def owned(inputs, grads, dim):
            part = dot_grad(inputs, grads).astype(bf16)
            part = lax.psum_scatter(part, "fsdp", scatter_dimension=dim, tiled=True)
            return lax.psum(part, "dp").astype(f32)

        grad_attn = jnp.stack(
            [owned(self_in[u // 3], self_grads[u], 0) for u in range(4)]
            + [
                owned(normed_one_low, cross_grads[0], 0),
                owned(state_rows, cross_dkv[0], 0),
                owned(state_rows, cross_dkv[1], 0),
                owned(cross_in[1], cross_grads[1], 0),
            ]
        )
        grad_fc1, grad_fc2 = owned(normed_two_low, env["grad_pre"], 0), owned(hidden, grad_ffn, 0)
        attn_new = adam_update(attn_w, attn_m, attn_v, grad_attn, matrix_rate, matrix_decay)
        fc1_new = adam_update(fc1_w, fc1_m, fc1_v, grad_fc1, matrix_rate, matrix_decay)
        fc2_new = adam_update(fc2_w, fc2_m, fc2_v, grad_fc2, matrix_rate, matrix_decay)
    grad_tokens, grad_states = env["grad_tokens"], env["grad_states"]
    stats = grad_vec[n_vec:]
    stream_rms = jnp.sqrt(jnp.sum(stats[:4], axis=1) / (stats[4, 0] * D))
    cols = vec_w.shape[1]
    vec_grad = lax.dynamic_slice_in_dim(grad_vec[:n_vec], lax.axis_index("fsdp") * cols, cols, 1)
    vec_new = adam_update(vec_w, CLOCK[0] if linked else vec_m, vec_v, vec_grad, vector_rate, 0.0)
    return (
        mixed.reshape(tokens.shape),
        grad_tokens.reshape(tokens.shape),
        grad_states.reshape(states.shape),
        stream_rms,
        *attn_new,
        *fc1_new,
        *fc2_new,
        *vec_new,
    )


def solution(mesh):
    rows = P(None, ("dp", "fsdp"), None, None)
    lens = P(None, ("dp", "fsdp"))
    attn, fc, vec = P(None, "fsdp", None), P("fsdp", None), P(None, "fsdp")
    state = (attn,) * 3 + (fc,) * 6 + (vec,) * 3
    return jax.shard_map(
        partial(on_device, mesh.shape["dp"], mesh.shape["fsdp"]),
        mesh=mesh,
        in_specs=(rows, rows, rows, lens, lens) + state,
        out_specs=(rows, rows, rows, P()) + state,
        check_vma=False,
    )
```

```python
from functools import partial

import jax
import jax.numpy as jnp
from jax import lax
from jax.experimental import pallas as pl
from jax.experimental.pallas import tpu as pltpu
from jax.sharding import PartitionSpec as P

D = 1024
H = 16
DH = 64
STEP = 7
PAIRS = H // 2
UNITS = 4
LANES = 128
TAIL = 16

momentum_decay = 0.9
square_decay = 0.999
matrix_rate = 0.08
vector_rate = 0.3
matrix_decay = 0.01
epsilon = 1e-08
norm_epsilon = 1e-05
fix_first = 1.0 - momentum_decay**STEP
fix_second = 1.0 - square_decay**STEP

f32 = jnp.float32
bf16 = jnp.bfloat16
ANY = pl.BlockSpec(memory_space=pl.ANY)
MIB = 1024 * 1024
FIRST, SECOND = (0, 1, 5, 6), (2, 3, 4, 7)


def params(mib):
    return pltpu.CompilerParams(vmem_limit_bytes=mib * MIB)


def cost(nbytes):
    return pl.CostEstimate(flops=0, bytes_accessed=int(nbytes), transcendentals=0)


def array(shape, kind=bf16):
    return jax.ShapeDtypeStruct(shape, kind)


def far_array(shape, kind=bf16):
    return pltpu.HBM(shape, kind)


def whole(shape):
    return pl.BlockSpec(shape, lambda *at: (0,) * len(shape))


def far(values):
    return pltpu.with_memory_space_constraint(values, pltpu.HBM)


def dot(left, right):
    return jnp.dot(left, right, preferred_element_type=f32)


def dot_back(left, right):
    return lax.dot_general(left, right, (((1,), (1,)), ((), ())), preferred_element_type=f32)


def dot_grad(inputs, grads):
    return lax.dot_general(inputs, grads, (((0,), (0,)), ((), ())), preferred_element_type=f32)


def norm_forward(stream, gain, bias):
    centred = stream - jnp.mean(stream, axis=-1, keepdims=True)
    spread = jnp.mean(centred * centred, axis=-1, keepdims=True)
    scale = lax.rsqrt(spread + norm_epsilon)
    unit = centred * scale
    return unit * gain + bias, unit, scale


def norm_backward(grad, unit, scale, gain):
    scaled = grad * gain
    mean = jnp.mean(scaled, axis=-1, keepdims=True)
    along = jnp.mean(scaled * unit, axis=-1, keepdims=True)
    return scale * (scaled - mean - unit * along), column_sum(grad * unit), column_sum(grad)


def column_sum(values):
    return jnp.sum(values.astype(f32), axis=0, keepdims=True)


def valid_rows(len_ref, rows, length):
    spot = lax.broadcasted_iota(jnp.int32, (rows, 1), 0)
    limit = jnp.full((rows, 1), len_ref[0], jnp.int32)
    for m in range(1, rows // length):
        limit = jnp.where(spot >= m * length, m * length + len_ref[m], limit)
    return spot < limit


def add_up(total_ref, step, part):
    @pl.when(step == 0)
    def _():
        total_ref[...] = part

    @pl.when(step > 0)
    def _():
        total_ref[...] += part


BLOCK = 1024


def project_kernel(x_ref, w_ref, b_ref, o_ref):
    o_ref[...] = (dot(x_ref[...], w_ref[...]) + b_ref[...]).astype(bf16)


def project(rows, weights, bias, at):
    n_rows, depth = rows.shape
    width = bias.shape[1]
    return pl.pallas_call(
        project_kernel,
        out_shape=array((n_rows, width)),
        grid=(width // BLOCK,),
        in_specs=[
            whole((n_rows, depth)),
            pl.BlockSpec((depth, BLOCK), lambda n: (0, at // BLOCK + n)),
            pl.BlockSpec((1, BLOCK), lambda n: (0, n)),
        ],
        out_specs=pl.BlockSpec((n_rows, BLOCK), lambda n: (0, n)),
        compiler_params=params(22),
        cost_estimate=cost(1024),
    )(rows, weights, bias)


def join_kernel(length, rows_at, len_ref, x_ref, w_ref, res_ref, vec_ref, *outs):
    h_ref, low_ref, unit_ref, scale_ref, sums_ref, total_ref = outs
    step = pl.program_id(0)
    add_up(total_ref, step, dot(x_ref[...], w_ref[...]))

    @pl.when(step == pl.num_programs(0) - 1)
    def _():
        bias, gain, offset = (vec_ref[r : r + 1, :] for r in rows_at)
        branch = total_ref[...] + bias
        out, unit, scale = norm_forward(res_ref[...].astype(f32) + branch, gain, offset)
        h_ref[...] = out
        low_ref[...] = out.astype(bf16)
        unit_ref[...] = unit
        scale_ref[...] = jnp.broadcast_to(scale, scale_ref.shape)
        valid = valid_rows(len_ref, branch.shape[0], length)
        sums_ref[...] = column_sum(jnp.where(valid, branch * branch, 0.0))


def join(lengths, rows, weights, at, residual, vec, rows_at):
    n_rows = residual.shape[0]
    slot = rows.ndim == 3
    x_spec = (
        pl.BlockSpec((None, n_rows, BLOCK), lambda k, n: (1, 0, k))
        if slot
        else pl.BlockSpec((n_rows, BLOCK), lambda k, n: (0, k))
    )
    return pl.pallas_call(
        partial(join_kernel, n_rows // lengths.shape[0], rows_at),
        out_shape=[
            array((n_rows, D), f32),
            array((n_rows, D)),
            far_array((n_rows, D), f32),
            array((n_rows, LANES), f32),
            array((1, D), f32),
        ],
        grid_spec=pltpu.PrefetchScalarGridSpec(
            num_scalar_prefetch=1,
            grid=(D // BLOCK,),
            in_specs=[
                x_spec,
                pl.BlockSpec((BLOCK, D), lambda k, n: (k, at // D)),
                whole((n_rows, D)),
                whole(vec.shape),
            ],
            out_specs=[whole((n_rows, D))] * 3 + [whole((n_rows, LANES)), whole((1, D))],
            scratch_shapes=[pltpu.VMEM((n_rows, D), f32)],
        ),
        compiler_params=params(12),
        cost_estimate=cost(1024),
    )(lengths, rows, weights, residual, vec)


def hidden_kernel(x_ref, w_ref, b_ref, g_ref, slope_ref):
    u = dot(x_ref[...], w_ref[...]) + b_ref[...]
    phi = 0.5 * (1.0 + lax.erf(u * 2.0**-0.5))
    g_ref[...] = (u * phi).astype(bf16)
    slope_ref[...] = (phi + u * jnp.exp(-0.5 * u * u) * (2.0 * jnp.pi) ** -0.5).astype(bf16)


def hidden_layer(rows, weights, bias):
    n_rows, depth = rows.shape
    width = weights.shape[1]
    out_spec = pl.BlockSpec((n_rows, BLOCK), lambda n: (0, n))
    return pl.pallas_call(
        hidden_kernel,
        out_shape=[array((n_rows, width))] * 2,
        grid=(width // BLOCK,),
        in_specs=[
            whole((n_rows, depth)),
            pl.BlockSpec((depth, BLOCK), lambda n: (0, n)),
            pl.BlockSpec((1, BLOCK), lambda n: (0, n)),
        ],
        out_specs=[out_spec] * 2,
        compiler_params=params(14),
        cost_estimate=cost(1024),
    )(rows, weights, bias)


def turn_kernel(length, rows_at, len_ref, x_ref, w_ref, res_ref, cot_ref, vec_ref, *outs):
    mixed_ref, dr_ref, low_ref, sums_ref, total_ref = outs
    step = pl.program_id(0)
    add_up(total_ref, step, dot(x_ref[...], w_ref[...]))

    @pl.when(step == pl.num_programs(0) - 1)
    def _():
        bias, gain, offset = (vec_ref[r : r + 1, :] for r in rows_at)
        branch = total_ref[...] + bias
        out, unit, scale = norm_forward(res_ref[...] + branch, gain, offset)
        mixed_ref[...] = out.astype(bf16)
        valid = valid_rows(len_ref, branch.shape[0], length)
        grad, grad_gain, grad_bias = norm_backward(cot_ref[...].astype(f32), unit, scale, gain)
        low = grad.astype(bf16)
        dr_ref[...] = grad
        low_ref[...] = low
        sums_ref[0:1, :] = column_sum(jnp.where(valid, out * out, 0.0))
        sums_ref[1:2, :] = column_sum(jnp.where(valid, branch * branch, 0.0))
        sums_ref[2:3, :] = grad_gain
        sums_ref[3:4, :] = grad_bias
        sums_ref[4:5, :] = column_sum(low)
        sums_ref[5:8, :] = jnp.zeros((3, D), f32)


def turn(lengths, rows, weights, residual, cotangent, vec, rows_at):
    n_rows, depth = rows.shape
    return pl.pallas_call(
        partial(turn_kernel, n_rows // lengths.shape[0], rows_at),
        out_shape=[array((n_rows, D)), far_array((n_rows, D), f32), array((n_rows, D)), array((8, D), f32)],
        grid_spec=pltpu.PrefetchScalarGridSpec(
            num_scalar_prefetch=1,
            grid=(depth // BLOCK,),
            in_specs=[
                pl.BlockSpec((n_rows, BLOCK), lambda k, n: (0, k)),
                pl.BlockSpec((BLOCK, D), lambda k, n: (k, 0)),
                whole((n_rows, D)),
                whole((n_rows, D)),
                whole(vec.shape),
            ],
            out_specs=[whole((n_rows, D))] * 3 + [whole((8, D))],
            scratch_shapes=[pltpu.VMEM((n_rows, D), f32)],
        ),
        compiler_params=params(14),
        cost_estimate=cost(1024),
    )(lengths, rows, weights, residual, cotangent, vec)


def hidden_back_kernel(e_ref, w_ref, slope_ref, du_ref, sums_ref):
    du = (dot_back(e_ref[...], w_ref[...]) * slope_ref[...].astype(f32)).astype(bf16)
    du_ref[...] = du
    sums_ref[...] = column_sum(du)


def hidden_back(grads, weights, slope):
    n_rows, width = slope.shape
    block = pl.BlockSpec((n_rows, BLOCK), lambda n: (0, n))
    return pl.pallas_call(
        hidden_back_kernel,
        out_shape=[far_array((n_rows, width)), array((1, width), f32)],
        grid=(width // BLOCK,),
        in_specs=[whole((n_rows, D)), pl.BlockSpec((BLOCK, D), lambda n: (n, 0)), block],
        out_specs=[block, pl.BlockSpec((1, BLOCK), lambda n: (0, n))],
        compiler_params=params(14),
        cost_estimate=cost(1024),
    )(grads, weights, slope)


def join_back_kernel(row_at, g_ref, w_ref, dr_ref, unit_ref, scale_ref, vec_ref, after_ref, *outs):
    out_ref, low_ref, next_ref, sums_ref, total_ref = outs
    step = pl.program_id(0)
    add_up(total_ref, step, dot_back(g_ref[...], w_ref[...]))

    @pl.when(step == pl.num_programs(0) - 1)
    def _():
        grad, grad_gain, grad_bias = norm_backward(
            dr_ref[...] + total_ref[...], unit_ref[...], scale_ref[:, 0:1], vec_ref[row_at : row_at + 1, :]
        )
        low = grad.astype(bf16)
        out_ref[...] = grad
        low_ref[...] = low
        next_ref[...] = dot_back(low, after_ref[...]).astype(bf16)
        sums_ref[0:1, :] = grad_gain
        sums_ref[1:2, :] = grad_bias
        sums_ref[2:3, :] = column_sum(low)
        sums_ref[3:8, :] = jnp.zeros((5, D), f32)


def join_back(grads, weights, at, above, unit, scale, vec, row_at, after, after_at):
    slot = grads.ndim == 3
    n_rows, width = grads.shape[-2:]
    g_spec = (
        pl.BlockSpec((None, n_rows, BLOCK), lambda k: (0, 0, k))
        if slot
        else pl.BlockSpec((n_rows, BLOCK), lambda k: (0, k))
    )
    return pl.pallas_call(
        partial(join_back_kernel, row_at),
        out_shape=[far_array((n_rows, D), f32), array((n_rows, D)), array((n_rows, D)), array((8, D), f32)],
        grid=(width // BLOCK,),
        in_specs=[
            g_spec,
            pl.BlockSpec((D, BLOCK), lambda k: (0, at // BLOCK + k)),
            whole((n_rows, D)),
            whole((n_rows, D)),
            whole((n_rows, LANES)),
            whole(vec.shape),
            pl.BlockSpec((D, D), lambda k: (0, after_at // D)),
        ],
        out_specs=[whole((n_rows, D))] * 3 + [whole((8, D))],
        scratch_shapes=[pltpu.VMEM((n_rows, D), f32)],
        compiler_params=params(18),
        cost_estimate=cost(1024),
    )(grads, far(weights), far(above), far(unit), scale, vec, far(after))


def input_grad_kernel(count, *refs):
    gs, ws, rest, o_ref = refs[:count], refs[count : 2 * count], refs[2 * count : -1], refs[-1]
    total = sum(dot_back(g[...], w[...]) for g, w in zip(gs, ws))
    if rest:
        total = total + rest[0][...]
    o_ref[...] = total.astype(bf16)


def input_grad(grads, slots, weights, ats, block, rest=()):
    n_rows = grads.shape[1]
    row_block = pl.BlockSpec((block, D), lambda r: (r, 0))
    return pl.pallas_call(
        partial(input_grad_kernel, len(slots)),
        out_shape=array((n_rows, D)),
        grid=(n_rows // block,),
        in_specs=[pl.BlockSpec((None, block, D), lambda r, s=s: (s, r, 0)) for s in slots]
        + [pl.BlockSpec((D, D), lambda r, a=a: (0, a // D)) for a in ats]
        + [row_block] * len(rest),
        out_specs=row_block,
        compiler_params=params(22),
        cost_estimate=cost(1024),
    )(*[far(grads)] * len(slots), *[far(w) for w in weights], *rest)


def state_grad_kernel(slot_ref, e_ref, g_ref, o_ref):
    o_ref[...] = dot_grad(e_ref[...], g_ref[...]).astype(bf16)


def state_grad(states, grads, slot):
    n_rows, block = states.shape[0], D // 2
    return pl.pallas_call(
        state_grad_kernel,
        out_shape=array((D, D)),
        grid_spec=pltpu.PrefetchScalarGridSpec(
            num_scalar_prefetch=1,
            grid=(D // block,),
            in_specs=[
                pl.BlockSpec((n_rows, block), lambda r, s: (0, r)),
                pl.BlockSpec((None, n_rows, D), lambda r, s: (s[0], 0, 0)),
            ],
            out_specs=pl.BlockSpec((block, D), lambda r, s: (r, 0)),
        ),
        compiler_params=params(18),
        cost_estimate=cost(1024),
    )(jnp.stack([slot]).astype(jnp.int32), states, far(grads))


def two_heads(rows):
    low_half = lax.broadcasted_iota(jnp.int32, rows.shape, 1) < DH
    zero = jnp.zeros_like(rows)
    return jnp.concatenate([jnp.where(low_half, rows, zero), jnp.where(low_half, zero, rows)], axis=0)


def one_row(both):
    half = both.shape[0] // 2
    low_half = lax.broadcasted_iota(jnp.int32, (half, both.shape[1]), 1) < DH
    return jnp.where(low_half, both[:half], both[half:])


def masked_exp(queries, keys, valid, causal):
    scores = dot_back(queries, keys)
    place = lax.broadcasted_iota(jnp.int32, (1, scores.shape[1]), 1)
    if causal:
        rows = scores.shape[0] // 2
        spot = lax.broadcasted_iota(jnp.int32, scores.shape, 0)
        spot = jnp.where(spot >= rows, spot - rows, spot)
        spots = lax.broadcasted_iota(jnp.int32, scores.shape, 1)
        allowed = (spots <= spot) & (spots < valid)
        scores = jnp.where(allowed, scores, -1e30)
    else:
        scores = scores + jnp.where(place < valid, 0.0, -1e30)
    top = jnp.max(scores, axis=-1, keepdims=True)
    exponent = jnp.exp(scores - top)
    return exponent, 1.0 / jnp.sum(exponent, axis=-1, keepdims=True)


def attend_kernel(causal, len_ref, q_ref, k_ref, v_ref, x_ref, o_ref):
    valid = len_ref[pl.program_id(0)]
    o_ref[0] = x_ref[...]
    for at in range(0, q_ref.shape[1], LANES):
        pair = slice(at, at + LANES)
        queries = two_heads(q_ref[:, pair] * DH**-0.5)
        exponent, inverse = masked_exp(queries, k_ref[:, pair], valid, causal)
        o_ref[1, :, pair] = one_row(dot(exponent.astype(bf16), v_ref[:, pair]) * inverse).astype(bf16)


def attend_back_kernel(causal, len_ref, q_ref, k_ref, v_ref, do_ref, x_ref, dq_ref, *more):
    dkv_refs, sums_ref = more[:-1], more[-1]
    valid = len_ref[pl.program_id(0)]
    dq_ref[dq_ref.shape[0] - 1] = x_ref[...]
    sums_ref[2:8, :] = jnp.zeros((6, sums_ref.shape[1]), f32)
    for at in range(0, q_ref.shape[1], LANES):
        pair = slice(at, at + LANES)
        keys = k_ref[:, pair]
        queries = two_heads(q_ref[:, pair] * DH**-0.5)
        exponent, inverse = masked_exp(queries, keys, valid, causal)
        grads = two_heads(do_ref[:, pair])
        grad_probs = dot_back(grads, v_ref[:, pair])
        row_dot = jnp.sum(exponent * grad_probs, axis=-1, keepdims=True) * inverse
        grad_scores = (exponent * (grad_probs - row_dot)).astype(bf16)
        dq = one_row(dot(grad_scores, keys) * (inverse * DH**-0.5)).astype(bf16)
        dk = dot_grad(grad_scores, (queries * inverse).astype(bf16)).astype(bf16)
        dv = dot_grad(exponent.astype(bf16), (grads * inverse).astype(bf16)).astype(bf16)
        dq_ref[0, :, pair] = dq
        if dkv_refs:
            dkv_refs[0][0, :, pair], dkv_refs[0][1, :, pair] = dk, dv
        else:
            dq_ref[1, :, pair], dq_ref[2, :, pair] = dk, dv
        sums_ref[0:1, pair] = column_sum(dq)
        sums_ref[1:2, pair] = column_sum(dv)


def head_block(rows, at, group):
    return pl.BlockSpec((rows, LANES * group), lambda m, p, n: (m, at // group + p))


def slots_block(slots, rows, group):
    return pl.BlockSpec((slots, rows, LANES * group), lambda m, p, n: (0, m, p))


def attend(lengths, queries, keys, values, beside, seqs, causal, q_at, k_at, v_at):
    q_rows, k_rows = queries.shape[0] // seqs, keys.shape[0] // seqs
    group = PAIRS if causal else PAIRS // 2
    return pl.pallas_call(
        partial(attend_kernel, causal),
        out_shape=array((2, seqs * q_rows, D)),
        grid_spec=pltpu.PrefetchScalarGridSpec(
            num_scalar_prefetch=1,
            grid=(seqs, PAIRS // group),
            in_specs=[
                head_block(q_rows, q_at, group),
                head_block(k_rows, k_at, group),
                head_block(k_rows, v_at, group),
                head_block(q_rows, 0, group),
            ],
            out_specs=slots_block(2, q_rows, group),
        ),
        compiler_params=params(20),
        cost_estimate=cost(1024),
    )(lengths, queries, keys, values, beside)


def attend_back(lengths, queries, keys, values, grads, beside, seqs, causal, q_at, k_at, v_at):
    q_rows, k_rows = queries.shape[0] // seqs, keys.shape[0] // seqs
    group = PAIRS if causal else PAIRS // 2
    slots = 4 if causal else 2
    out_shape = [(far_array if causal else array)((slots, seqs * q_rows, D))]
    out_specs = [slots_block(slots, q_rows, group)]
    if not causal:
        out_shape.append(far_array((2, seqs * k_rows, D)))
        out_specs.append(slots_block(2, k_rows, group))
    out_shape.append(array((8 * seqs, D), f32))
    out_specs.append(head_block(8, 0, group))
    return pl.pallas_call(
        partial(attend_back_kernel, causal),
        out_shape=out_shape,
        grid_spec=pltpu.PrefetchScalarGridSpec(
            num_scalar_prefetch=1,
            grid=(seqs, PAIRS // group),
            in_specs=[
                head_block(q_rows, q_at, group),
                head_block(k_rows, k_at, group),
                head_block(k_rows, v_at, group),
                head_block(q_rows, 0, group),
                head_block(q_rows, 0, group),
            ],
            out_specs=out_specs,
        ),
        compiler_params=params(22),
        cost_estimate=cost(1024),
    )(lengths, queries, keys if causal else far(keys), values if causal else far(values), grads, beside)


def place_kernel(rows, idx_ref, *refs):
    slot = 0
    for piece in refs[:-1]:
        for j in range(piece.shape[0] // rows):
            at = pl.multiple_of(idx_ref[slot] * rows, rows)
            refs[-1][pl.ds(at, rows), :] = piece[j * rows : (j + 1) * rows, :]
            slot += 1


def place(pieces, slots):
    total, width = sum(piece.shape[0] for piece in pieces), pieces[0].shape[1]
    return pl.pallas_call(
        partial(place_kernel, total // len(slots)),
        out_shape=array((total, width), pieces[0].dtype),
        grid_spec=pltpu.PrefetchScalarGridSpec(
            num_scalar_prefetch=1,
            grid=(),
            in_specs=[pl.BlockSpec(memory_space=pltpu.VMEM)] * len(pieces),
            out_specs=pl.BlockSpec(memory_space=pltpu.VMEM),
        ),
        compiler_params=params(6),
        cost_estimate=cost(1024),
    )(jnp.stack(slots).astype(jnp.int32), *pieces)


def under(first, second):
    return place([first, second], [jnp.int32(0), jnp.int32(1)])


def assemble_kernel(wide, rows, step, counts, idx_ref, *refs):
    pieces, (out_ref, held, in_sems, out_sems) = refs[: len(counts)], refs[len(counts) :]
    loads, at = [], 0
    for i, (piece, count) in enumerate(zip(pieces, counts)):
        loads.append(pltpu.make_async_copy(piece, held.at[pl.ds(at * step, count * step), :], in_sems.at[i]))
        at += count
    for load in loads:
        load.start()
    stores, copy = [], 0
    for load, count in zip(loads, counts):
        load.wait()
        for _ in range(count):
            unit, shard = idx_ref[0, copy], idx_ref[1, copy]
            if wide:
                target = out_ref.at[
                    pl.ds(pl.multiple_of(shard * rows, rows), rows), pl.ds(pl.multiple_of(unit * D, D), D)
                ]
            else:
                row = (shard * UNITS + unit) * rows
                target = out_ref.at[pl.ds(pl.multiple_of(row, rows), rows), :]
            store = pltpu.make_async_copy(held.at[pl.ds(copy * step, rows), :], target, out_sems.at[copy])
            store.start()
            stores.append(store)
            copy += 1
    for store in stores:
        store.wait()


def assemble(pieces, places, rows, step, wide):
    counts = [piece.shape[0] // step for piece in pieces]
    shards = len(places) // UNITS
    return pl.pallas_call(
        partial(assemble_kernel, wide, rows, step, counts),
        out_shape=array((shards * rows, UNITS * D) if wide else (UNITS * shards * rows, D)),
        grid_spec=pltpu.PrefetchScalarGridSpec(
            num_scalar_prefetch=1,
            grid=(),
            in_specs=[ANY] * len(pieces),
            out_specs=ANY,
            scratch_shapes=[
                pltpu.VMEM((len(places) * step, D), bf16),
                pltpu.SemaphoreType.DMA((len(pieces),)),
                pltpu.SemaphoreType.DMA((len(places),)),
            ],
        ),
        compiler_params=params(10),
        cost_estimate=cost(1024),
    )(jnp.stack([jnp.stack([place[j] for place in places]) for j in range(2)]).astype(jnp.int32), *pieces)


def store_plane(step, plane, outs):
    @pl.when(step < 2)
    def _():
        outs[0][...] = plane

    @pl.when(step == 2)
    def _():
        outs[1][...] = plane

    @pl.when(step == 3)
    def _():
        outs[2][...] = plane


def planes_kernel(depth, idx_ref, *refs):
    x_mine, x_peer = refs[:depth], refs[depth : 2 * depth]
    inputs = jnp.concatenate(
        [jnp.concatenate([x[...] for x in xs], axis=1) for xs in (x_mine, x_peer)], axis=0
    )
    grads = jnp.concatenate([y[...] for y in refs[2 * depth : 2 * depth + 2]], axis=0)
    store_plane(pl.program_id(0), dot_grad(inputs, grads).astype(bf16), refs[-3:])


def sum_planes_kernel(depth, idx_ref, *refs):
    mine, peer, outs = refs[:depth], refs[depth : 2 * depth], refs[-3:]
    plane = jnp.concatenate([a[...].astype(f32) + b[...].astype(f32) for a, b in zip(mine, peer)], axis=0)
    store_plane(pl.program_id(0), plane.astype(bf16), outs)


def planes_call(kernel, table, in_specs, operands, plane, width):
    return pl.pallas_call(
        kernel,
        out_shape=[array((n * plane, width)) for n in (2, 1, 1)],
        grid_spec=pltpu.PrefetchScalarGridSpec(
            num_scalar_prefetch=1,
            grid=(4,),
            in_specs=in_specs,
            out_specs=[
                pl.BlockSpec((plane, width), lambda k, i: (jnp.minimum(k, 1), 0)),
                pl.BlockSpec((plane, width), lambda k, i: (0, 0)),
                pl.BlockSpec((plane, width), lambda k, i: (0, 0)),
            ],
        ),
        compiler_params=params(13),
        cost_estimate=cost(1024),
    )(jnp.stack(table).astype(jnp.int32), *operands)


def column(spots, j):
    return jnp.stack([spot[j] for spot in spots])


def unit_planes(x_mine, x_peer, y_mine, y_peer, spots, z, stride, rows, width=D):
    depth, tokens = 4, x_mine.shape[1]
    blocks = x_mine.shape[2] // rows

    def x_spec(j):
        def at(k, i):
            block = i[0, k] + stride * i[3, j]
            return (block // blocks, 0, block % blocks)

        return pl.BlockSpec((None, tokens, rows), at)

    x_specs = [x_spec(j) for j in range(depth)]
    y_spec = pl.BlockSpec((None, tokens, width), lambda k, i: (i[1, k], 0, i[2, k]))
    table = [column(spots, j) for j in range(3)] + [jnp.stack([z, z ^ 2, z ^ 1, z ^ 3])]
    if x_peer.shape[2] > 2 * D:
        x_mine, x_peer = far(x_mine), far(x_peer)
    operands = [x_mine] * depth + [x_peer] * depth + [y_mine, y_peer]
    return planes_call(
        partial(planes_kernel, depth), table, x_specs * 2 + [y_spec] * 2, operands, depth * rows, width
    )


def sum_planes(mine, peer, spots, z, rows, width):
    depth = 4
    specs = [
        pl.BlockSpec((rows, width), lambda k, i, j=j: (2 * i[2, j] + i[0, k], i[1, k])) for j in range(depth)
    ]
    table = [column(spots, j) for j in range(2)] + [jnp.stack([z, z ^ 2, z ^ 1, z ^ 3])]
    return planes_call(
        partial(sum_planes_kernel, depth), table, specs * 2, [mine] * depth + [peer] * depth, depth * rows, width
    )


def adam_update(weight, first, second, grad, rate, decay):
    first = momentum_decay * first + (1.0 - momentum_decay) * grad
    second = square_decay * second + (1.0 - square_decay) * grad * grad
    update = first / fix_first / (jnp.sqrt(second / fix_second) + epsilon) + decay * weight
    return (weight - rate * update, first, second)


def adam_kernel(idx_ref, here_ref, there_ref, w_ref, m_ref, v_ref, *rest):
    w_out, m_out, v_out = rest[-3:]
    away = pl.program_id(0) ^ idx_ref[0]
    grad = jnp.where(away % 2 == 0, here_ref[...], there_ref[...]).astype(f32)
    if len(w_ref.shape) == 3:
        grad = grad[None]
    w_out[...], m_out[...], v_out[...] = adam_update(
        w_ref[...], m_ref[...], v_ref[...], grad, matrix_rate, matrix_decay
    )


def adam_pair_kernel(cuts, idx_ref, here_ref, there_ref, w_ref, m_ref, v_ref, *rest):
    w_out, m_out, v_out = rest[-3:]
    for unit, cut in enumerate(cuts):
        grad = jnp.where(idx_ref[0] % 2 == unit, here_ref[...], there_ref[...]).astype(f32)
        if len(w_ref.shape) == 3:
            grad = grad[None]
        w_out[cut], m_out[cut], v_out[cut] = adam_update(
            w_ref[cut], m_ref[cut], v_ref[cut], grad, matrix_rate, matrix_decay
        )


def adam_pairs(spot, grads, state, block_shape, dim, earlier=None):
    pair = tuple(2 * n if d == dim else n for d, n in enumerate(block_shape))
    spec = pl.BlockSpec(pair, lambda p, i: tuple(p if d == dim else 0 for d in range(len(pair))))
    cuts = [
        tuple(slice(k * n, (k + 1) * n) if d == dim else slice(None) for d, n in enumerate(block_shape))
        for k in range(2)
    ]
    rows, width = grads[0].shape[0] // 2, grads[0].shape[1]
    g_spec = pl.BlockSpec((rows, width), lambda p, i: (p ^ (i[0] // 2), 0))
    extra = list(earlier) if earlier is not None else []
    state = [far(a) for a in state]
    outs = pl.pallas_call(
        partial(adam_pair_kernel, cuts),
        out_shape=[array(a.shape, f32) for a in state],
        grid_spec=pltpu.PrefetchScalarGridSpec(
            num_scalar_prefetch=1,
            grid=(UNITS // 2,),
            in_specs=[g_spec] * 2 + [spec] * 3 + [ANY] * len(extra),
            out_specs=[spec] * 3,
        ),
        input_output_aliases={6 + i: i for i in range(len(extra))},
        compiler_params=params(18),
        cost_estimate=cost(1024),
    )(jnp.stack([spot]).astype(jnp.int32), *grads, *state, *extra)
    return list(outs)


def adam_units(spot, grads, state, block_shape, at, earlier=None):
    spec = pl.BlockSpec(block_shape, lambda u, i: at(u))
    rows, width = grads[0].shape[0] // 2, grads[0].shape[1]
    g_spec = pl.BlockSpec((rows, width), lambda u, i: ((u ^ i[0]) // 2, 0))
    extra = list(earlier) if earlier is not None else []
    state = [far(a) for a in state]
    outs = pl.pallas_call(
        adam_kernel,
        out_shape=[array(a.shape, f32) for a in state],
        grid_spec=pltpu.PrefetchScalarGridSpec(
            num_scalar_prefetch=1,
            grid=(UNITS,),
            in_specs=[g_spec] * 2 + [spec] * 3 + [ANY] * len(extra),
            out_specs=[spec] * 3,
        ),
        input_output_aliases={6 + i: i for i in range(len(extra))},
        compiler_params=params(8),
        cost_estimate=cost(1024),
    )(jnp.stack([spot]).astype(jnp.int32), *grads, *state, *extra)
    return list(outs)


CLOCK = []


def hold(*values):
    CLOCK[0], *held = lax.optimization_barrier((CLOCK[0], *values))
    return held


class Links:
    def __init__(self, n_dp, n_fsdp):
        self.n_fsdp, self.depth = n_fsdp, n_fsdp // 2
        spot = lax.axis_index("dp")
        shard = lax.axis_index("fsdp")
        self.spot, self.shard = spot, shard
        self.x, self.core = spot // 2, spot % 2
        self.z, self.y = shard // 2, shard % 2
        ids = [
            (x, c, z, y) for x in range(2) for c in range(2) for z in range(self.depth) for y in range(2)
        ]

        def number(x, c, z, y):
            return ((x * 2 + c) * self.depth + z) * 2 + y

        def perm(to):
            return [(number(*i), number(*to(*i))) for i in ids]

        flip_x = lambda x, c, z, y: (1 - x, c, z, y)
        flip_y = lambda x, c, z, y: (x, c, z, 1 - y)
        self.to_core = perm(lambda x, c, z, y: (x, 1 - c, z, y))
        self.to_x = perm(flip_x)
        self.to_y = perm(flip_y)
        self.swap1 = perm(lambda x, c, z, y: flip_y(x, c, z, y) if c == 0 else flip_x(x, c, z, y))
        self.swap2 = perm(lambda x, c, z, y: flip_x(x, c, z, y) if c == 0 else flip_y(x, c, z, y))
        self.to_z1 = perm(lambda x, c, z, y: (x, c, z ^ 1, y))
        self.to_z2 = perm(lambda x, c, z, y: (x, c, z ^ 2, y))

    def send(self, block, perm):
        return lax.ppermute(block, ("dp", "fsdp"), perm)

    def column(self, arrived):
        return place(arrived, [self.z ^ away for away in (0, 2, 1, 3)])

    def kinds(self, core):
        x, y = self.x, self.y
        return ((x, y), (x ^ core, y ^ (1 - core)), (x ^ (1 - core), y ^ core), (1 - x, 1 - y))

    def finish(self, pieces, rows, wide, more=0):
        places = [
            (ux * 2 + core, 2 * z + y)
            for core in (self.core, 1 - self.core)
            for ux, y in self.kinds(core)
            for z in range(self.depth)
        ]
        return assemble(pieces, places, rows, rows + more, wide)

    def vectors(self, here, cols):
        half = here[0].shape[0] // 2
        step = half // self.depth

        def tails(piece, first):
            return jnp.stack(
                [
                    lax.slice(piece, (first + (z + 1) * step - TAIL, 0), (first + (z + 1) * step, 2 * cols))
                    for z in range(self.depth)
                ]
            )

        own, other = tails(here[0], 0), tails(here[1], half)
        pair = [jnp.where(self.y == 0, own, other), jnp.where(self.y == 0, other, own)]
        parts = [pair[f % 2][f // 2] for f in range(self.n_fsdp)]
        return jnp.concatenate(
            [
                jnp.concatenate([part[:, :cols] for part in parts], axis=1),
                jnp.concatenate([part[:1, cols:] for part in parts], axis=1),
            ],
            axis=0,
        )

    def plane_order(self):
        own, near, far, both = self.kinds(self.core)
        return far, both, near, own


def add_kernel(rows, count, *refs):
    ins, outs = refs[: len(rows)], refs[len(rows) :]
    total = sum(a[r : r + count, :].astype(f32) for a, r in zip(ins, rows)).astype(bf16)
    part = count // len(outs)
    for i, out in enumerate(outs):
        out[...] = total[i * part : (i + 1) * part]


def add_rows(terms, count, parts=1):
    width = terms[0][0].shape[1]
    vmem = pl.BlockSpec(memory_space=pltpu.VMEM)
    return pl.pallas_call(
        partial(add_kernel, [r for _, r in terms], count),
        out_shape=[array((count // parts, width))] * parts,
        in_specs=[vmem] * len(terms),
        out_specs=[vmem] * parts,
        compiler_params=params(8),
        cost_estimate=cost(1024),
    )(*[a for a, _ in terms])


class Sum:
    def __init__(self, links, planes):
        self.links, self.parts, self.step = links, list(planes), 0

    def add(self):
        parts = self.parts
        if self.step == 1:
            got, second, kept = parts
            half = second.shape[0]
            parts[1:2] = add_rows([(second, 0), (got, half)], half)
        elif self.step == 2:
            got, got_second, kept = parts
            self.parts = add_rows([(kept, 0), (got, 0), (got_second, 0)], kept.shape[0], 2)
        elif self.step == 3:
            self.parts = add_rows([(part, 0) for part in parts], parts[0].shape[0], 2)
        elif self.step == 4:
            self.parts = add_rows([(part, 0) for part in parts], parts[0].shape[0])
        elif self.step == 5:
            self.parts = [under(*parts)]
        self.parts = list(self.parts)

    def send(self):
        links, parts = self.links, self.parts
        if self.step == 0:
            parts[0] = links.send(parts[0], links.swap2)
        elif self.step < 4:
            parts[1] = links.send(parts[1], (links.swap1, links.to_z1, links.to_z2)[self.step - 1])
        elif self.step == 4:
            parts.append(links.send(parts[0], links.to_x))
        else:
            parts.append(links.send(parts[0], links.to_core))
        self.step += 1


def land(sums, *values):
    parts = hold(*values, *(part for one in sums for part in one.parts))
    values, parts = parts[: len(values)], parts[len(values) :]
    for one in sums:
        one.parts, parts = parts[: len(one.parts)], parts[len(one.parts) :]
    return values


def add(*sums):
    for one in sums:
        one.add()


def go(*sums):
    for one in sums:
        one.send()


PLAN = (
    ("", "give grad_ffn", "give hidden"),
    ("hidden", "land grad_ffn", "land hidden", "give grad_pre", "give normed_two_low"),
    ("planes_2", "land grad_pre", "land normed_two_low", "sum 2"),
    ("two",),
    ("planes_1",),
    ("", "sum 1"),
    ("cross", "sum 2", "give cross_grads"),
    ("one", "land cross_grads"),
    ("self",),
    ("planes_t", "sum 1", "sum 2", "give self_grads", "vec c"),
    ("", "sum t"),
    ("theirs", "land self_grads", "land vec", "sum 2", "give theirs"),
    ("planes_a", "vec z1", "sum 1", "sum t"),
    ("", "sum a"),
    ("mine", "land theirs", "land vec", "vec z2", "sum t"),
    ("planes_e", "sum 2"),
    ("tokens", "vec s1", "sum 1", "sum e", "land vec"),
    ("", "sum a", "sum t", "sum 2"),
    ("states", "land vec", "vec s2"),
    ("", "sum 1"),
    ("adam_2", "sum e", "sum a"),
    ("", "sum t", "sum 1"),
    ("adam_1", "sum e", "sum t", "land vec"),
    ("", "sum a"),
    ("adam_t", "sum e"),
    ("", "sum a"),
    ("", "sum e"),
    ("", "sum a", "sum e"),
    ("adam_e",),
    ("adam_a",),
)


def on_device(
    n_dp,
    n_fsdp,
    tokens,
    states,
    cotangent,
    seq_len,
    enc_len,
    attn_w,
    attn_m,
    attn_v,
    fc1_w,
    fc1_m,
    fc1_v,
    fc2_w,
    fc2_m,
    fc2_v,
    vec_w,
    vec_m,
    vec_v,
):
    micro, local, length, width = tokens.shape
    enc_length = states.shape[2]
    seqs = micro * local
    shard_rows = attn_w.shape[1]
    linked = n_dp == 4 and n_fsdp == 8 and vec_w.shape[0] == TAIL + 1
    token_rows = tokens.reshape(seqs * length, width)
    state_rows = states.reshape(seqs * enc_length, width)
    cotan_rows = cotangent.reshape(seqs * length, width)
    tok_lens = seq_len.reshape(seqs)
    enc_lens = enc_len.reshape(seqs)

    if linked:
        links = Links(n_dp, n_fsdp)
        spot, core = links.spot, links.core
        peer = lambda rows: links.send(rows, links.to_core)
        part_a = lax.dynamic_index_in_dim(attn_w, spot + jnp.where(spot < 2, 0, 3), 0, keepdims=False).astype(bf16)
        part_b = lax.dynamic_index_in_dim(attn_w, spot + jnp.where(spot < 3, 2, 4), 0, keepdims=False).astype(bf16)
        part_1 = lax.dynamic_slice_in_dim(fc1_w, spot * D, D, 1).astype(bf16)
        part_2 = lax.dynamic_slice_in_dim(fc2_w, spot * shard_rows, shard_rows, 0).astype(bf16)
        vec_cols = vec_w.shape[1]
        small = vec_w.astype(bf16)
        small = jnp.concatenate(
            [
                small[:TAIL],
                jnp.pad(small[TAIL:], ((0, TAIL - 1), (0, 0))),
                jnp.zeros((TAIL, D - 2 * vec_cols), bf16),
            ],
            axis=1,
        )
        part_a = jnp.concatenate([part_a, small], axis=0)

        to_z1, to_z2, swap1, swap2 = links.to_z1, links.to_z2, links.swap1, links.swap2
        send = links.send
        CLOCK[:] = [vec_m]
        a_2, a_1 = send(part_a, to_z2), send(part_a, to_z1)
        part_a, part_b, a_2, a_1 = hold(part_a, part_b, a_2, a_1)

        a_3, b_2, b_1 = send(a_2, to_z1), send(part_b, to_z2), send(part_b, to_z1)
        (a_3,) = hold(a_3)
        a_own = links.column([part_a, a_2, a_1, a_3])
        a_near = send(a_own, swap1)
        part_b, part_1, b_2, b_1, a_near = hold(part_b, part_1, b_2, b_1, a_near)

        a_here = [under(a_own, a_near)]
        a_here.append(send(a_here[0], swap2))
        b_3, c_2 = send(b_2, to_z1), send(part_1, to_z2)
        part_1, b_3, c_2 = hold(part_1, b_3, c_2)
        b_own = links.column([part_b, b_2, b_1, b_3])
        b_near = send(b_own, swap1)
        c_1 = send(under(part_1, c_2), to_z1)
        a_there = [peer(a_here[0])]
        part_1, c_1 = hold(part_1, c_1)
        c_own = links.column([part_1, c_2, c_1])
        c_own, part_2, b_own, b_near, *held = hold(c_own, part_2, b_own, b_near, *a_here, a_there[0])
        a_here, a_there = held[:2], held[2:]

        c_near = send(c_own, swap1)
        b_here = [under(b_own, b_near)]
        b_here.append(send(b_here[0], swap2))
        d_2 = send(part_2, to_z2)
        a_there.append(peer(a_here[1]))
        first_w = links.finish(a_here + a_there, shard_rows, True, TAIL)
        vectors = links.vectors(a_here, vec_cols)
    else:
        vectors = lax.all_gather(vec_w.astype(bf16), "fsdp", axis=1, tiled=True)
        attn = lax.all_gather(attn_w.astype(bf16), "fsdp", axis=1, tiled=True)
        first_w = jnp.concatenate([attn[u] for u in FIRST], axis=1)
        second_w = jnp.concatenate([attn[u] for u in SECOND], axis=1)
        fc_in = lax.all_gather(fc1_w.astype(bf16), "fsdp", axis=0, tiled=True)
        fc_out = lax.all_gather(fc2_w.astype(bf16), "fsdp", axis=0, tiled=True)
    vec = vectors.astype(f32)
    zeros = jnp.zeros((1, width), f32)
    qk_bias = jnp.concatenate([vec[0:1], zeros], axis=1)
    kv_bias = jnp.concatenate([zeros, vec[4:5]], axis=1)
    fc_bias = vec[13:].reshape(1, -1)

    queries_keys = project(token_rows, first_w, qk_bias, 0)
    if linked:
        queries_keys, first_w, part_2, d_2 = hold(queries_keys, first_w, part_2, d_2)
        d_1 = send(under(part_2, d_2), to_z1)
        b_there = [peer(b_here[0])]
    cross_kv = project(state_rows, first_w, kv_bias, 2 * D)
    if linked:
        cross_kv, d_1 = hold(cross_kv, d_1)
        d_own = links.column([part_2, d_2, d_1])
        d_own, c_own, c_near, b_here[1], b_there[0] = hold(d_own, c_own, c_near, b_here[1], b_there[0])
        c_here = [under(c_own, c_near)]
        c_here.append(send(c_here[0], swap2))
        d_near = send(d_own, swap1)
        b_there.append(peer(b_here[1]))
        second_w = links.finish(b_here + b_there, shard_rows, True)
        c_there = [peer(c_here[0])]
    values = project(token_rows, second_w, vec[1:2], 0)
    self_in = attend(tok_lens, queries_keys, queries_keys, values, token_rows, seqs, True, 0, PAIRS, 0)
    if linked:
        self_in_peer = peer(self_in)
    normed_one, normed_one_low, unit_one, scale_one, sums_one = join(
        tok_lens, self_in, second_w, D, token_rows, vec, (2, 7, 8)
    )
    cross_q = project(normed_one_low, second_w, vec[3:4], 2 * D)
    cross_in = attend(enc_lens, cross_q, cross_kv, cross_kv, normed_one_low, seqs, False, 0, 0, PAIRS)
    normed_two, normed_two_low, unit_two, scale_two, sums_two = join(
        tok_lens, cross_in, second_w, 3 * D, normed_one, vec, (5, 9, 10)
    )
    if linked:
        normed_two_low, d_own, d_near, c_here[1], c_there[0] = hold(
            normed_two_low, d_own, d_near, c_here[1], c_there[0]
        )
        d_here = [under(d_own, d_near)]
        d_here.append(send(d_here[0], swap2))
        c_there.append(peer(c_here[1]))
        fc_in = links.finish(c_here + c_there, shard_rows, True)
        d_there = [peer(d_here[0])]
        cross_in_peer = peer(cross_in)
    hidden, slope = hidden_layer(normed_two_low, fc_in, fc_bias)
    if linked:
        hidden, normed_two_low, d_here[1], d_there[0] = hold(hidden, normed_two_low, d_here[1], d_there[0])
        d_there.append(peer(d_here[1]))
        fc_out = links.finish(d_here + d_there, shard_rows, False)
    mixed, grad_three, grad_ffn, sums_three = turn(
        tok_lens, hidden, fc_out, normed_two, cotan_rows, vec, (6, 11, 12)
    )

    env = dict(
        hidden=hidden, normed_two_low=normed_two_low, grad_three=grad_three, grad_ffn=grad_ffn, self_in=self_in,
        cross_in=cross_in, sums_three=sums_three,
    )

    def k_hidden(e):
        e["grad_pre"], e["sums_pre"] = hidden_back(e["grad_ffn"], fc_out, slope)

    def k_two(e):
        e["grad_two"], e["grad_cross"], e["grad_ctx"], e["sums_two"] = join_back(
            e["grad_pre"], fc_in, 0, grad_three, unit_two, scale_two, vec, 9, second_w, 3 * D
        )

    def k_cross(e):
        e["cross_grads"], e["cross_dkv"], e["sums_cross"] = attend_back(
            enc_lens, cross_q, cross_kv, cross_kv, e["grad_ctx"], e["grad_cross"], seqs, False, 0, 0, PAIRS
        )

    def k_one(e):
        e["grad_one"], e["grad_self"], e["grad_ctx"], e["sums_one"] = join_back(
            e["cross_grads"], second_w, 2 * D, e["grad_two"], unit_one, scale_one, vec, 7, second_w, D
        )

    def k_self(e):
        e["self_grads"], sums_self = attend_back(
            tok_lens, queries_keys, queries_keys, values, e["grad_ctx"], e["grad_self"], seqs, True, 0, PAIRS, 0
        )
        sums_cross = e["sums_cross"].reshape(seqs, 8, width).sum(axis=0)
        sums_self = sums_self.reshape(seqs, 8, width).sum(axis=0)
        last = e["sums_three"]
        e["grad_vec"] = jnp.concatenate(
            [
                sums_self[0:2],
                e["sums_one"][2:3],
                sums_cross[0:2],
                e["sums_two"][2:3],
                last[4:5],
                e["sums_one"][0:2],
                e["sums_two"][0:2],
                last[2:4],
                e["sums_pre"].reshape(-1, width),
                last[0:1],
                sums_one,
                sums_two,
                last[1:2],
                jnp.broadcast_to(jnp.sum(seq_len).astype(f32), (1, width)),
            ],
            axis=0,
        )

    def k_states(e):
        e["grad_states"] = input_grad(e["cross_dkv"], (0, 1), (first_w, first_w), (2 * D, 3 * D), BLOCK)

    def k_tokens(e):
        e["grad_tokens"] = input_grad(
            e["self_grads"], (0, 1, 2), (first_w, first_w, second_w), (0, D, 0), seqs * length, (e["grad_one"],)
        )

    kernels = {
        "hidden": (k_hidden, ("grad_ffn",), ("grad_pre", "sums_pre")),
        "two": (k_two, ("grad_pre",), ("grad_two", "grad_cross", "grad_ctx", "sums_two")),
        "cross": (k_cross, ("grad_ctx", "grad_cross"), ("cross_grads", "cross_dkv", "sums_cross")),
        "one": (k_one, ("cross_grads",), ("grad_one", "grad_self", "grad_ctx", "sums_one")),
        "self": (k_self, ("grad_ctx", "grad_self"), ("self_grads", "grad_vec")),
        "states": (k_states, ("cross_dkv",), ("grad_states",)),
        "tokens": (k_tokens, ("self_grads",), ("grad_tokens",)),
    }
    n_vec = vec_w.shape[0]
    if linked:
        order = links.plane_order()
        sums = {}

        def planes_of(name, x_mine, x_peer, y_mine, y_peer, x_at, y_at, stride, wide=D):
            spots = [(x_at(ux, y), *y_at(ux)) for ux, y in order]
            slots = [a if a.ndim == 3 else a[None] for a in (x_mine, x_peer, y_mine, y_peer)]
            sums[name] = Sum(links, unit_planes(*slots, spots, links.z, stride, shard_rows, wide))

        def k_planes_2(e):
            planes_of(
                "2", e["hidden"], e["hidden_peer"], e["grad_ffn"], e["grad_ffn_peer"],
                lambda ux, y: y * UNITS + ux * 2 + core, lambda ux: (0 * ux, 0 * ux), 2 * UNITS,
            )

        def k_planes_1(e):
            planes_of(
                "1", e["normed_two_low"], e["normed_two_low_peer"], e["grad_pre"], e["grad_pre_peer"],
                lambda ux, y: y, lambda ux: (0 * ux, ux * 2 + core), 2,
            )

        def k_planes_t(e):
            planes_of(
                "t", e["cross_in"], e["cross_in_peer"], e["cross_grads"], e["cross_grads_peer"],
                lambda ux, y: core * 2 * links.depth + y, lambda ux: (core + 0 * ux, ux), 2, D // 2,
            )

        def k_planes_a(e):
            planes_of(
                "a", e["self_in"], e["self_in_peer"], e["self_grads"], e["self_grads_peer"],
                lambda ux, y: y + 2 * links.depth * (ux * core), lambda ux: (ux * 2 + core, 0 * ux), 2,
            )

        def k_theirs(e):
            e["theirs"] = state_grad(state_rows, e["cross_dkv"], 1 - core)

        def k_mine(e):
            e["mine"] = state_grad(state_rows, e["cross_dkv"], core)

        def k_planes_e(e):
            spots = [(y, ux) for ux, y in order]
            sums["e"] = Sum(links, sum_planes(e["mine"], e["theirs_peer"], spots, links.z, shard_rows, D // 2))

        states_of = {"1": (fc1_w, fc1_m, fc1_v), "2": (fc2_w, fc2_m, fc2_v)}
        whole_unit, half_unit = (1, shard_rows, D), (1, shard_rows, D // 2)
        ways = {
            "2": ((shard_rows, D), lambda u: (u, 0)),
            "1": ((shard_rows, D), lambda u: (0, u)),
            "a": (whole_unit, lambda u: (u, 0, 0)),
            "t": (half_unit, lambda u: (4 + 3 * (u % 2), 0, u // 2)),
            "e": (half_unit, lambda u: (5 + u % 2, 0, u // 2)),
        }

        pairs = {"a": (whole_unit, 0), "2": ((shard_rows, D), 0), "1": ((shard_rows, D), 1)}

        def k_adam(name):
            def kernel(e):
                place_of = name if name in states_of else "attn"
                state = states_of.get(name, (attn_w, attn_m, attn_v))
                if name in pairs:
                    e[place_of] = adam_pairs(spot, sums[name].parts, state, *pairs[name], e.get(place_of))
                else:
                    e[place_of] = adam_units(spot, sums[name].parts, state, *ways[name], e.get(place_of))

            return kernel

        kernels |= {
            "planes_2": (k_planes_2, ("hidden", "hidden_peer", "grad_ffn", "grad_ffn_peer"), ()),
            "planes_1": (k_planes_1, ("normed_two_low", "normed_two_low_peer", "grad_pre", "grad_pre_peer"), ()),
            "planes_t": (k_planes_t, ("cross_in", "cross_in_peer", "cross_grads", "cross_grads_peer"), ()),
            "planes_a": (k_planes_a, ("self_in", "self_in_peer", "self_grads", "self_grads_peer"), ()),
            "theirs": (k_theirs, ("cross_dkv",), ("theirs",)),
            "mine": (k_mine, ("cross_dkv",), ("mine",)),
            "planes_e": (k_planes_e, ("mine", "theirs_peer"), ()),
        }
        for name in "21ate":
            kernels["adam_" + name] = (k_adam(name), (), ())
        env |= {"self_in_peer": self_in_peer, "cross_in_peer": cross_in_peer}
        vec_perms = {"c": links.to_core, "z1": to_z1, "z2": to_z2, "s1": swap1, "s2": swap2}
        CLOCK[:] = [CLOCK[0]]
        for at, (kernel, *events) in enumerate(PLAN):
            if kernel:
                kernels[kernel][0](env)
            moved = [event[4:] for event in events if event.startswith("sum ")]
            made = [name[-1] for name in (kernel,) if name.startswith("planes")]
            landing = [event[5:] for event in events if event.startswith("land ")]
            names = set(kernels[kernel][2]) if kernel else set()
            for later in PLAN[at + 1 :]:
                if later[0]:
                    names |= set(kernels[later[0]][1])
                    break
            names |= {name + "_peer" for name in landing}
            names |= {event[5:] for event in events if event.startswith("give ")}
            if "vec" in landing or any(event.startswith("vec ") for event in events):
                names |= {"grad_vec"}
            names = sorted(name for name in names if name in env)
            here = [sums[name] for name in sorted({*moved, *made})]
            arrays = [env[name] for name in names]
            if kernel.startswith("adam"):
                place_of = kernel[5:] if kernel[5:] in states_of else "attn"
                arrays.append(env[place_of][0])
            held = land(here, *arrays)
            env.update(zip(names, held))
            if kernel.startswith("adam"):
                env[place_of][0] = held[-1]
            if "vec" in landing:
                env["grad_vec"] = env["grad_vec"] + env["vec_peer"]
            add(*[sums[name] for name in moved])
            if moved:
                held = land(here, *[env[name] for name in names])
                env.update(zip(names, held))
            go(*[sums[name] for name in moved])
            for event in events:
                if event.startswith("give "):
                    env[event[5:] + "_peer"] = peer(env[event[5:]])
                elif event.startswith("vec "):
                    env["vec_peer"] = send(env["grad_vec"], vec_perms[event[4:]])
        fc1_new, fc2_new, attn_new = env["1"], env["2"], env["attn"]
        grad_vec = env["grad_vec"]
    else:
        for name in ("hidden", "two", "cross", "one", "self", "states", "tokens"):
            kernels[name][0](env)
        self_grads, cross_grads, cross_dkv = env["self_grads"], env["cross_grads"], env["cross_dkv"]
        grad_vec = lax.psum(env["grad_vec"], ("dp", "fsdp"))

        def owned(inputs, grads, dim):
            part = dot_grad(inputs, grads).astype(bf16)
            part = lax.psum_scatter(part, "fsdp", scatter_dimension=dim, tiled=True)
            return lax.psum(part, "dp").astype(f32)

        grad_attn = jnp.stack(
            [owned(self_in[u // 3], self_grads[u], 0) for u in range(4)]
            + [
                owned(normed_one_low, cross_grads[0], 0),
                owned(state_rows, cross_dkv[0], 0),
                owned(state_rows, cross_dkv[1], 0),
                owned(cross_in[1], cross_grads[1], 0),
            ]
        )
        grad_fc1, grad_fc2 = owned(normed_two_low, env["grad_pre"], 0), owned(hidden, grad_ffn, 0)
        attn_new = adam_update(attn_w, attn_m, attn_v, grad_attn, matrix_rate, matrix_decay)
        fc1_new = adam_update(fc1_w, fc1_m, fc1_v, grad_fc1, matrix_rate, matrix_decay)
        fc2_new = adam_update(fc2_w, fc2_m, fc2_v, grad_fc2, matrix_rate, matrix_decay)
    grad_tokens, grad_states = env["grad_tokens"], env["grad_states"]
    stats = grad_vec[n_vec:]
    stream_rms = jnp.sqrt(jnp.sum(stats[:4], axis=1) / (stats[4, 0] * D))
    cols = vec_w.shape[1]
    vec_grad = lax.dynamic_slice_in_dim(grad_vec[:n_vec], lax.axis_index("fsdp") * cols, cols, 1)
    vec_new = adam_update(vec_w, CLOCK[0] if linked else vec_m, vec_v, vec_grad, vector_rate, 0.0)
    return (
        mixed.reshape(tokens.shape),
        grad_tokens.reshape(tokens.shape),
        grad_states.reshape(states.shape),
        stream_rms,
        *attn_new,
        *fc1_new,
        *fc2_new,
        *vec_new,
    )


def solution(mesh):
    rows = P(None, ("dp", "fsdp"), None, None)
    lens = P(None, ("dp", "fsdp"))
    attn, fc, vec = P(None, "fsdp", None), P("fsdp", None), P(None, "fsdp")
    state = (attn,) * 3 + (fc,) * 6 + (vec,) * 3
    return jax.shard_map(
        partial(on_device, mesh.shape["dp"], mesh.shape["fsdp"]),
        mesh=mesh,
        in_specs=(rows, rows, rows, lens, lens) + state,
        out_specs=(rows, rows, rows, P()) + state,
        check_vma=False,
    )
```
